128 devices in a mesh: gx: 16 (over x, y), gy: 8 (over z, core).
Axes of the slice: x: 4, y: 4, z: 4, core: 2. Of those that a mesh axis runs over, the one named last changes fastest.
Arguments:
- tokens: bfloat16 [64, 1024, 256], P('gx', 'gy'), may hold values from -6 to 6
- lengths: int32 [64], P('gx'), may hold values from 513 to 1024, as said below
- w_in: bfloat16 [256, 768], P(('gx', 'gy')), may hold values from -0.375 to 0.375
- b_q: bfloat16 [256], P(('gx', 'gy')), may hold values from -3 to 3
- b_v: bfloat16 [256], P(('gx', 'gy')), may hold values from -3 to 3
- w_out: bfloat16 [256, 256], P(('gx', 'gy')), may hold values from -3 to 3
- b_out: bfloat16 [256], P(('gx', 'gy')), may hold values from -3 to 3
- gain_first: bfloat16 [256], P(('gx', 'gy')), may hold values from 0.099609375 to 1.8984375
- shift_first: bfloat16 [256], P(('gx', 'gy')), may hold values from -3 to 3
- w_up: bfloat16 [256, 2048], P(('gx', 'gy')), may hold values from -0.375 to 0.375
- b_up: bfloat16 [2048], P(('gx', 'gy')), may hold values from -3 to 3
- w_down: bfloat16 [2048, 256], P(('gx', 'gy')), may hold values from -0.1875 to 0.1875
- b_down: bfloat16 [256], P(('gx', 'gy')), may hold values from -3 to 3
- gain_second: bfloat16 [256], P(('gx', 'gy')), may hold values from 0.099609375 to 1.8984375
- shift_second: bfloat16 [256], P(('gx', 'gy')), may hold values from -3 to 3
- cotangent: bfloat16 [64, 1024, 256], P('gx', 'gy'), may hold values from -6 to 6
Outputs:
- layer_out: bfloat16 [64, 1024, 256], P('gx', 'gy')
- grad_tokens: float32 [64, 1024, 256], P('gx', 'gy')
- grad_w_in: float32 [256, 768], P(('gx', 'gy'))
- grad_b_q: float32 [256], P(('gx', 'gy'))
- grad_b_v: float32 [256], P(('gx', 'gy'))
- grad_w_out: float32 [256, 256], P(('gx', 'gy'))
- grad_b_out: float32 [256], P(('gx', 'gy'))
- grad_gain_first: float32 [256], P(('gx', 'gy'))
- grad_shift_first: float32 [256], P(('gx', 'gy'))
- grad_w_up: float32 [256, 2048], P(('gx', 'gy'))
- grad_b_up: float32 [2048], P(('gx', 'gy'))
- grad_w_down: float32 [2048, 256], P(('gx', 'gy'))
- grad_b_down: float32 [256], P(('gx', 'gy'))
- grad_gain_second: float32 [256], P(('gx', 'gy'))
- grad_shift_second: float32 [256], P(('gx', 'gy'))
The draws below stay inside these ranges and needn't reach their ends.
Inputs may be any that keep to these rules, and one draw needn't show every extreme that they name: `lengths`: each image's number of real tokens; among the 4 images of each index of gx one has more than 896; at least one image of all has 1024.
All inputs are finite; a program needn't handle non-finite values.
Results may differ from the reference program's by a relative error of at most 0.02.
Values may be sent and summed in bfloat16 or wider, within the bound.
A program may use at most 128 MiB of HBM per device.

```python
import math
import jax
import jax.numpy as jnp
from jax import lax

D = 256
H = 8
HD = 32
FF = 2048
IMGS = 4
SPAN = 1024
SEG = 128
IMAGES = 64


def draw_lengths(key, part):
    key = jax.random.fold_in(key, 11)
    key_lens, key_pick, key_far, key_full = jax.random.split(key, 4)
    drawn = jax.random.randint(key_lens, (IMAGES,), SPAN // 2 + 1, SPAN + 1, dtype=jnp.int32)
    far_reach = jax.random.randint(key_far, (IMAGES,), SPAN - SEG + 1, SPAN + 1, dtype=jnp.int32)
    chosen = jax.random.randint(key_pick, (IMAGES // IMGS,), 0, IMGS, dtype=jnp.int32)
    in_group = jnp.arange(IMAGES, dtype=jnp.int32) % IMGS
    longest = in_group == jnp.repeat(chosen, IMGS)
    full_image = jax.random.randint(key_full, (), 0, IMAGES // IMGS, dtype=jnp.int32) * IMGS
    full_image = full_image + jnp.repeat(chosen, IMGS)[0] * 0
    group_of = jnp.arange(IMAGES, dtype=jnp.int32) // IMGS
    is_full = longest & (group_of == full_image // IMGS)
    result = jnp.where(longest, far_reach, drawn)
    return jnp.where(is_full, SPAN, result).astype(jnp.int32)


def levels(own_key, extent, shards, least, largest):
    factor_of = 1.0
    for dim, shards_of in shards:
        heights = jax.random.uniform(jax.random.fold_in(jax.random.fold_in(own_key, 6), dim), (shards_of,), jnp.float32, least / len(shards), largest / len(shards))
        factor_of = factor_of * jnp.repeat(jnp.exp(heights), extent[dim] // shards_of).reshape((-1,) + (1,) * (len(extent) - 1 - dim))
    return factor_of


def normal_values(stream_key, extent, width, limit, cuts=(), kind=jnp.bfloat16):
    loudness = levels(stream_key, extent, cuts, -0.22, 0.18) if cuts else 1.0
    array = jax.random.normal(stream_key, extent, jnp.float32) * width * loudness
    return jnp.minimum(jnp.maximum(array, -limit), limit).astype(kind)


def setup_inputs(seed: int = 0) -> dict:
    arg_keys = jax.random.split(jax.random.key(seed), 17)
    tokens = normal_values(arg_keys[0], (IMAGES, SPAN, D), 1.0, 6.0, ((0, 16), (1, 8)))
    lengths = draw_lengths(jax.random.fold_in(arg_keys[16], 71), 0)
    w_in = normal_values(arg_keys[2], (D, 3 * D), D ** -0.5, 0.375, ((0, 128),))
    b_q = normal_values(arg_keys[3], (D,), 0.5, 3.0, ((0, 128),))
    b_v = normal_values(arg_keys[4], (D,), 0.5, 3.0, ((0, 128),))
    w_out = normal_values(arg_keys[5], (D, D), 4 ** -0.5, 3.0, ((0, 128),))
    b_out = normal_values(arg_keys[6], (D,), 0.5, 3.0, ((0, 128),))
    gain_first = jnp.clip(1.0 + 0.18 * jax.random.normal(arg_keys[7], (D,), jnp.float32), 0.099609375, 1.8984375).astype(jnp.bfloat16)
    shift_first = normal_values(arg_keys[8], (D,), 0.5, 3.0, ((0, 128),))
    w_up = normal_values(arg_keys[9], (D, FF), D ** -0.5, 0.375, ((0, 128),))
    b_up = normal_values(arg_keys[10], (FF,), 0.5, 3.0, ((0, 128),))
    w_down = normal_values(arg_keys[11], (FF, D), (FF // 2) ** -0.5, 0.1875, ((0, 128),))
    b_down = normal_values(arg_keys[12], (D,), 0.5, 3.0, ((0, 128),))
    gain_second = jnp.clip(1.0 + 0.18 * jax.random.normal(arg_keys[13], (D,), jnp.float32), 0.099609375, 1.8984375).astype(jnp.bfloat16)
    shift_second = normal_values(arg_keys[14], (D,), 0.5, 3.0, ((0, 128),))
    cotangent = normal_values(arg_keys[15], (IMAGES, SPAN, D), 1.0, 6.0, ((0, 16), (1, 8)))
    return {"tokens": tokens, "lengths": lengths, "w_in": w_in, "b_q": b_q, "b_v": b_v, "w_out": w_out, "b_out": b_out, "gain_first": gain_first, "shift_first": shift_first, "w_up": w_up, "b_up": b_up, "w_down": w_down, "b_down": b_down, "gain_second": gain_second, "shift_second": shift_second, "cotangent": cotangent}


@jax.custom_vjp
def low(v):
    return lax.optimization_barrier(v.astype(jnp.bfloat16)).astype(jnp.float32)

@jax.custom_vjp
def low_back(v):
    return v

def low_keep(v):
    return (low(v), None)

def low_pass(kept, grad):
    return (grad,)

def back_keep(v):
    return (v, None)

def back_low(kept, grad):
    return (low(grad),)
low.defvjp(low_keep, low_pass)
low_back.defvjp(back_keep, back_low)
EPSILON = 1e-05
GELU_SCALE = math.sqrt(2.0 / math.pi)

def layer_norm(values, gain_vec, shift_vec):
    centre = lax.optimization_barrier(jnp.mean(values, axis=-1, keepdims=True))
    shifted = values - centre
    spread = lax.optimization_barrier(jnp.mean(shifted * shifted, axis=-1, keepdims=True))
    return shifted * lax.rsqrt(spread + EPSILON) * gain_vec + shift_vec

def gelu_tanh(values):
    return 0.5 * values * (1.0 + jnp.tanh(GELU_SCALE * (values + 0.044715 * values * values * values)))

def sine_table(place, model_width):
    column = jnp.arange(model_width, dtype=jnp.int32)
    frequency = jnp.power(10000.0, -(2 * (column // 2)).astype(jnp.float32) / model_width)
    phase_angle = place.astype(jnp.float32)[:, None] * frequency[None, :]
    return jnp.where(column % 2 == 0, jnp.sin(phase_angle), jnp.cos(phase_angle))

def matmul_high(left, right):
    return jnp.dot(left, right, precision=lax.Precision.HIGHEST)

def encoder_layer(params, rows_in, position, length):
    w_in, b_q, b_v, w_out, b_out, gain_first, shift_first, w_up, b_up, w_down, b_down, gain_second, shift_second = params
    shifted = low(rows_in + position)
    query_rows = low_back(low(matmul_high(shifted, w_in[:, :D]) + b_q))
    key_rows = low_back(low(matmul_high(shifted, w_in[:, D:2 * D])))
    value_rows = low_back(low(matmul_high(rows_in, w_in[:, 2 * D:]) + b_v))
    score_scale = 1.0 / math.sqrt(HD)
    scores = jnp.einsum('qhd,khd->hqk', query_rows.reshape(SPAN, H, HD), key_rows.reshape(SPAN, H, HD), precision=lax.Precision.HIGHEST)
    scores = low_back(scores * score_scale)
    is_valid = jnp.arange(SPAN).astype(jnp.int32) < length
    scores = jnp.where(is_valid[None, None, :], scores, -1e+30)
    row_peak = lax.optimization_barrier(jnp.max(scores, axis=-1, keepdims=True))
    exponent = jnp.exp(scores - row_peak)
    attn_probs = exponent / lax.optimization_barrier(jnp.sum(exponent, axis=-1, keepdims=True))
    attn_mixed = jnp.einsum('hqk,khd->qhd', low(attn_probs), value_rows.reshape(SPAN, H, HD), precision=lax.Precision.HIGHEST).reshape(SPAN, D)
    attn_mixed = low_back(low(attn_mixed))
    branch = low_back(matmul_high(attn_mixed, w_out) + b_out)
    hidden = layer_norm(rows_in + branch, gain_first, shift_first)
    up_proj = low_back(matmul_high(low(hidden), w_up) + b_up)
    second_branch = low_back(matmul_high(low(gelu_tanh(up_proj)), w_down) + b_down)
    return layer_norm(hidden + second_branch, gain_second, shift_second)

def reference(tokens, lengths, w_in, b_q, b_v, w_out, b_out, gain_first, shift_first, w_up, b_up, w_down, b_down, gain_second, shift_second, cotangent):
    params = tuple((element.astype(jnp.float32) for element in (w_in, b_q, b_v, w_out, b_out, gain_first, shift_first, w_up, b_up, w_down, b_down, gain_second, shift_second)))
    position = sine_table(jnp.arange(SPAN).astype(jnp.int32), D)

    def per_image(running, image_item):
        image_rows, length, image_cot = image_item

        def layer_fn(weights_in, rows_in):
            return encoder_layer(weights_in, rows_in, position, length)
        output, pull_back = jax.vjp(layer_fn, params, image_rows.astype(jnp.float32))
        grad_params, grad_input = pull_back(image_cot.astype(jnp.float32))
        running = tuple((former + latest for former, latest in zip(running, grad_params)))
        return (running, (output.astype(jnp.bfloat16), grad_input))
    initial = tuple((jnp.zeros_like(element) for element in params))
    grad_sums, (outputs, grad_inputs) = lax.scan(per_image, initial, (tokens, lengths, cotangent))
    return (outputs, grad_inputs, grad_sums[0], grad_sums[1], grad_sums[2], grad_sums[3], grad_sums[4], grad_sums[5], grad_sums[6], grad_sums[7], grad_sums[8], grad_sums[9], grad_sums[10], grad_sums[11], grad_sums[12])
```

```python
import math

import jax
import jax.numpy as jnp
import numpy as np
from jax import lax
from jax.experimental import pallas as pl
from jax.experimental.pallas import tpu as pltpu
from jax.sharding import PartitionSpec as P

MESH = pl.DeviceIdType.MESH
F32 = jnp.float32
BF16 = jnp.bfloat16

D = 256
HD = 32
EPSILON = 1e-05
GELU_SCALE = math.sqrt(2.0 / math.pi)
SCORE_SCALE = 1.0 / math.sqrt(HD)
EXP2_SCALE = SCORE_SCALE * math.log2(math.e)


def dot(left, right):
    return jnp.dot(left, right, preferred_element_type=F32)


def dot_nt(left, right):
    return lax.dot_general(left, right, (((1,), (1,)), ((), ())), preferred_element_type=F32)


def dot_tn(left, right):
    return lax.dot_general(left, right, (((0,), (0,)), ((), ())), preferred_element_type=F32)


def iota(shape, dim):
    return lax.broadcasted_iota(jnp.int32, shape, dim)


def column_sum(values):
    return jnp.sum(values, axis=0, keepdims=True)


def norm_forward(values, gain, shift):
    centre = jnp.mean(values, axis=-1, keepdims=True)
    moved = values - centre
    spread = jnp.mean(moved * moved, axis=-1, keepdims=True)
    inverse = lax.rsqrt(spread + EPSILON)
    unit = moved * inverse
    return unit * gain + shift, unit, inverse


def norm_backward(d_out, unit, inverse, gain):
    d_unit = d_out * gain
    mean_d = jnp.mean(d_unit, axis=-1, keepdims=True)
    mean_du = jnp.mean(d_unit * unit, axis=-1, keepdims=True)
    return inverse * (d_unit - mean_d - unit * mean_du)


SCRATCH = dict(
    pf=((48, 128), F32),
    s1=((8, 112, 128), BF16),
    asmf=((384, 128), F32),
    img=((4, 2, 128, 256), BF16),
    cotb=((4, 128, 256), BF16),
    wio=((16, 112, 128), BF16),
    ff=((2, 16, 128, 256), BF16),
    vecs=((16, 256), F32),
    sh=((1024, 256), BF16),
    sht=((256, 1024), BF16),
    imgt=((256, 1024), BF16),
    kk=((1024, 128), BF16),
    vv=((1024, 128), BF16),
    qq=((1024, 128), BF16),
    kt=((128, 1024), BF16),
    vt=((128, 1024), BF16),
    qt=((256, 1024), BF16),
    ee=((4, 1024, 1024), BF16),
    ot=((128, 1024), F32),
    ri=((8, 1024), F32),
    mx=((4, 2, 128, 128), BF16),
    mr=((4, 128, 128), BF16),
    hid=((512, 256), F32),
    hlow=((512, 256), BF16),
    hlt=((256, 512), BF16),
    unit1=((512, 256), F32),
    inv1=((512, 1), F32),
    act=((8, 512, 256), BF16),
    dgl=((8, 512, 256), BF16),
    acc=((512, 256), F32),
    lob=((4, 128, 256), BF16),
    lor=((4, 128, 256), BF16),
    dffn=((512, 256), BF16),
    gp=((2, 16, 128, 256), BF16),
    gs=((16, 128, 256), BF16),
    rs=((16, 128, 256), BF16),
    r1=((3, 4, 128, 256), BF16),
    s2=((4, 128, 256), BF16),
    r2=((3, 128, 256), BF16),
    fin=((2, 128, 128), F32),
    gv=((16, 256), F32),
    dfirst=((512, 256), F32),
    dms=((4, 128, 128), BF16),
    dmx=((4, 2, 128, 128), BF16),
    dot_=((256, 1024), BF16),
    doo=((1024, 128), BF16),
    ds=((1024, 1024), BF16),
    dqt=((128, 1024), F32),
    dk=((1024, 128), F32),
    dv=((1024, 128), F32),
    gio=((16, 80, 128), BF16),
    q1=((3, 4, 80, 128), BF16),
    qs2=((4, 80, 128), BF16),
    q2=((3, 80, 128), BF16),
    fio=((80, 128), F32),
    v0=((16, 256), F32),
    vr1=((3, 16, 256), F32),
    v1=((16, 256), F32),
    vr2=((3, 16, 256), F32),
    v2=((16, 256), F32),
    vr3=((8, 16, 256), F32),
    gt=((4, 2, 128, 256), BF16),
    gtr=((4, 128, 256), BF16),
    gob=((4, 128, 256), BF16),
    gor=((4, 128, 256), BF16),
    p3f=((8, 48, 128), F32),
    p3=((8, 48, 128), BF16),
    r3=((8, 48, 128), BF16),
)

SEMS = dict(
    s1_s=7, s1_r=8, tk_s=3, tk_r=4, tf_s=4, tf_r=4, ct_s=3, ct_r=4,
    wi_sa=3, wi_sb=12, wi_r=16, wo_sa=3, wo_sb=12, wo_r=16,
    ff_sa=3, ff_sb=12, ff_r=16, fw_s=16, fw_r=16,
    mx_s=1, mx_r=1, dm_s=1, dm_r=1, lo_s=3, lo_r=4, gs_s=1, gs_r=1,
    r1_s=3, r1_r=3, r2_s=3, r2_r=3, q1_s=3, q1_r=3, q2_s=3, q2_r=3,
    v1_s=3, v1_r=3, v2_s=3, v2_r=3, v3_s=7, v3_r=8,
    gt_s=1, gt_r=1, go_s=3, go_r=4, p3_s=7, p3_r=8,
)

INPUTS = (
    "tok", "cot", "lens", "freq", "w_in", "w_out", "w_up", "w_down",
    "b_q", "b_v", "b_out", "gain1", "shift1", "b_down", "gain2", "shift2", "b_up",
)
OUTPUTS = (
    "layer_out", "grad_tokens", "g_w_in", "g_b_q", "g_b_v", "g_w_out", "g_b_out",
    "g_gain1", "g_shift1", "g_w_up", "g_b_up", "g_w_down", "g_b_down", "g_gain2", "g_shift2",
)
SMALL = ("b_q", "b_v", "b_out", "gain1", "shift1", "b_down", "gain2", "shift2")
G_SMALL = tuple("g_" + name for name in SMALL)
ROW = {name: row for row, name in enumerate(SMALL)}


class Refs:
    pass


def kernel(*refs):
    r = Refs()
    names = INPUTS + OUTPUTS + tuple(SCRATCH) + tuple(SEMS)
    for name, ref in zip(names, refs):
        setattr(r, name, ref)

    gx, gy = lax.axis_index("gx"), lax.axis_index("gy")
    x, y = lax.div(gx, 4), lax.rem(gx, 4)
    z, c = lax.div(gy, 2), lax.rem(gy, 2)
    a = x * (1 - c) + y * c
    b = y * (1 - c) + x * c

    def group(a_at, b_at):
        return a_at * (4 - 3 * c) + b_at * (1 + 3 * c)

    def ring(at, step, size=4):
        return lax.rem(at + (step % size), size)

    def a_peer(step):
        return (group(ring(a, step), b), gy)

    def b_peer(step):
        return (group(a, ring(b, step)), gy)

    def z_peer(step):
        return (gx, 2 * ring(z, step) + c)

    def gy_peer(step):
        return (gx, ring(gy, step, 8))

    sibling = (gx, 2 * z + 1 - c)
    here = group(a, b)

    def remote(src, dst, send, recv, device):
        return pltpu.make_async_remote_copy(
            src_ref=src, dst_ref=dst, send_sem=send, recv_sem=recv,
            device_id=device, device_id_type=MESH,
        )

    sent = []

    def send(make):
        make().start()
        sent.append(make)

    def await_recv(ref, sem):
        remote(ref, ref, sem, sem, sibling).wait_recv()

    barrier = pltpu.get_barrier_semaphore()
    peers = [a_peer(k) for k in (1, 2, 3)] + [b_peer(k) for k in (1, 2, 3)]
    peers += [gy_peer(k) for k in range(1, 8)]
    for peer in peers:
        pl.semaphore_signal(barrier, inc=1, device_id=peer, device_id_type=MESH)

    column = 0
    for ref, chunks in ((r.w_in, 6), (r.w_out, 2), (r.w_up, 16)):
        rows = ref[...].astype(F32)
        for k in range(chunks):
            for row in range(2):
                at = row * 24 + column
                r.pf[at : at + 1, :] = rows[row : row + 1, k * 128 : (k + 1) * 128]
            column += 1
    lane = iota((1, 256), 1)
    place = 2 * (8 * gx + gy)
    small_rows = []
    for name in SMALL:
        pair = getattr(r, name)[...].astype(F32).reshape(1, 2)
        row = jnp.where(lane == place, pair[:, 0:1], 0.0)
        small_rows.append(jnp.where(lane == place + 1, pair[:, 1:2], row))
    up_bias = r.b_up[...].astype(F32).reshape(1, 16)
    up_place = 128 * lax.rem(gx, 2) + 16 * gy
    up_row = jnp.zeros((1, 256), F32)
    for k in range(16):
        up_row = jnp.where(lane == up_place + k, up_bias[:, k : k + 1], up_row)
    up_rows = jnp.where(iota((8, 256), 0) == lax.div(gx, 2), up_row, 0.0)
    vec_low = jnp.concatenate(small_rows + [up_rows], axis=0).astype(BF16)
    r.s1[gy, 0:48, :] = r.pf[...].astype(BF16)
    r.s1[gy, 48:64, :] = r.w_down[:, 0:128]
    r.s1[gy, 64:80, :] = r.w_down[:, 128:256]
    r.s1[gy, 80:96, :] = vec_low[:, 0:128]
    r.s1[gy, 96:112, :] = vec_low[:, 128:256]

    pl.semaphore_wait(barrier, 13)

    for k in range(1, 8):
        send(lambda k=k: remote(
            r.s1.at[gy], r.s1.at[gy], r.s1_s.at[k - 1], r.s1_r.at[gy], gy_peer(k)))
    for k in (1, 2, 3):
        send(lambda k=k: remote(
            r.tok.at[ring(z, k)], r.img.at[z, c], r.tk_s.at[k - 1], r.tk_r.at[z], z_peer(k)))
    r.img[z, c] = r.tok[z]
    send(lambda: remote(r.img.at[z, c], r.img.at[z, c], r.tf_s.at[0], r.tf_r.at[z], sibling))
    r.cotb[z] = r.cot[z]

    freq = r.freq[...]
    even = lax.rem(iota((1, 256), 1), 2) == 0
    fine = iota((32, 256), 0).astype(F32) * freq
    coarse = iota((32, 256), 0).astype(F32) * 32.0 * freq
    sin_f, cos_f = jnp.sin(fine), jnp.cos(fine)
    sin_c, cos_c = jnp.sin(coarse), jnp.cos(coarse)
    first_c = jnp.where(even, sin_c, cos_c)
    second_c = jnp.where(even, cos_c, -sin_c)

    for k in range(1, 8):
        at = ring(gy, -k, 8)
        await_recv(r.s1.at[at], r.s1_r.at[at])
    vec_sum = jnp.zeros((32, 128), F32)
    for i in range(8):
        piece = r.s1[i, 0:48, :].astype(F32)
        for row in range(2):
            r.asmf[pl.ds(2 * i + row, 24, stride=16), :] = piece[row * 24 : row * 24 + 24]
        vec_sum = vec_sum + r.s1[i, 80:112, :].astype(F32)
    for k in range(3):
        rows = r.asmf[pl.ds(pl.multiple_of(32 * k + 16 * c, 16), 16), :]
        r.wio[here, 16 * k : 16 * k + 16, :] = rows.astype(BF16)
    r.wio[here, 48:80, :] = vec_sum.astype(BF16)
    r.wio[here, 80:112, :] = r.asmf[96:128, :].astype(BF16)

    def block(ref, at, part):
        return ref.at[at, pl.ds(part[0], part[1])]

    def gather_start(view, sem_a, sem_b, recv):
        for k in (1, 2, 3):
            send(lambda k=k: remote(
                view(here), view(here), sem_a.at[k - 1], recv.at[here], a_peer(k)))
        for k in (1, 2, 3):
            send(lambda k=k: remote(
                view(here), view(here), sem_b.at[k - 1], recv.at[here], b_peer(k)))

    def gather_relay(view, sem_b, recv):
        for i in (1, 2, 3):
            at = group(ring(a, -i), b)
            await_recv(view(at), recv.at[at])
            for k in (1, 2, 3):
                send(lambda k=k, i=i, at=at: remote(
                    view(at), view(at), sem_b.at[3 * i + k - 1], recv.at[at], b_peer(k)))

    def gather_wait(view, recv):
        for k in (1, 2, 3):
            for i in range(4):
                at = group(ring(a, -i), ring(b, -k))
                await_recv(view(at), recv.at[at])

    def wi_view(at):
        return r.wio.at[at, pl.ds(0, 80)]

    def wo_view(at):
        return r.wio.at[at, pl.ds(80, 32)]

    def ff_view(at):
        return r.ff.at[c, at]

    gather_start(wi_view, r.wi_sa, r.wi_sb, r.wi_r)

    @pl.when(c == 0)
    def _():
        for j in range(8):
            for half in range(2):
                at = 16 * (8 + 2 * j + half)
                r.ff[0, here, 16 * j : 16 * j + 16, 128 * half : 128 * half + 128] = (
                    r.asmf[at : at + 16, :].astype(BF16))

    @pl.when(c == 1)
    def _():
        for i in range(8):
            for half in range(2):
                r.ff[1, here, 16 * i : 16 * i + 16, 128 * half : 128 * half + 128] = (
                    r.s1[i, 48 + 16 * half : 64 + 16 * half, :])

    gather_start(ff_view, r.ff_sa, r.ff_sb, r.ff_r)
    gather_start(wo_view, r.wo_sa, r.wo_sb, r.wo_r)

    for k in (1, 2, 3):
        at = ring(z, -k)
        await_recv(r.img.at[at, c], r.tk_r.at[at])
        send(lambda k=k, at=at: remote(
            r.img.at[at, c], r.img.at[at, c], r.tf_s.at[k], r.tf_r.at[at], sibling))
    for k in (1, 2, 3):
        send(lambda k=k: remote(
            r.cot.at[ring(z, k)], r.cotb.at[z], r.ct_s.at[k - 1], r.ct_r.at[z], z_peer(k)))

    gather_relay(wi_view, r.wi_sb, r.wi_r)

    for k in range(4):
        at = ring(z, -k)
        await_recv(r.img.at[at, 1 - c], r.tf_r.at[at])

    for i in range(8):
        rows = r.img[i // 2, i % 2].astype(F32)
        for k in range(4):
            at = 4 * i + k
            pos = first_c[at : at + 1] * cos_f + second_c[at : at + 1] * sin_f
            r.sh[32 * at : 32 * at + 32, :] = (rows[32 * k : 32 * k + 32] + pos).astype(BF16)
    image = r.img[...].reshape(1024, 256)

    gather_relay(ff_view, r.ff_sb, r.ff_r)
    gather_relay(wo_view, r.wo_sb, r.wo_r)

    r.sht[...] = r.sh[...].T
    r.imgt[...] = image.T

    gather_wait(wi_view, r.wi_r)
    vec_sum = jnp.zeros((32, 128), F32)
    for i in range(16):
        vec_sum = vec_sum + r.wio[i, 48:80, :].astype(F32)
    r.vecs[:, 0:128] = vec_sum[0:16]
    r.vecs[:, 128:256] = vec_sum[16:32]

    def own_half(row):
        both = r.vecs[row : row + 1, :]
        return both[:, 0:128] * (1 - c).astype(F32) + both[:, 128:256] * c.astype(F32)

    def w_part(k):
        return r.wio[:, 16 * k : 16 * k + 16, :].reshape(256, 128)

    queries = (dot(r.sh[...], w_part(0)) + own_half(ROW["b_q"])).astype(BF16)
    keys = dot(r.sh[...], w_part(1)).astype(BF16)
    values = (dot(image, w_part(2)) + own_half(ROW["b_v"])).astype(BF16)
    r.qq[...] = queries
    r.kk[...] = keys
    r.vv[...] = values
    r.kt[...] = keys.T
    r.vt[...] = values.T
    r.qt[0:128, :] = queries.T
    ones_row = iota((128, 1024), 0) == 0
    r.qt[128:256, :] = jnp.where(ones_row, 1.0, 0.0).astype(BF16)

    length = r.lens[z]

    def head_lanes(head):
        return lax.div(iota((1024, 128), 1), HD) == head

    def forward_head(head, carry):
        masked = jnp.where(head_lanes(head), r.kk[...], jnp.zeros((), BF16))
        hidden_key = (iota((1024, 128), 0) >= length) & (iota((1024, 128), 1) == 0)
        bias = jnp.where(hidden_key, -1e30, 0.0).astype(BF16)
        scores = dot(jnp.concatenate([masked, bias], axis=1), r.qt[...])
        peak = jnp.max(scores, axis=0, keepdims=True)
        weights = jnp.exp2(scores * EXP2_SCALE - peak * EXP2_SCALE).astype(BF16)
        r.ee[head] = weights
        rows = r.vt[pl.ds(pl.multiple_of(head * HD, HD), HD), :]
        left = jnp.concatenate([rows, jnp.ones((16, 1024), BF16)], axis=0)
        mixed = dot(left, weights)
        inverse = 1.0 / mixed[HD : HD + 1]
        r.ot[pl.ds(pl.multiple_of(head * HD, HD), HD), :] = mixed[0:HD] * inverse
        r.ri[pl.ds(head, 1), :] = inverse

        @pl.when(head == 2)
        def _():
            gather_wait(ff_view, r.ff_r)
            for i in range(16):
                remote(ff_view(i), ff_view(i), r.fw_s.at[i], r.fw_r.at[i], sibling).start()

        return carry

    lax.fori_loop(0, 4, forward_head, 0)
    for i in range(16):
        sent.append(lambda i=i: remote(
            ff_view(i), ff_view(i), r.fw_s.at[i], r.fw_r.at[i], sibling))

    r.mx[...] = r.ot[...].T.astype(BF16).reshape(4, 2, 128, 128)
    send(lambda: remote(r.mx.at[:, 1 - c], r.mr, r.mx_s.at[0], r.mx_r.at[0], sibling))

    gather_wait(wo_view, r.wo_r)

    def w_out_rows(half):
        low = r.wio[pl.ds(8 * half, 8), 80:96, :].reshape(128, 128)
        high = r.wio[pl.ds(8 * half, 8), 96:112, :].reshape(128, 128)
        return jnp.concatenate([low, high], axis=1)

    def vec(name):
        return r.vecs[ROW[name] : ROW[name] + 1, :]

    mixed_own = r.mx[:, c].reshape(512, 128)
    branch = dot(mixed_own, w_out_rows(c))
    await_recv(r.mr, r.mx_r.at[0])
    mixed_other = r.mr[...].reshape(512, 128)
    branch = branch + dot(mixed_other, w_out_rows(1 - c))
    first_sum = r.img[:, c].reshape(512, 256).astype(F32) + branch + vec("b_out")
    hidden, unit, inverse = norm_forward(first_sum, vec("gain1"), vec("shift1"))
    r.unit1[...] = unit
    r.inv1[...] = inverse
    r.hid[...] = hidden
    hidden_low = hidden.astype(BF16)
    r.hlow[...] = hidden_low
    r.hlt[...] = hidden_low.T

    for i in range(16):
        await_recv(r.ff.at[1 - c, i], r.fw_r.at[i])

    def up_block(j):
        return r.ff[0, :, pl.ds(pl.multiple_of(16 * j, 16), 16), :].reshape(256, 256)

    def down_block(j):
        return r.ff[1, pl.ds(2 * j, 2), :, :].reshape(256, 256)

    def forward_ffn(j, carry):
        up = dot(r.hlow[...], up_block(j)) + r.vecs[pl.ds(8 + j, 1), :]
        square = up * up
        wave = jnp.tanh(GELU_SCALE * (up + 0.044715 * up * square))
        active = (0.5 * up * (1.0 + wave)).astype(BF16)
        slope = GELU_SCALE * (1.0 + 3 * 0.044715 * square)
        grad = 0.5 * (1.0 + wave) + 0.5 * up * (1.0 - wave * wave) * slope
        r.act[j] = active
        r.dgl[j] = grad.astype(BF16)
        r.acc[...] += dot(active, down_block(j))
        return carry

    r.acc[...] = r.hid[...] + vec("b_down")
    lax.fori_loop(0, 8, forward_ffn, 0)

    out, unit, inverse = norm_forward(r.acc[...], vec("gain2"), vec("shift2"))
    r.lob[...] = out.astype(BF16).reshape(4, 128, 256)
    for k in (1, 2, 3):
        send(lambda k=k: remote(
            r.lob.at[ring(z, k)], r.lor.at[z], r.lo_s.at[k - 1], r.lo_r.at[z], z_peer(k)))
    r.lor[z] = r.lob[z]

    for k in (1, 2, 3):
        at = ring(z, -k)
        await_recv(r.cotb.at[at], r.ct_r.at[at])
    d_out = r.cotb[...].reshape(512, 256).astype(F32)
    r.gv[ROW["gain2"] : ROW["gain2"] + 1, :] = column_sum(d_out * unit)
    r.gv[ROW["shift2"] : ROW["shift2"] + 1, :] = column_sum(d_out)
    d_second = norm_backward(d_out, unit, inverse, vec("gain2"))
    d_ffn = d_second.astype(BF16)
    r.dffn[...] = d_ffn
    r.gv[ROW["b_down"] : ROW["b_down"] + 1, :] = column_sum(d_ffn.astype(F32))
    r.acc[...] = d_second

    def backward_ffn(j, carry):
        d_active = dot_nt(r.dffn[...], down_block(j))
        d_up = (d_active * r.dgl[j].astype(F32)).astype(BF16)
        g_down = dot_tn(r.act[j], r.dffn[...])
        r.gp[1, pl.ds(2 * j, 2)] = g_down.astype(BF16).reshape(2, 128, 256)
        g_up = dot(r.hlt[...], d_up)
        r.gp[0, :, pl.ds(pl.multiple_of(16 * j, 16), 16), :] = (
            g_up.astype(BF16).reshape(16, 16, 256))
        r.gv[pl.ds(8 + j, 1), :] = column_sum(d_up.astype(F32))
        r.acc[...] += dot_nt(d_up, up_block(j))
        return carry

    lax.fori_loop(0, 8, backward_ffn, 0)
    send(lambda: remote(r.gp.at[1 - c], r.gs, r.gs_s.at[0], r.gs_r.at[0], sibling))

    d_hidden = r.acc[...]
    unit = r.unit1[...]
    r.gv[ROW["gain1"] : ROW["gain1"] + 1, :] = column_sum(d_hidden * unit)
    r.gv[ROW["shift1"] : ROW["shift1"] + 1, :] = column_sum(d_hidden)
    d_first = norm_backward(d_hidden, unit, r.inv1[...], vec("gain1"))
    r.dfirst[...] = d_first
    d_branch = d_first.astype(BF16)
    r.gv[ROW["b_out"] : ROW["b_out"] + 1, :] = column_sum(d_branch.astype(F32))
    r.dms[...] = dot_nt(d_branch, w_out_rows(1 - c)).astype(BF16).reshape(4, 128, 128)
    send(lambda: remote(r.dms, r.dmx.at[:, c], r.dm_s.at[0], r.dm_r.at[0], sibling))
    r.dmx[:, c] = dot_nt(d_branch, w_out_rows(c)).astype(BF16).reshape(4, 128, 128)

    def spot(g):
        return g * (1 - c) + (4 * lax.rem(g, 4) + lax.div(g, 4)) * c

    for half, mixed in ((c, r.mx[:, c].reshape(512, 128)), (1 - c, r.mr[...].reshape(512, 128))):
        g_out = dot_tn(mixed, d_branch).astype(BF16)
        for i in range(8):
            at = spot(8 * half + i)
            r.gio[at, 48:64, :] = g_out[16 * i : 16 * i + 16, 0:128]
            r.gio[at, 64:80, :] = g_out[16 * i : 16 * i + 16, 128:256]

    await_recv(r.dmx.at[:, 1 - c], r.dm_r.at[0])
    d_mixed_t = r.dmx[...].reshape(1024, 128).astype(F32).T
    extra = []
    for head in range(4):
        rows = slice(32 * head, 32 * head + 32)
        scaled = d_mixed_t[rows] * r.ri[head : head + 1, :]
        r.dot_[rows, :] = scaled.astype(BF16)
        inner = -column_sum(scaled * r.ot[rows, :])
        high = inner.astype(BF16).astype(F32)
        extra += [high, inner - high]
    extra.append(jnp.zeros((8, 1024), F32))
    r.dot_[128:144, :] = jnp.concatenate(extra, axis=0).astype(BF16)
    r.dot_[144:256, :] = jnp.zeros((112, 1024), BF16)
    r.doo[...] = r.dot_[0:128, :].T
    r.dk[...] = jnp.zeros((1024, 128), F32)
    r.dv[...] = jnp.zeros((1024, 128), F32)

    def add_siblings():
        await_recv(r.gs, r.gs_r.at[0])

        def add(i, carry):
            at = group(lax.div(i, 4), lax.rem(i, 4))
            r.rs[i] = (r.gp[c, at].astype(F32) + r.gs[at].astype(F32)).astype(BF16)
            return carry

        lax.fori_loop(0, 16, add, 0)
        for k in (1, 2, 3):
            ff_first(k).start()

    def ff_first(k):
        return remote(
            r.rs.at[pl.ds(4 * ring(a, k), 4)], r.r1.at[k - 1], r.r1_s.at[k - 1],
            r.r1_r.at[k - 1], a_peer(k))

    def ff_second(k):
        return remote(
            r.s2.at[ring(b, k)], r.r2.at[k - 1], r.r2_s.at[k - 1], r.r2_r.at[k - 1], b_peer(k))

    def add_first():
        for k in range(3):
            await_recv(r.r1.at[k], r.r1_r.at[k])

        def add(i, carry):
            total = r.rs[4 * a + i].astype(F32)
            for k in range(3):
                total = total + r.r1[k, i].astype(F32)
            r.s2[i] = total.astype(BF16)
            return carry

        lax.fori_loop(0, 4, add, 0)
        for k in (1, 2, 3):
            ff_second(k).start()

    def backward_head(head, carry):
        lanes = head_lanes(head)
        zero = jnp.zeros((), BF16)
        masked = jnp.where(lanes, r.vv[...], zero)
        ones = jnp.where(lax.div(iota((1024, 128), 1), 2) == head, 1.0, 0.0).astype(BF16)
        d_probs = dot(jnp.concatenate([masked, ones], axis=1), r.dot_[...])
        d_scores = r.ee[head] * d_probs.astype(BF16)
        r.ds[...] = d_scores
        at = pl.ds(pl.multiple_of(head * HD, HD), HD)
        r.dqt[at, :] = dot(r.kt[at, :], d_scores)
        q_masked = jnp.where(lanes, r.qq[...], zero)
        do_masked = jnp.where(lanes, r.doo[...], zero)
        for k in range(0, 1024, 256):
            r.dk[k : k + 256, :] += dot(r.ds[k : k + 256, :], q_masked)
            r.dv[k : k + 256, :] += dot(r.ee[head, k : k + 256, :], do_masked)

        @pl.when(head == 0)
        def _():
            add_siblings()

        @pl.when(head == 3)
        def _():
            add_first()

        return carry

    lax.fori_loop(0, 4, backward_head, 0)
    for k in (1, 2, 3):
        sent.append(lambda k=k: ff_first(k))
        sent.append(lambda k=k: ff_second(k))

    d_queries = (r.dqt[...] * SCORE_SCALE).T.astype(BF16)
    d_keys = (r.dk[...] * SCORE_SCALE).astype(BF16)
    d_values = r.dv[...].astype(BF16)
    for k, (left, right) in enumerate(((r.sht, d_queries), (r.sht, d_keys), (r.imgt, d_values))):
        g_part = dot(left[...], right).astype(BF16)
        for i in range(16):
            r.gio[spot(i), 16 * k : 16 * k + 16, :] = g_part[16 * i : 16 * i + 16, :]

    def io_first(k):
        return remote(
            r.gio.at[pl.ds(4 * ring(a, k), 4)], r.q1.at[k - 1], r.q1_s.at[k - 1],
            r.q1_r.at[k - 1], a_peer(k))

    for k in (1, 2, 3):
        send(lambda k=k: io_first(k))
    low_half, high_half = (1 - c).astype(F32), c.astype(F32)
    for name, d_rows in (("b_q", d_queries), ("b_v", d_values)):
        sums = column_sum(d_rows.astype(F32))
        r.gv[ROW[name] : ROW[name] + 1, :] = jnp.concatenate(
            [sums * low_half, sums * high_half], axis=1)
    r.v0[...] = r.gv[...]
    for k in (1, 2, 3):
        send(lambda k=k: remote(
            r.v0, r.vr1.at[k - 1], r.v1_s.at[k - 1], r.v1_r.at[k - 1], a_peer(k)))

    d_tokens = (
        dot_nt(d_queries, w_part(0)) + dot_nt(d_keys, w_part(1)) + dot_nt(d_values, w_part(2)))
    r.gt[...] = d_tokens.astype(BF16).reshape(4, 2, 128, 256)
    send(lambda: remote(r.gt.at[:, 1 - c], r.gtr, r.gt_s.at[0], r.gt_r.at[0], sibling))

    for k in range(3):
        await_recv(r.q1.at[k], r.q1_r.at[k])
    for i in range(4):
        total = r.gio[4 * a + i].astype(F32)
        for k in range(3):
            total = total + r.q1[k, i].astype(F32)
        r.qs2[i] = total.astype(BF16)
    for k in (1, 2, 3):
        send(lambda k=k: remote(
            r.qs2.at[ring(b, k)], r.q2.at[k - 1], r.q2_s.at[k - 1], r.q2_r.at[k - 1], b_peer(k)))
    total = r.v0[...]
    for k in range(3):
        await_recv(r.vr1.at[k], r.v1_r.at[k])
        total = total + r.vr1[k]
    r.v1[...] = total
    for k in (1, 2, 3):
        send(lambda k=k: remote(
            r.v1, r.vr2.at[k - 1], r.v2_s.at[k - 1], r.v2_r.at[k - 1], b_peer(k)))

    await_recv(r.gtr, r.gt_r.at[0])
    full = (
        r.dfirst[...]
        + r.gt[:, c].reshape(512, 256).astype(F32)
        + r.gtr[...].reshape(512, 256).astype(F32))
    r.gob[...] = full.astype(BF16).reshape(4, 128, 256)
    for k in (1, 2, 3):
        send(lambda k=k: remote(
            r.gob.at[ring(z, k)], r.gor.at[z], r.go_s.at[k - 1], r.go_r.at[z], z_peer(k)))
    r.gor[z] = r.gob[z]

    for k in range(3):
        await_recv(r.r2.at[k], r.r2_r.at[k])
    total = r.s2[b].astype(F32)
    for k in range(3):
        total = total + r.r2[k].astype(F32)
    r.fin[0] = total[:, 0:128]
    r.fin[1] = total[:, 128:256]
    for k in range(3):
        await_recv(r.q2.at[k], r.q2_r.at[k])
    total = r.qs2[b].astype(F32)
    for k in range(3):
        total = total + r.q2[k].astype(F32)
    r.fio[...] = total

    r.p3f[...] = jnp.zeros((8, 48, 128), F32)

    @pl.when(c == 0)
    def _():
        for i in range(8):
            for half in range(2):
                for row in range(2):
                    at = 16 * half + 8 * row
                    r.p3f[i, at : at + 8, :] = r.fin.at[half][
                        pl.ds(2 * i + row, 8, stride=16), :]

    @pl.when(c == 1)
    def _():
        for i in range(8):
            for half in range(2):
                r.p3f[i, 16 * half : 16 * half + 16, :] = r.fin[half, 16 * i : 16 * i + 16, :]

    for i in range(8):
        for row in range(2):
            at = 32 + 8 * row
            r.p3f[i, at : at + 5, :] = r.fio[pl.ds(2 * i + row, 5, stride=16), :]
    r.p3[...] = r.p3f[...].astype(BF16)
    for k in range(1, 8):
        send(lambda k=k: remote(
            r.p3.at[ring(gy, k, 8)], r.r3.at[gy], r.p3_s.at[k - 1], r.p3_r.at[gy], gy_peer(k)))
    r.r3[gy] = r.p3[gy]

    total = r.v1[...]
    for k in range(3):
        await_recv(r.vr2.at[k], r.v2_r.at[k])
        total = total + r.vr2[k]
    r.v2[...] = total
    for k in range(1, 8):
        send(lambda k=k: remote(
            r.v2, r.vr3.at[gy], r.v3_s.at[k - 1], r.v3_r.at[gy], gy_peer(k)))
    r.vr3[gy] = r.v2[...]

    for k in (1, 2, 3):
        at = ring(z, -k)
        await_recv(r.lor.at[at], r.lo_r.at[at])
    r.layer_out[...] = r.lor[...]
    for k in (1, 2, 3):
        at = ring(z, -k)
        await_recv(r.gor.at[at], r.go_r.at[at])
    r.grad_tokens[...] = r.gor[...].astype(F32)

    for k in range(1, 8):
        at = ring(gy, -k, 8)
        await_recv(r.r3.at[at], r.p3_r.at[at])
    core0 = jnp.zeros((48, 128), F32)
    core1 = jnp.zeros((48, 128), F32)
    for i in range(4):
        core0 = core0 + r.r3[2 * i].astype(F32)
        core1 = core1 + r.r3[2 * i + 1].astype(F32)
    r.g_w_down[:, 0:128] = core1[0:16]
    r.g_w_down[:, 128:256] = core1[16:32]
    for row in range(2):
        out_row = slice(row, row + 1)
        for j in range(8):
            for half in range(2):
                at = 16 * half + 8 * row + j
                lanes = 256 * j + 128 * half
                r.g_w_up[out_row, lanes : lanes + 128] = core0[at : at + 1]
        base = 32 + 8 * row
        for k in range(3):
            at = base + k
            r.g_w_in[out_row, 256 * k : 256 * k + 128] = core0[at : at + 1]
            r.g_w_in[out_row, 256 * k + 128 : 256 * k + 256] = core1[at : at + 1]
        both = core0 + core1
        r.g_w_out[out_row, 0:128] = both[base + 3 : base + 4]
        r.g_w_out[out_row, 128:256] = both[base + 4 : base + 5]

    for k in range(1, 8):
        at = ring(gy, -k, 8)
        await_recv(r.vr3.at[at], r.v3_r.at[at])
    total = jnp.zeros((16, 256), F32)
    for i in range(8):
        total = total + r.vr3[i]
    moved = pltpu.roll(total, lax.rem(256 - place, 256), axis=1)
    for name in SMALL:
        row = ROW[name]
        getattr(r, "g_" + name)[...] = moved[row : row + 1, 0:2].reshape(2)
    up_total = column_sum(jnp.where(iota((8, 256), 0) == lax.div(gx, 2), total[8:16], 0.0))
    up_total = jnp.broadcast_to(up_total, (8, 256))
    up_total = pltpu.roll(up_total, lax.rem(256 - up_place, 256), axis=1)
    r.g_b_up[...] = up_total[0:1, 0:16].reshape(16)

    for make in sent:
        make().wait_send()


def body(
    tokens, lengths, w_in, b_q, b_v, w_out, b_out, gain_first, shift_first, w_up, b_up,
    w_down, b_down, gain_second, shift_second, cotangent,
):
    column = np.arange(D)
    freq = np.power(10000.0, -(2.0 * (column // 2)) / D).astype(np.float32)[None, :]
    args = (
        tokens, cotangent, lengths, jnp.asarray(freq), w_in, w_out, w_up, w_down,
        b_q, b_v, b_out, gain_first, shift_first, b_down, gain_second, shift_second, b_up,
    )
    vmem = pl.BlockSpec(memory_space=pltpu.VMEM)
    in_specs = [vmem] * len(args)
    in_specs[2] = pl.BlockSpec(memory_space=pltpu.SMEM)
    shape = jax.ShapeDtypeStruct
    vector = shape((2,), F32)
    out_shape = (
        shape((4, 128, 256), BF16), shape((4, 128, 256), F32), shape((2, 768), F32),
        vector, vector, shape((2, 256), F32), vector, vector, vector,
        shape((2, 2048), F32), shape((16,), F32), shape((16, 256), F32),
        vector, vector, vector,
    )
    scratch = [pltpu.VMEM(dims, kind) for dims, kind in SCRATCH.values()]
    scratch += [pltpu.SemaphoreType.DMA((count,)) for count in SEMS.values()]
    return pl.pallas_call(
        kernel,
        out_shape=out_shape,
        in_specs=in_specs,
        out_specs=tuple([vmem] * len(out_shape)),
        scratch_shapes=scratch,
        compiler_params=pltpu.CompilerParams(
            collective_id=0, has_side_effects=True, vmem_limit_bytes=62 * 2**20),
        name="encoder_layer",
    )(*args)


def solution(mesh):
    both = ("gx", "gy")
    rows, vector, whole = P(both, None), P(both), P("gx", "gy", None)
    return jax.shard_map(
        body,
        mesh=mesh,
        in_specs=(
            whole, P("gx"), rows, vector, vector, rows, vector, vector, vector, rows, vector,
            rows, vector, vector, vector, whole,
        ),
        out_specs=(
            whole, whole, rows, vector, vector, rows, vector, vector, vector, rows, vector,
            rows, vector, vector, vector,
        ),
        check_vma=False,
    )
```

```python
import math

import jax
import jax.numpy as jnp
import numpy as np
from jax import lax
from jax.experimental import pallas as pl
from jax.experimental.pallas import tpu as pltpu
from jax.sharding import PartitionSpec as P

MESH = pl.DeviceIdType.MESH
F32 = jnp.float32
BF16 = jnp.bfloat16

D = 256
HD = 32
VMEM_LIMIT = 56 * 2**20
EPSILON = 1e-05
GELU_SCALE = math.sqrt(2.0 / math.pi)
SCORE_SCALE = 1.0 / math.sqrt(HD)
EXP2_SCALE = SCORE_SCALE * math.log2(math.e)


def dot(left, right):
    return jnp.dot(left, right, preferred_element_type=F32)


def dot_nt(left, right):
    return lax.dot_general(left, right, (((1,), (1,)), ((), ())), preferred_element_type=F32)


def dot_tn(left, right):
    return lax.dot_general(left, right, (((0,), (0,)), ((), ())), preferred_element_type=F32)


def iota(shape, dim):
    return lax.broadcasted_iota(jnp.int32, shape, dim)


def column_sum(values):
    return jnp.sum(values, axis=0, keepdims=True)


def norm_forward(values, gain, shift):
    centre = jnp.mean(values, axis=-1, keepdims=True)
    moved = values - centre
    spread = jnp.mean(moved * moved, axis=-1, keepdims=True)
    inverse = lax.rsqrt(spread + EPSILON)
    unit = moved * inverse
    return unit * gain + shift, unit, inverse


def norm_backward(d_out, unit, inverse, gain):
    d_unit = d_out * gain
    mean_d = jnp.mean(d_unit, axis=-1, keepdims=True)
    mean_du = jnp.mean(d_unit * unit, axis=-1, keepdims=True)
    return inverse * (d_unit - mean_d - unit * mean_du)


SCRATCH = dict(
    pf=((64, 128), F32),
    s1=((8, 128, 128), BF16),
    asmf=((384, 128), F32),
    img=((4, 2, 128, 256), BF16),
    cotb=((4, 128, 256), BF16),
    wio=((16, 128, 128), BF16),
    ff=((2, 16, 128, 256), BF16),
    vecs=((16, 256), F32),
    sh=((1024, 256), BF16),
    sht=((256, 1024), BF16),
    imgt=((256, 1024), BF16),
    kk=((1024, 128), BF16),
    vv=((1024, 128), BF16),
    qq=((1024, 128), BF16),
    kt=((128, 1024), BF16),
    vt=((128, 1024), BF16),
    qt=((256, 1024), BF16),
    ee=((4, 1024, 1024), BF16),
    ot=((128, 1024), F32),
    ri=((8, 1024), F32),
    mx=((4, 2, 128, 128), BF16),
    mr=((4, 128, 128), BF16),
    hid=((512, 256), F32),
    hlow=((512, 256), BF16),
    hlt=((256, 512), BF16),
    unit1=((512, 256), F32),
    inv1=((512, 1), F32),
    act=((8, 512, 256), BF16),
    dgl=((8, 512, 256), BF16),
    acc=((512, 256), F32),
    lob=((4, 128, 256), BF16),
    dffn=((512, 256), BF16),
    gp=((2, 16, 128, 256), BF16),
    gs=((16, 128, 256), BF16),
    rs=((16, 128, 256), BF16),
    r1=((3, 4, 128, 256), BF16),
    s2=((4, 128, 256), BF16),
    r2=((3, 128, 256), BF16),
    fin=((2, 128, 128), F32),
    gv=((16, 256), F32),
    dfirst=((512, 256), F32),
    dms=((4, 128, 128), BF16),
    dmx=((4, 2, 128, 128), BF16),
    dot_=((256, 1024), BF16),
    doo=((1024, 128), BF16),
    ds=((1024, 1024), BF16),
    dqt=((128, 1024), F32),
    dk=((1024, 128), F32),
    dv=((1024, 128), F32),
    gwo=((16, 32, 128), BF16),
    wo1=((3, 4, 32, 128), BF16),
    wos=((4, 32, 128), BF16),
    wo2=((3, 32, 128), BF16),
    fwo=((32, 128), F32),
    gio=((16, 64, 128), BF16),
    q1=((16, 64, 128), BF16),
    fio=((64, 128), F32),
    v0=((16, 256), F32),
    vr1=((3, 16, 256), F32),
    v1=((16, 256), F32),
    vr2=((3, 16, 256), F32),
    v2=((16, 256), F32),
    gt=((4, 2, 128, 256), BF16),
    gtr=((4, 128, 256), BF16),
    gob=((4, 128, 256), BF16),
    p3f=((8, 48, 128), F32),
    p3=((8, 48, 128), BF16),
    p4f=((8, 16, 128), F32),
    p4=((8, 16, 128), BF16),
)

SEMS = dict(
    in_s=17, s1_s=7, s1_r=8, s2_s=7, s2_r=8, tk_s=3, tk_r=4, tf_s=4, tf_r=4, ct_s=3, ct_r=4,
    wi_s=15, wi_r=16, wo_sa=3, wo_sb=12, wo_r=16,
    ff_sa=3, ff_sb=12, ff_r=16, fw_s=16, fw_r=16,
    mx_s=1, mx_r=1, dm_s=1, dm_r=1, lo_s=3, lo_r=4, gs_s=8, gs_r=8,
    r1_s=3, r1_r=3, r2_s=3, r2_r=3, q1_s=15, q1_r=16,
    g1_s=3, g1_r=3, g2_s=3, g2_r=3,
    v1_s=3, v1_r=3, v2_s=3, v2_r=3, v3_s=7, v3_r=8,
    gt_s=1, gt_r=1, go_s=3, go_r=4, p3_s=7, p3_r=8, p4_s=7, p4_r=8, own_s=5,
)

INPUTS = (
    "tok", "cot", "lens", "freq", "w_in", "w_out", "w_up", "w_down",
    "b_q", "b_v", "b_out", "gain1", "shift1", "b_down", "gain2", "shift2", "b_up",
)
OUTPUTS = (
    "layer_out", "grad_tokens", "g_w_in", "g_b_q", "g_b_v", "g_w_out", "g_b_out",
    "g_gain1", "g_shift1", "g_w_up", "g_b_up", "g_w_down", "g_b_down", "g_gain2", "g_shift2",
)
PACKED = dict(
    lor=((4, 128, 256), BF16),
    gor=((4, 128, 256), BF16),
    r3=((8, 48, 128), BF16),
    r4=((8, 16, 128), BF16),
    vr3=((8, 16, 256), F32),
)
LOADED = INPUTS[3:]
SMALL = ("b_q", "b_v", "b_out", "gain1", "shift1", "b_down", "gain2", "shift2")
ROW = {name: row for row, name in enumerate(SMALL)}


class Refs:
    pass


def kernel(*refs):
    r = Refs()
    held = tuple("v_" + name for name in LOADED)
    names = INPUTS + tuple(PACKED) + held + tuple(SCRATCH) + tuple(SEMS)
    for name, ref in zip(names, refs):
        setattr(r, name, ref)

    gx, gy = lax.axis_index("gx"), lax.axis_index("gy")
    x, y = lax.div(gx, 4), lax.rem(gx, 4)
    z, c = lax.div(gy, 2), lax.rem(gy, 2)
    a = x * (1 - c) + y * c
    b = y * (1 - c) + x * c

    def group(a_at, b_at):
        return a_at * (4 - 3 * c) + b_at * (1 + 3 * c)

    def ring(at, step, size=4):
        return lax.rem(at + (step % size), size)

    def a_peer(step):
        return (group(ring(a, step), b), gy)

    def b_peer(step):
        return (group(a, ring(b, step)), gy)

    def gx_peer(step):
        return (ring(gx, step, 16), gy)

    def z_peer(step):
        return (gx, 2 * ring(z, step) + c)

    def gy_peer(step):
        return (gx, ring(gy, step, 8))

    sibling = (gx, 2 * z + 1 - c)
    here = group(a, b)

    def remote(src, dst, send, recv, device):
        return pltpu.make_async_remote_copy(
            src_ref=src, dst_ref=dst, send_sem=send, recv_sem=recv,
            device_id=device, device_id_type=MESH,
        )

    sent = []

    def send(make):
        make().start()
        sent.append(make)

    def await_recv(ref, sem):
        remote(ref, ref, sem, sem, sibling).wait_recv()

    loads = [
        pltpu.make_async_copy(getattr(r, name), getattr(r, "v_" + name), r.in_s.at[i])
        for i, name in enumerate(LOADED)
    ]
    loads.append(pltpu.make_async_copy(r.tok.at[z], r.img.at[z, c], r.in_s.at[15]))
    loads.append(pltpu.make_async_copy(r.cot.at[z], r.cotb.at[z], r.in_s.at[16]))

    barrier = pltpu.get_barrier_semaphore()
    peers = [gx_peer(k) for k in range(1, 16)] + [gy_peer(k) for k in range(1, 8)]
    for peer in peers:
        pl.semaphore_signal(barrier, inc=1, device_id=peer, device_id_type=MESH)
    for load in loads:
        load.start()
    for load in loads:
        load.wait()

    rows = r.v_w_in[...].astype(F32)
    for row in range(2):
        for k in range(6):
            at = 6 * row + k
            r.pf[at : at + 1, :] = rows[row : row + 1, k * 128 : (k + 1) * 128]
    column = 0
    for ref, chunks in ((r.v_w_out, 2), (r.v_w_up, 16)):
        rows = ref[...].astype(F32)
        for k in range(chunks):
            for row in range(2):
                at = 16 + row * 18 + column
                r.pf[at : at + 1, :] = rows[row : row + 1, k * 128 : (k + 1) * 128]
            column += 1
    lane = iota((1, 256), 1)
    place = 2 * (8 * gx + gy)
    small_rows = []
    for name in SMALL:
        pair = getattr(r, "v_" + name)[...].astype(F32).reshape(1, 2)
        row = jnp.where(lane == place, pair[:, 0:1], 0.0)
        small_rows.append(jnp.where(lane == place + 1, pair[:, 1:2], row))
    up_bias = r.v_b_up[...].astype(F32).reshape(1, 16)
    up_place = 128 * lax.rem(gx, 2) + 16 * gy
    up_row = jnp.zeros((1, 256), F32)
    for k in range(16):
        up_row = jnp.where(lane == up_place + k, up_bias[:, k : k + 1], up_row)
    up_rows = jnp.where(iota((8, 256), 0) == lax.div(gx, 2), up_row, 0.0)
    vec_low = jnp.concatenate(small_rows + [up_rows], axis=0).astype(BF16)
    for row in range(2):
        r.pf[12 + 2 * row : 13 + 2 * row, :] = small_rows[row][:, 0:128]
        r.pf[13 + 2 * row : 14 + 2 * row, :] = small_rows[row][:, 128:256]
    r.pf[52:64, :] = jnp.zeros((12, 128), F32)
    r.s1[gy, 0:64, :] = r.pf[...].astype(BF16)
    r.s1[gy, 64:80, :] = r.v_w_down[:, 0:128]
    r.s1[gy, 80:96, :] = r.v_w_down[:, 128:256]
    r.s1[gy, 96:112, :] = vec_low[:, 0:128]
    r.s1[gy, 112:128, :] = vec_low[:, 128:256]

    pl.semaphore_wait(barrier, 22)

    def first_part(at):
        return r.s1.at[at, pl.ds(0, 16)]

    def second_part(at):
        return r.s1.at[at, pl.ds(16, 112)]

    for k in range(1, 8):
        send(lambda k=k: remote(
            first_part(gy), first_part(gy), r.s1_s.at[k - 1], r.s1_r.at[gy], gy_peer(k)))
    for k in (1, 2, 3):
        send(lambda k=k: remote(
            r.tok.at[ring(z, k)], r.img.at[z, c], r.tk_s.at[k - 1], r.tk_r.at[z], z_peer(k)))
    for k in range(1, 8):
        send(lambda k=k: remote(
            second_part(gy), second_part(gy), r.s2_s.at[k - 1], r.s2_r.at[gy], gy_peer(k)))
    send(lambda: remote(r.img.at[z, c], r.img.at[z, c], r.tf_s.at[0], r.tf_r.at[z], sibling))

    freq = r.v_freq[...]
    even = lax.rem(iota((1, 256), 1), 2) == 0
    fine = iota((32, 256), 0).astype(F32) * freq
    coarse = iota((32, 256), 0).astype(F32) * 32.0 * freq
    sin_f, cos_f = jnp.sin(fine), jnp.cos(fine)
    sin_c, cos_c = jnp.sin(coarse), jnp.cos(coarse)
    first_c = jnp.where(even, sin_c, cos_c)
    second_c = jnp.where(even, cos_c, -sin_c)

    for k in range(1, 8):
        at = ring(gy, -k, 8)
        await_recv(first_part(at), r.s1_r.at[at])
    bias_low, bias_high = jnp.zeros((1, 128), F32), jnp.zeros((1, 128), F32)
    share0, share1 = (1 - c).astype(F32), c.astype(F32)
    for i in range(8):
        piece = r.s1[i, 0:16, :].astype(F32)
        for row in range(2):
            r.asmf[pl.ds(2 * i + row, 6, stride=16), :] = piece[row * 6 : row * 6 + 6]
        bias_low = bias_low + piece[12:13] * share0 + piece[13:14] * share1
        bias_high = bias_high + piece[14:15] * share0 + piece[15:16] * share1
    for k in range(3):
        rows = r.asmf[pl.ds(pl.multiple_of(32 * k + 16 * c, 16), 16), :]
        r.wio[here, 16 * k : 16 * k + 16, :] = rows.astype(BF16)
    r.wio[here, 48:64, :] = jnp.concatenate(
        [bias_low, bias_high, jnp.zeros((14, 128), F32)], axis=0).astype(BF16)

    def wi_view(at):
        return r.wio.at[at, pl.ds(0, 64)]

    for k in range(1, 16):
        send(lambda k=k: remote(
            wi_view(gx), wi_view(gx), r.wi_s.at[k - 1], r.wi_r.at[gx], gx_peer(k)))

    for k in range(1, 8):
        at = ring(gy, -k, 8)
        await_recv(second_part(at), r.s2_r.at[at])
    vec_sum = jnp.zeros((32, 128), F32)
    for i in range(8):
        piece = r.s1[i, 16:64, :].astype(F32)
        for row in range(2):
            r.asmf[pl.ds(96 + 2 * i + row, 18, stride=16), :] = piece[row * 18 : row * 18 + 18]
        vec_sum = vec_sum + r.s1[i, 96:128, :].astype(F32)
    r.wio[here, 64:96, :] = r.asmf[96:128, :].astype(BF16)
    r.wio[here, 96:128, :] = vec_sum.astype(BF16)

    def gather_start(view, sem_a, sem_b, recv):
        for k in (1, 2, 3):
            send(lambda k=k: remote(
                view(here), view(here), sem_a.at[k - 1], recv.at[here], a_peer(k)))
        for k in (1, 2, 3):
            send(lambda k=k: remote(
                view(here), view(here), sem_b.at[k - 1], recv.at[here], b_peer(k)))

    def gather_relay(view, sem_b, recv):
        for i in (1, 2, 3):
            at = group(ring(a, -i), b)
            await_recv(view(at), recv.at[at])
            for k in (1, 2, 3):
                send(lambda k=k, i=i, at=at: remote(
                    view(at), view(at), sem_b.at[3 * i + k - 1], recv.at[at], b_peer(k)))

    def gather_wait(view, recv):
        for k in (1, 2, 3):
            for i in range(4):
                at = group(ring(a, -i), ring(b, -k))
                await_recv(view(at), recv.at[at])

    def wo_view(at):
        return r.wio.at[at, pl.ds(64, 64)]

    def ff_view(at):
        return r.ff.at[c, at]

    @pl.when(c == 0)
    def _():
        for j in range(8):
            for half in range(2):
                at = 16 * (8 + 2 * j + half)
                r.ff[0, here, 16 * j : 16 * j + 16, 128 * half : 128 * half + 128] = (
                    r.asmf[at : at + 16, :].astype(BF16))

    @pl.when(c == 1)
    def _():
        for i in range(8):
            for half in range(2):
                r.ff[1, here, 16 * i : 16 * i + 16, 128 * half : 128 * half + 128] = (
                    r.s1[i, 64 + 16 * half : 80 + 16 * half, :])

    gather_start(ff_view, r.ff_sa, r.ff_sb, r.ff_r)
    gather_start(wo_view, r.wo_sa, r.wo_sb, r.wo_r)

    for k in (1, 2, 3):
        at = ring(z, -k)
        await_recv(r.img.at[at, c], r.tk_r.at[at])
        send(lambda k=k, at=at: remote(
            r.img.at[at, c], r.img.at[at, c], r.tf_s.at[k], r.tf_r.at[at], sibling))
    for k in (1, 2, 3):
        send(lambda k=k: remote(
            r.cot.at[ring(z, k)], r.cotb.at[z], r.ct_s.at[k - 1], r.ct_r.at[z], z_peer(k)))

    for k in range(4):
        at = ring(z, -k)
        await_recv(r.img.at[at, 1 - c], r.tf_r.at[at])

    for i in range(8):
        rows = r.img[i // 2, i % 2].astype(F32)
        for k in range(4):
            at = 4 * i + k
            pos = first_c[at : at + 1] * cos_f + second_c[at : at + 1] * sin_f
            r.sh[32 * at : 32 * at + 32, :] = (rows[32 * k : 32 * k + 32] + pos).astype(BF16)
    image = r.img[...].reshape(1024, 256)

    gather_relay(ff_view, r.ff_sb, r.ff_r)
    gather_relay(wo_view, r.wo_sb, r.wo_r)

    r.sht[...] = r.sh[...].T
    r.imgt[...] = image.T

    for k in range(1, 16):
        at = ring(gx, -k, 16)
        await_recv(wi_view(at), r.wi_r.at[at])
    biases = jnp.zeros((16, 128), F32)
    for i in range(16):
        biases = biases + r.wio[i, 48:64, :].astype(F32)

    def w_part(k):
        return r.wio[:, 16 * k : 16 * k + 16, :].reshape(256, 128)

    queries = (dot(r.sh[...], w_part(0)) + biases[0:1]).astype(BF16)
    keys = dot(r.sh[...], w_part(1)).astype(BF16)
    values = (dot(image, w_part(2)) + biases[1:2]).astype(BF16)
    r.qq[...] = queries
    r.kk[...] = keys
    r.vv[...] = values
    r.kt[...] = keys.T
    r.vt[...] = values.T
    r.qt[0:128, :] = queries.T
    ones_row = iota((128, 1024), 0) == 0
    r.qt[128:256, :] = jnp.where(ones_row, 1.0, 0.0).astype(BF16)

    length = r.lens[z]

    def head_lanes(head):
        return lax.div(iota((1024, 128), 1), HD) == head

    def forward_head(head, carry):
        masked = jnp.where(head_lanes(head), r.kk[...], jnp.zeros((), BF16))
        hidden_key = (iota((1024, 128), 0) >= length) & (iota((1024, 128), 1) == 0)
        bias = jnp.where(hidden_key, -1e30, 0.0).astype(BF16)
        scores = dot(jnp.concatenate([masked, bias], axis=1), r.qt[...])
        peak = jnp.max(scores, axis=0, keepdims=True)
        weights = jnp.exp2(scores * EXP2_SCALE - peak * EXP2_SCALE).astype(BF16)
        r.ee[head] = weights
        rows = r.vt[pl.ds(pl.multiple_of(head * HD, HD), HD), :]
        left = jnp.concatenate([rows, jnp.ones((16, 1024), BF16)], axis=0)
        mixed = dot(left, weights)
        inverse = 1.0 / mixed[HD : HD + 1]
        r.ot[pl.ds(pl.multiple_of(head * HD, HD), HD), :] = mixed[0:HD] * inverse
        r.ri[pl.ds(head, 1), :] = inverse

        @pl.when(head == 2)
        def _():
            gather_wait(ff_view, r.ff_r)
            for i in range(16):
                remote(ff_view(i), ff_view(i), r.fw_s.at[i], r.fw_r.at[i], sibling).start()

        return carry

    lax.fori_loop(0, 4, forward_head, 0)
    for i in range(16):
        sent.append(lambda i=i: remote(
            ff_view(i), ff_view(i), r.fw_s.at[i], r.fw_r.at[i], sibling))

    r.mx[...] = r.ot[...].T.astype(BF16).reshape(4, 2, 128, 128)
    send(lambda: remote(r.mx.at[:, 1 - c], r.mr, r.mx_s.at[0], r.mx_r.at[0], sibling))

    gather_wait(wo_view, r.wo_r)
    vec_sum = jnp.zeros((32, 128), F32)
    for i in range(16):
        vec_sum = vec_sum + r.wio[i, 96:128, :].astype(F32)
    r.vecs[:, 0:128] = vec_sum[0:16]
    r.vecs[:, 128:256] = vec_sum[16:32]

    def w_out_rows(half):
        low = r.wio[pl.ds(8 * half, 8), 64:80, :].reshape(128, 128)
        high = r.wio[pl.ds(8 * half, 8), 80:96, :].reshape(128, 128)
        return jnp.concatenate([low, high], axis=1)

    def vec(name):
        return r.vecs[ROW[name] : ROW[name] + 1, :]

    mixed_own = r.mx[:, c].reshape(512, 128)
    branch = dot(mixed_own, w_out_rows(c))
    await_recv(r.mr, r.mx_r.at[0])
    mixed_other = r.mr[...].reshape(512, 128)
    branch = branch + dot(mixed_other, w_out_rows(1 - c))
    first_sum = r.img[:, c].reshape(512, 256).astype(F32) + branch + vec("b_out")
    hidden, unit, inverse = norm_forward(first_sum, vec("gain1"), vec("shift1"))
    r.unit1[...] = unit
    r.inv1[...] = inverse
    r.hid[...] = hidden
    hidden_low = hidden.astype(BF16)
    r.hlow[...] = hidden_low
    r.hlt[...] = hidden_low.T

    for i in range(16):
        await_recv(r.ff.at[1 - c, i], r.fw_r.at[i])

    def up_block(j):
        return r.ff[0, :, pl.ds(pl.multiple_of(16 * j, 16), 16), :].reshape(256, 256)

    def down_block(j):
        return r.ff[1, pl.ds(2 * j, 2), :, :].reshape(256, 256)

    def forward_ffn(j, carry):
        up = dot(r.hlow[...], up_block(j)) + r.vecs[pl.ds(8 + j, 1), :]
        square = up * up
        wave = jnp.tanh(GELU_SCALE * (up + 0.044715 * up * square))
        active = (0.5 * up * (1.0 + wave)).astype(BF16)
        slope = GELU_SCALE * (1.0 + 3 * 0.044715 * square)
        grad = 0.5 * (1.0 + wave) + 0.5 * up * (1.0 - wave * wave) * slope
        r.act[j] = active
        r.dgl[j] = grad.astype(BF16)
        r.acc[...] += dot(active, down_block(j))
        return carry

    r.acc[...] = r.hid[...] + vec("b_down")
    lax.fori_loop(0, 8, forward_ffn, 0)

    out, unit, inverse = norm_forward(r.acc[...], vec("gain2"), vec("shift2"))
    r.lob[...] = out.astype(BF16).reshape(4, 128, 256)
    for k in (1, 2, 3):
        send(lambda k=k: remote(
            r.lob.at[ring(z, k)], r.lor.at[z], r.lo_s.at[k - 1], r.lo_r.at[z], z_peer(k)))
    own_copies = [pltpu.make_async_copy(r.lob.at[z], r.lor.at[z], r.own_s.at[0])]
    own_copies[0].start()

    for k in (1, 2, 3):
        at = ring(z, -k)
        await_recv(r.cotb.at[at], r.ct_r.at[at])
    d_out = r.cotb[...].reshape(512, 256).astype(F32)
    r.gv[ROW["gain2"] : ROW["gain2"] + 1, :] = column_sum(d_out * unit)
    r.gv[ROW["shift2"] : ROW["shift2"] + 1, :] = column_sum(d_out)
    d_second = norm_backward(d_out, unit, inverse, vec("gain2"))
    d_ffn = d_second.astype(BF16)
    r.dffn[...] = d_ffn
    r.gv[ROW["b_down"] : ROW["b_down"] + 1, :] = column_sum(d_ffn.astype(F32))
    r.acc[...] = d_second

    def down_send(j):
        part = pl.ds(2 * j, 2)
        return remote(r.gp.at[1, part], r.gs.at[part], r.gs_s.at[j], r.gs_r.at[j], sibling)

    def up_send(j):
        part = pl.ds(pl.multiple_of(16 * j, 16), 16)
        return remote(r.gp.at[0, :, part], r.gs.at[:, part], r.gs_s.at[j], r.gs_r.at[j], sibling)

    def backward_ffn(j, carry):
        d_active = dot_nt(r.dffn[...], down_block(j))
        d_up = (d_active * r.dgl[j].astype(F32)).astype(BF16)
        g_down = dot_tn(r.act[j], r.dffn[...])
        r.gp[1, pl.ds(2 * j, 2)] = g_down.astype(BF16).reshape(2, 128, 256)
        g_up = dot(r.hlt[...], d_up)
        r.gp[0, :, pl.ds(pl.multiple_of(16 * j, 16), 16), :] = (
            g_up.astype(BF16).reshape(16, 16, 256))
        r.gv[pl.ds(8 + j, 1), :] = column_sum(d_up.astype(F32))
        r.acc[...] += dot_nt(d_up, up_block(j))

        @pl.when(c == 0)
        def _():
            down_send(j).start()

        @pl.when(c == 1)
        def _():
            up_send(j).start()

        return carry

    lax.fori_loop(0, 8, backward_ffn, 0)

    d_hidden = r.acc[...]
    unit = r.unit1[...]
    r.gv[ROW["gain1"] : ROW["gain1"] + 1, :] = column_sum(d_hidden * unit)
    r.gv[ROW["shift1"] : ROW["shift1"] + 1, :] = column_sum(d_hidden)
    d_first = norm_backward(d_hidden, unit, r.inv1[...], vec("gain1"))
    r.dfirst[...] = d_first
    d_branch = d_first.astype(BF16)
    r.gv[ROW["b_out"] : ROW["b_out"] + 1, :] = column_sum(d_branch.astype(F32))
    r.dms[...] = dot_nt(d_branch, w_out_rows(1 - c)).astype(BF16).reshape(4, 128, 128)
    send(lambda: remote(r.dms, r.dmx.at[:, c], r.dm_s.at[0], r.dm_r.at[0], sibling))
    r.dmx[:, c] = dot_nt(d_branch, w_out_rows(c)).astype(BF16).reshape(4, 128, 128)

    def spot(g):
        return g * (1 - c) + (4 * lax.rem(g, 4) + lax.div(g, 4)) * c

    for half, mixed in ((c, r.mx[:, c].reshape(512, 128)), (1 - c, r.mr[...].reshape(512, 128))):
        g_out = dot_tn(mixed, d_branch).astype(BF16)
        for i in range(8):
            at = spot(8 * half + i)
            r.gwo[at, 0:16, :] = g_out[16 * i : 16 * i + 16, 0:128]
            r.gwo[at, 16:32, :] = g_out[16 * i : 16 * i + 16, 128:256]
    r.gv[0:2, :] = jnp.zeros((2, 256), F32)
    r.v0[...] = r.gv[...]

    @pl.when(c == 0)
    def _():
        for j in range(8):
            part = pl.ds(16 * j, 16)
            await_recv(r.gs.at[:, part], r.gs_r.at[j])
            down_send(j).wait_send()

    @pl.when(c == 1)
    def _():
        for j in range(8):
            part = pl.ds(2 * j, 2)
            await_recv(r.gs.at[part], r.gs_r.at[j])
            up_send(j).wait_send()

    def add_cores(i, carry):
        at = group(lax.div(i, 4), lax.rem(i, 4))
        r.rs[i] = (r.gp[c, at].astype(F32) + r.gs[at].astype(F32)).astype(BF16)
        return carry

    lax.fori_loop(0, 16, add_cores, 0)

    def first_sum_send(k, i):
        part, to = pl.ds(4 * ring(a, k), 4), a_peer(k)
        if i == 0:
            return remote(r.rs.at[part], r.r1.at[k - 1], r.r1_s.at[k - 1], r.r1_r.at[k - 1], to)
        if i == 1:
            return remote(r.gwo.at[part], r.wo1.at[k - 1], r.g1_s.at[k - 1], r.g1_r.at[k - 1], to)
        return remote(r.v0, r.vr1.at[k - 1], r.v1_s.at[k - 1], r.v1_r.at[k - 1], to)

    def second_sum_send(k, i):
        part, to = ring(b, k), b_peer(k)
        if i == 0:
            return remote(r.s2.at[part], r.r2.at[k - 1], r.r2_s.at[k - 1], r.r2_r.at[k - 1], to)
        if i == 1:
            return remote(r.wos.at[part], r.wo2.at[k - 1], r.g2_s.at[k - 1], r.g2_r.at[k - 1], to)
        return remote(r.v1, r.vr2.at[k - 1], r.v2_s.at[k - 1], r.v2_r.at[k - 1], to)

    for k in (1, 2, 3):
        for i in range(3):
            send(lambda k=k, i=i: first_sum_send(k, i))

    await_recv(r.dmx.at[:, 1 - c], r.dm_r.at[0])
    d_mixed_t = r.dmx[...].reshape(1024, 128).astype(F32).T
    extra = []
    for head in range(4):
        rows = slice(32 * head, 32 * head + 32)
        scaled = d_mixed_t[rows] * r.ri[head : head + 1, :]
        r.dot_[rows, :] = scaled.astype(BF16)
        inner = -column_sum(scaled * r.ot[rows, :])
        high = inner.astype(BF16).astype(F32)
        extra += [high, inner - high]
    extra.append(jnp.zeros((8, 1024), F32))
    r.dot_[128:144, :] = jnp.concatenate(extra, axis=0).astype(BF16)
    r.dot_[144:256, :] = jnp.zeros((112, 1024), BF16)
    r.doo[...] = r.dot_[0:128, :].T
    r.dk[...] = jnp.zeros((1024, 128), F32)
    r.dv[...] = jnp.zeros((1024, 128), F32)

    def add_first():
        for k in range(3):
            await_recv(r.r1.at[k], r.r1_r.at[k])
            await_recv(r.wo1.at[k], r.g1_r.at[k])
            await_recv(r.vr1.at[k], r.v1_r.at[k])

        def add(i, carry):
            total = r.rs[4 * a + i].astype(F32)
            small = r.gwo[4 * a + i].astype(F32)
            for k in range(3):
                total = total + r.r1[k, i].astype(F32)
                small = small + r.wo1[k, i].astype(F32)
            r.s2[i] = total.astype(BF16)
            r.wos[i] = small.astype(BF16)
            return carry

        lax.fori_loop(0, 4, add, 0)
        r.v1[...] = r.v0[...] + r.vr1[0] + r.vr1[1] + r.vr1[2]
        for k in (1, 2, 3):
            for i in range(3):
                second_sum_send(k, i).start()

    def backward_head(head, carry):
        lanes = head_lanes(head)
        zero = jnp.zeros((), BF16)
        masked = jnp.where(lanes, r.vv[...], zero)
        ones = jnp.where(lax.div(iota((1024, 128), 1), 2) == head, 1.0, 0.0).astype(BF16)
        d_probs = dot(jnp.concatenate([masked, ones], axis=1), r.dot_[...])
        d_scores = r.ee[head] * d_probs.astype(BF16)
        r.ds[...] = d_scores
        at = pl.ds(pl.multiple_of(head * HD, HD), HD)
        r.dqt[at, :] = dot(r.kt[at, :], d_scores)
        q_masked = jnp.where(lanes, r.qq[...], zero)
        do_masked = jnp.where(lanes, r.doo[...], zero)
        for k in range(0, 1024, 256):
            r.dk[k : k + 256, :] += dot(r.ds[k : k + 256, :], q_masked)
            r.dv[k : k + 256, :] += dot(r.ee[head, k : k + 256, :], do_masked)

        @pl.when(head == 3)
        def _():
            add_first()

        return carry

    lax.fori_loop(0, 4, backward_head, 0)
    for k in (1, 2, 3):
        for i in range(3):
            sent.append(lambda k=k, i=i: second_sum_send(k, i))

    d_queries = (r.dqt[...] * SCORE_SCALE).T.astype(BF16)
    d_keys = (r.dk[...] * SCORE_SCALE).astype(BF16)
    d_values = r.dv[...].astype(BF16)
    for k, (left, right) in enumerate(((r.sht, d_queries), (r.sht, d_keys), (r.imgt, d_values))):
        g_part = dot(left[...], right).astype(BF16)
        for i in range(16):
            r.gio[i, 16 * k : 16 * k + 16, :] = g_part[16 * i : 16 * i + 16, :]
    ones = jnp.ones((1024, 128), BF16)
    sums = jnp.where(
        iota((128, 128), 1) < 64, dot_tn(d_queries, ones), dot_tn(d_values, ones)).astype(BF16)
    for i in range(8):
        r.gio[8 * c + i, 48:64, :] = sums[16 * i : 16 * i + 16, :]
        r.gio[8 * (1 - c) + i, 48:64, :] = jnp.zeros((16, 128), BF16)
    for k in range(1, 16):
        send(lambda k=k: remote(
            r.gio.at[ring(gx, k, 16)], r.q1.at[gx], r.q1_s.at[k - 1], r.q1_r.at[gx], gx_peer(k)))

    d_tokens = (
        dot_nt(d_queries, w_part(0)) + dot_nt(d_keys, w_part(1)) + dot_nt(d_values, w_part(2)))
    r.gt[...] = d_tokens.astype(BF16).reshape(4, 2, 128, 256)
    send(lambda: remote(r.gt.at[:, 1 - c], r.gtr, r.gt_s.at[0], r.gt_r.at[0], sibling))

    for k in range(3):
        await_recv(r.r2.at[k], r.r2_r.at[k])
        await_recv(r.wo2.at[k], r.g2_r.at[k])
        await_recv(r.vr2.at[k], r.v2_r.at[k])
    total = r.s2[b].astype(F32)
    small = r.wos[b].astype(F32)
    for k in range(3):
        total = total + r.r2[k].astype(F32)
        small = small + r.wo2[k].astype(F32)
    r.fin[0] = total[:, 0:128]
    r.fin[1] = total[:, 128:256]
    r.fwo[...] = small
    r.v2[...] = r.v1[...] + r.vr2[0] + r.vr2[1] + r.vr2[2]
    r.p3f[...] = jnp.zeros((8, 48, 128), F32)

    @pl.when(c == 0)
    def _():
        for i in range(8):
            for half in range(2):
                for row in range(2):
                    at = 16 * half + 8 * row
                    r.p3f[i, at : at + 8, :] = r.fin.at[half][
                        pl.ds(2 * i + row, 8, stride=16), :]

    @pl.when(c == 1)
    def _():
        for i in range(8):
            for half in range(2):
                r.p3f[i, 16 * half : 16 * half + 16, :] = r.fin[half, 16 * i : 16 * i + 16, :]

    for i in range(8):
        for row in range(2):
            at = 32 + 8 * row
            r.p3f[i, at : at + 2, :] = r.fwo[pl.ds(2 * i + row, 2, stride=16), :]
    r.p3[...] = r.p3f[...].astype(BF16)
    for k in range(1, 8):
        send(lambda k=k: remote(
            r.p3.at[ring(gy, k, 8)], r.r3.at[gy], r.p3_s.at[k - 1], r.p3_r.at[gy], gy_peer(k)))
        send(lambda k=k: remote(
            r.v2, r.vr3.at[gy], r.v3_s.at[k - 1], r.v3_r.at[gy], gy_peer(k)))

    await_recv(r.gtr, r.gt_r.at[0])
    full = (
        r.dfirst[...]
        + r.gt[:, c].reshape(512, 256).astype(F32)
        + r.gtr[...].reshape(512, 256).astype(F32))
    r.gob[...] = full.astype(BF16).reshape(4, 128, 256)
    for k in (1, 2, 3):
        send(lambda k=k: remote(
            r.gob.at[ring(z, k)], r.gor.at[z], r.go_s.at[k - 1], r.go_r.at[z], z_peer(k)))

    total = r.gio[gx].astype(F32)
    for k in range(1, 16):
        at = ring(gx, -k, 16)
        await_recv(r.q1.at[at], r.q1_r.at[at])
        total = total + r.q1[at].astype(F32)
    r.fio[...] = total
    r.p4f[...] = jnp.zeros((8, 16, 128), F32)
    for i in range(8):
        for row in range(2):
            at = 8 * row
            r.p4f[i, at : at + 4, :] = r.fio[pl.ds(2 * i + row, 4, stride=16), :]
    r.p4[...] = r.p4f[...].astype(BF16)
    for k in range(1, 8):
        send(lambda k=k: remote(
            r.p4.at[ring(gy, k, 8)], r.r4.at[gy], r.p4_s.at[k - 1], r.p4_r.at[gy], gy_peer(k)))

    own_copies += [
        pltpu.make_async_copy(r.gob.at[z], r.gor.at[z], r.own_s.at[1]),
        pltpu.make_async_copy(r.p3.at[gy], r.r3.at[gy], r.own_s.at[2]),
        pltpu.make_async_copy(r.p4.at[gy], r.r4.at[gy], r.own_s.at[3]),
        pltpu.make_async_copy(r.v2, r.vr3.at[gy], r.own_s.at[4]),
    ]
    for copy in own_copies[1:]:
        copy.start()
    for k in (1, 2, 3):
        at = ring(z, -k)
        await_recv(r.lor.at[at], r.lo_r.at[at])
        await_recv(r.gor.at[at], r.go_r.at[at])
    for k in range(1, 8):
        at = ring(gy, -k, 8)
        await_recv(r.r3.at[at], r.p3_r.at[at])
        await_recv(r.vr3.at[at], r.v3_r.at[at])
        await_recv(r.r4.at[at], r.p4_r.at[at])
    for copy in own_copies:
        copy.wait()
    for make in sent:
        make().wait_send()


def unpack(*refs):
    r = Refs()
    for name, ref in zip(tuple(PACKED) + OUTPUTS, refs):
        setattr(r, name, ref)
    gx, gy = lax.axis_index("gx"), lax.axis_index("gy")
    place = 2 * (8 * gx + gy)
    up_place = 128 * lax.rem(gx, 2) + 16 * gy
    r.layer_out[...] = r.lor[...]
    r.grad_tokens[...] = r.gor[...].astype(F32)
    core0 = jnp.zeros((48, 128), F32)
    core1 = jnp.zeros((48, 128), F32)
    into0 = jnp.zeros((16, 128), F32)
    into1 = jnp.zeros((16, 128), F32)
    total = jnp.zeros((16, 256), F32)
    for i in range(4):
        core0 = core0 + r.r3[2 * i].astype(F32)
        core1 = core1 + r.r3[2 * i + 1].astype(F32)
        into0 = into0 + r.r4[2 * i].astype(F32)
        into1 = into1 + r.r4[2 * i + 1].astype(F32)
        total = total + r.vr3[2 * i] + r.vr3[2 * i + 1]
    r.g_w_down[:, 0:128] = core1[0:16]
    r.g_w_down[:, 128:256] = core1[16:32]
    w_out = core0 + core1
    for row in range(2):
        out_row = slice(row, row + 1)
        for j in range(8):
            for half in range(2):
                at = 16 * half + 8 * row + j
                lanes = 256 * j + 128 * half
                r.g_w_up[out_row, lanes : lanes + 128] = core0[at : at + 1]
        for k in range(3):
            at = 8 * row + k
            r.g_w_in[out_row, 256 * k : 256 * k + 128] = into0[at : at + 1]
            r.g_w_in[out_row, 256 * k + 128 : 256 * k + 256] = into1[at : at + 1]
        at = 32 + 8 * row
        r.g_w_out[out_row, 0:128] = w_out[at : at + 1]
        r.g_w_out[out_row, 128:256] = w_out[at + 1 : at + 2]
    biases = into0 + into1
    for name, lane in (("b_q", 0), ("b_v", 64)):
        pair = jnp.concatenate(
            [biases[3:4, lane : lane + 1], biases[11:12, lane : lane + 1]], axis=1)
        getattr(r, "g_" + name)[...] = pair.reshape(2)
    moved = pltpu.roll(total, lax.rem(256 - place, 256), axis=1)
    for name in SMALL[2:]:
        row = ROW[name]
        getattr(r, "g_" + name)[...] = moved[row : row + 1, 0:2].reshape(2)
    up_total = column_sum(jnp.where(iota((8, 256), 0) == lax.div(gx, 2), total[8:16], 0.0))
    up_total = jnp.broadcast_to(up_total, (8, 256))
    up_total = pltpu.roll(up_total, lax.rem(256 - up_place, 256), axis=1)
    r.g_b_up[...] = up_total[0:1, 0:16].reshape(16)


def body(
    tokens, lengths, w_in, b_q, b_v, w_out, b_out, gain_first, shift_first, w_up, b_up,
    w_down, b_down, gain_second, shift_second, cotangent,
):
    column = np.arange(D)
    freq = np.power(10000.0, -(2.0 * (column // 2)) / D).astype(np.float32)[None, :]
    args = (
        tokens, cotangent, lengths, jnp.asarray(freq), w_in, w_out, w_up, w_down,
        b_q, b_v, b_out, gain_first, shift_first, b_down, gain_second, shift_second, b_up,
    )
    vmem = pl.BlockSpec(memory_space=pltpu.VMEM)
    anywhere = pl.BlockSpec(memory_space=pl.ANY)
    in_specs = [anywhere] * len(args)
    in_specs[2] = pl.BlockSpec(memory_space=pltpu.SMEM)
    shape = jax.ShapeDtypeStruct
    vector = shape((2,), F32)
    scratch = [pltpu.VMEM(args[INPUTS.index(name)].shape, args[INPUTS.index(name)].dtype)
               for name in LOADED]
    scratch += [pltpu.VMEM(dims, kind) for dims, kind in SCRATCH.values()]
    scratch += [pltpu.SemaphoreType.DMA((count,)) for count in SEMS.values()]
    packed = pl.pallas_call(
        kernel,
        out_shape=tuple(shape(dims, kind) for dims, kind in PACKED.values()),
        in_specs=in_specs,
        out_specs=tuple([anywhere] * len(PACKED)),
        scratch_shapes=scratch,
        compiler_params=pltpu.CompilerParams(
            collective_id=0, has_side_effects=True, vmem_limit_bytes=VMEM_LIMIT),
        name="encoder_layer",
    )(*args)
    out_shape = (
        shape((4, 128, 256), BF16), shape((4, 128, 256), F32), shape((2, 768), F32),
        vector, vector, shape((2, 256), F32), vector, vector, vector,
        shape((2, 2048), F32), shape((16,), F32), shape((16, 256), F32),
        vector, vector, vector,
    )
    return pl.pallas_call(
        unpack,
        out_shape=out_shape,
        in_specs=[vmem] * len(packed),
        out_specs=tuple([vmem] * len(out_shape)),
        name="unpack_results",
    )(*packed)


def solution(mesh):
    both = ("gx", "gy")
    rows, vector, whole = P(both, None), P(both), P("gx", "gy", None)
    return jax.shard_map(
        body,
        mesh=mesh,
        in_specs=(
            whole, P("gx"), rows, vector, vector, rows, vector, vector, vector, rows, vector,
            rows, vector, vector, vector, whole,
        ),
        out_specs=(
            whole, whole, rows, vector, vector, rows, vector, vector, vector, rows, vector,
            rows, vector, vector, vector,
        ),
        check_vma=False,
    )
```

```python
import math

import jax
import jax.numpy as jnp
import numpy as np
from jax import lax
from jax.experimental import pallas as pl
from jax.experimental.pallas import tpu as pltpu
from jax.sharding import PartitionSpec as P

MESH = pl.DeviceIdType.MESH
F32 = jnp.float32
BF16 = jnp.bfloat16

D = 256
HD = 32
VMEM_LIMIT = 56 * 2**20
EPSILON = 1e-05
GELU_SCALE = math.sqrt(2.0 / math.pi)
SCORE_SCALE = 1.0 / math.sqrt(HD)
EXP2_SCALE = SCORE_SCALE * math.log2(math.e)


def dot(left, right):
    return jnp.dot(left, right, preferred_element_type=F32)


def dot_nt(left, right):
    return lax.dot_general(left, right, (((1,), (1,)), ((), ())), preferred_element_type=F32)


def dot_tn(left, right):
    return lax.dot_general(left, right, (((0,), (0,)), ((), ())), preferred_element_type=F32)


def iota(shape, dim):
    return lax.broadcasted_iota(jnp.int32, shape, dim)


def column_sum(values):
    return jnp.sum(values, axis=0, keepdims=True)


def norm_forward(values, gain, shift):
    centre = jnp.mean(values, axis=-1, keepdims=True)
    moved = values - centre
    spread = jnp.mean(moved * moved, axis=-1, keepdims=True)
    inverse = lax.rsqrt(spread + EPSILON)
    unit = moved * inverse
    return unit * gain + shift, unit, inverse


def norm_backward(d_out, unit, inverse, gain):
    d_unit = d_out * gain
    mean_d = jnp.mean(d_unit, axis=-1, keepdims=True)
    mean_du = jnp.mean(d_unit * unit, axis=-1, keepdims=True)
    return inverse * (d_unit - mean_d - unit * mean_du)


SCRATCH = dict(
    pf=((112, 128), F32),
    s1=((8, 112, 128), BF16),
    asmf=((384, 128), F32),
    img=((4, 2, 128, 256), BF16),
    cotb=((4, 128, 256), BF16),
    wio=((16, 112, 128), BF16),
    ff=((2, 16, 128, 256), BF16),
    vecs=((16, 256), F32),
    sh=((1024, 256), BF16),
    sht=((256, 1024), BF16),
    imgt=((256, 1024), BF16),
    kx=((4, 1024, 256), BF16),
    vx=((4, 1024, 256), BF16),
    qm=((4, 1024, 128), BF16),
    vv=((1024, 128), BF16),
    qq=((1024, 128), BF16),
    kt=((128, 1024), BF16),
    vt=((128, 1024), BF16),
    qt=((256, 1024), BF16),
    ee=((4, 1024, 1024), BF16),
    ot=((128, 1024), F32),
    ri=((8, 1024), F32),
    mx=((4, 2, 128, 128), BF16),
    mr=((4, 128, 128), BF16),
    hid=((512, 256), F32),
    hlow=((512, 256), BF16),
    hlt=((256, 512), BF16),
    unit1=((512, 256), F32),
    inv1=((512, 1), F32),
    act=((4, 512, 512), BF16),
    dgl=((4, 512, 512), BF16),
    acc=((512, 256), F32),
    lob=((4, 128, 256), BF16),
    dffn=((512, 256), BF16),
    gp=((2, 16, 128, 256), BF16),
    gs=((16, 128, 256), BF16),
    rs=((16, 128, 256), BF16),
    r1=((3, 4, 128, 256), BF16),
    s2=((4, 128, 256), BF16),
    r2=((3, 128, 256), BF16),
    fin=((2, 128, 128), F32),
    gv=((16, 256), F32),
    dfirst=((512, 256), F32),
    dms=((4, 128, 128), BF16),
    dmx=((4, 2, 128, 128), BF16),
    dot_=((256, 1024), BF16),
    doo=((1024, 128), BF16),
    ds=((2, 1024, 1024), BF16),
    dqt=((128, 1024), F32),
    dk=((1024, 128), F32),
    dv=((1024, 128), F32),
    gwo=((16, 32, 128), BF16),
    wo1=((3, 4, 32, 128), BF16),
    wos=((4, 32, 128), BF16),
    wo2=((3, 32, 128), BF16),
    fwo=((32, 128), F32),
    gio=((16, 64, 128), BF16),
    q1=((16, 64, 128), BF16),
    fio=((64, 128), F32),
    v0=((16, 256), F32),
    vr1=((3, 16, 256), F32),
    v1=((16, 256), F32),
    vr2=((3, 16, 256), F32),
    v2=((16, 256), F32),
    gt=((4, 2, 128, 256), BF16),
    gtr=((4, 128, 256), BF16),
    gob=((4, 128, 256), BF16),
    p3f=((8, 48, 128), F32),
    p3=((8, 48, 128), BF16),
    p4f=((8, 16, 128), F32),
    p4=((8, 16, 128), BF16),
)

GROUPS = (
    "s1", "s2", "tk", "tf", "ct", "wi", "wa", "wb", "fa", "fb", "fc", "fw", "mx", "dm", "lo",
    "gs", "r1", "r2", "g1", "g2", "v1", "v2", "v3", "q1", "gt", "go", "p3", "p4",
)
SEMS = dict(in_s=16, own_s=5, tk_r=3)
for group_name in GROUPS:
    SEMS.setdefault(group_name + "_s", 1)
    SEMS.setdefault(group_name + "_r", 1)

INPUTS = (
    "tok", "cot", "lens", "freq", "w_in", "w_out", "w_up", "w_down",
    "b_q", "b_v", "b_out", "gain1", "shift1", "b_down", "gain2", "shift2", "b_up",
)
OUTPUTS = (
    "layer_out", "grad_tokens", "g_w_in", "g_b_q", "g_b_v", "g_w_out", "g_b_out",
    "g_gain1", "g_shift1", "g_w_up", "g_b_up", "g_w_down", "g_b_down", "g_gain2", "g_shift2",
)
PACKED = dict(
    lor=((4, 128, 256), BF16),
    gor=((4, 128, 256), BF16),
    r3=((8, 48, 128), BF16),
    r4=((8, 16, 128), BF16),
    vr3=((8, 16, 256), F32),
)
LOADED = INPUTS[3:]
SMALL = ("b_q", "b_v", "b_out", "gain1", "shift1", "b_down", "gain2", "shift2")
ROW = {name: row for row, name in enumerate(SMALL)}


class Refs:
    pass


def kernel(*refs):
    r = Refs()
    held = tuple("v_" + name for name in LOADED)
    names = INPUTS + tuple(PACKED) + held + tuple(SCRATCH) + tuple(SEMS)
    for name, ref in zip(names, refs):
        setattr(r, name, ref)

    gx, gy = lax.axis_index("gx"), lax.axis_index("gy")
    x, y = lax.div(gx, 4), lax.rem(gx, 4)
    z, c = lax.div(gy, 2), lax.rem(gy, 2)
    a = x * (1 - c) + y * c
    b = y * (1 - c) + x * c

    def group(a_at, b_at):
        return a_at * (4 - 3 * c) + b_at * (1 + 3 * c)

    def ring(at, step, size=4):
        return lax.rem(at + (step % size), size)

    def a_peer(step):
        return (group(ring(a, step), b), gy)

    def b_peer(step):
        return (group(a, ring(b, step)), gy)

    def gx_peer(step):
        return (ring(gx, step, 16), gy)

    def z_peer(step):
        return (gx, 2 * ring(z, step) + c)

    def gy_peer(step):
        return (gx, ring(gy, step, 8))

    sibling = (gx, 2 * z + 1 - c)
    here = group(a, b)

    def remote(src, dst, send, recv, device):
        return pltpu.make_async_remote_copy(
            src_ref=src, dst_ref=dst, send_sem=send, recv_sem=recv,
            device_id=device, device_id_type=MESH,
        )

    closing = []

    def sem(name):
        return getattr(r, name).at[0]

    def copy_to(name, src, dst, device, recv=None):
        return remote(src, dst, sem(name + "_s"), recv or sem(name + "_r"), device)

    def sends_end(name, ref):
        closing.append(lambda: remote(ref, ref, sem(name + "_s"), sem(name + "_s"), sibling))

    def await_recv(name, ref, at=0):
        done = getattr(r, name + "_r").at[at]
        remote(ref, ref, done, done, sibling).wait_recv()

    loads = [
        pltpu.make_async_copy(getattr(r, name), getattr(r, "v_" + name), r.in_s.at[i])
        for i, name in enumerate(LOADED)
    ]
    loads.append(pltpu.make_async_copy(r.tok.at[z], r.img.at[z, c], r.in_s.at[14]))
    loads.append(pltpu.make_async_copy(r.cot.at[z], r.cotb.at[z], r.in_s.at[15]))

    barrier = pltpu.get_barrier_semaphore()
    peers = [gx_peer(k) for k in range(1, 16)] + [gy_peer(k) for k in range(1, 8)]
    for peer in peers:
        pl.semaphore_signal(barrier, inc=1, device_id=peer, device_id_type=MESH)
    for load in loads:
        load.start()
    for load in loads:
        load.wait()

    rows = r.v_w_in[...].astype(F32)
    for row in range(2):
        for k in range(6):
            at = 6 * row + k
            r.pf[at : at + 1, :] = rows[row : row + 1, k * 128 : (k + 1) * 128]
    lane = iota((1, 256), 1)
    place = 2 * (8 * gx + gy)
    for i, name in enumerate(("b_q", "b_v")):
        pair = getattr(r, "v_" + name)[...].astype(F32).reshape(1, 2)
        row = jnp.where(lane == place, pair[:, 0:1], 0.0)
        row = jnp.where(lane == place + 1, pair[:, 1:2], row)
        r.pf[12 + 2 * i : 13 + 2 * i, :] = row[:, 0:128]
        r.pf[13 + 2 * i : 14 + 2 * i, :] = row[:, 128:256]
    r.s1[gy, 0:16, :] = r.pf[0:16, :].astype(BF16)

    rows = r.v_w_out[...].astype(F32)
    r.pf[16:32, :] = jnp.zeros((16, 128), F32)
    for row in range(2):
        for k in range(2):
            at = 16 + 2 * row + k
            r.pf[at : at + 1, :] = rows[row : row + 1, k * 128 : (k + 1) * 128]
    thin = iota((1, 128), 1)
    packed = jnp.zeros((1, 128), F32)
    for i, name in enumerate(SMALL):
        pair = getattr(r, "v_" + name)[...].astype(F32).reshape(1, 2)
        packed = jnp.where(thin == 2 * i, pair[:, 0:1], packed)
        packed = jnp.where(thin == 2 * i + 1, pair[:, 1:2], packed)
    up_bias = r.v_b_up[...].astype(F32).reshape(1, 16)
    for k in range(16):
        packed = jnp.where(thin == 16 + k, up_bias[:, k : k + 1], packed)
    r.pf[20:21, :] = packed
    rows = r.v_w_up[...].astype(F32)
    for row in range(2):
        for k in range(16):
            at = 32 + 16 * row + k
            r.pf[at : at + 1, :] = rows[row : row + 1, k * 128 : (k + 1) * 128]
    r.s1[gy, 16:64, :] = r.pf[16:64, :].astype(BF16)
    r.s1[gy, 64:80, :] = r.v_w_down[:, 0:128]
    r.s1[gy, 80:96, :] = r.v_w_down[:, 128:256]
    r.s1[gy, 96:112, :] = r.pf[16:32, :].astype(BF16)

    pl.semaphore_wait(barrier, 22)

    def first_part(at):
        return r.s1.at[at, pl.ds(0, 16)]

    def second_part(at, core):
        return r.s1.at[at, pl.ds(pl.multiple_of(16 + 48 * core, 16), 48)]

    for k in range(1, 8):
        copy_to("s1", first_part(gy), first_part(gy), gy_peer(k)).start()
    sends_end("s1", r.s1.at[pl.ds(0, 7), pl.ds(0, 16)])
    for k in (1, 2, 3):
        copy_to("tk", r.tok.at[ring(z, k)], r.img.at[z, c], z_peer(k), r.tk_r.at[k - 1]).start()
    sends_end("tk", r.cotb.at[pl.ds(0, 3)])
    for k in range(1, 8):
        part = second_part(gy, lax.rem(gy + k, 2))
        copy_to("s2", part, part, gy_peer(k)).start()
    sends_end("s2", r.s1.at[pl.ds(0, 7), pl.ds(0, 48)])
    copy_to("tf", r.img.at[z, c], r.img.at[z, c], sibling).start()

    freq = r.v_freq[...]
    even = lax.rem(iota((1, 256), 1), 2) == 0
    fine = iota((32, 256), 0).astype(F32) * freq
    coarse = iota((32, 256), 0).astype(F32) * 32.0 * freq
    sin_f, cos_f = jnp.sin(fine), jnp.cos(fine)
    sin_c, cos_c = jnp.sin(coarse), jnp.cos(coarse)
    first_c = jnp.where(even, sin_c, cos_c)
    second_c = jnp.where(even, cos_c, -sin_c)

    await_recv("s1", r.s1.at[pl.ds(0, 7), pl.ds(0, 16)])
    bias_low, bias_high = jnp.zeros((1, 128), F32), jnp.zeros((1, 128), F32)
    share0, share1 = (1 - c).astype(F32), c.astype(F32)
    for i in range(8):
        piece = r.s1[i, 0:16, :].astype(F32)
        for row in range(2):
            r.asmf[pl.ds(2 * i + row, 6, stride=16), :] = piece[row * 6 : row * 6 + 6]
        bias_low = bias_low + piece[12:13] * share0 + piece[13:14] * share1
        bias_high = bias_high + piece[14:15] * share0 + piece[15:16] * share1
    for k in range(3):
        rows = r.asmf[pl.ds(pl.multiple_of(32 * k + 16 * c, 16), 16), :]
        r.wio[here, 16 * k : 16 * k + 16, :] = rows.astype(BF16)
    r.wio[here, 48:64, :] = jnp.concatenate(
        [bias_low, bias_high, jnp.zeros((14, 128), F32)], axis=0).astype(BF16)

    def wi_view(at):
        return r.wio.at[at, pl.ds(0, 64)]

    for k in range(1, 16):
        copy_to("wi", wi_view(gx), wi_view(gx), gx_peer(k)).start()
    sends_end("wi", r.wio.at[pl.ds(0, 15), pl.ds(0, 64)])

    await_recv("s2", r.s1.at[pl.ds(0, 7), pl.ds(0, 48)])

    def wo_view(at):
        return r.wio.at[at, pl.ds(64, 48)]

    def ff_view(at):
        return r.ff.at[c, at]

    @pl.when(c == 0)
    def _():
        for i in range(8):
            piece = r.s1[i, 32:64, :].astype(F32)
            for row in range(2):
                r.asmf[pl.ds(128 + 2 * i + row, 16, stride=16), :] = (
                    piece[16 * row : 16 * row + 16])
        for j in range(8):
            for half in range(2):
                at = 128 + 16 * (2 * j + half)
                r.ff[0, here, 16 * j : 16 * j + 16, 128 * half : 128 * half + 128] = (
                    r.asmf[at : at + 16, :].astype(BF16))

    @pl.when(c == 1)
    def _():
        for i in range(8):
            for half in range(2):
                r.ff[1, here, 16 * i : 16 * i + 16, 128 * half : 128 * half + 128] = (
                    r.s1[i, 64 + 16 * half : 80 + 16 * half, :])

    for k in (1, 2, 3):
        copy_to("fa", ff_view(here), ff_view(here), a_peer(k)).start()
    for k in (1, 2, 3):
        copy_to("fb", ff_view(here), ff_view(here), b_peer(k)).start()

    r.asmf[96:112, :] = jnp.zeros((16, 128), F32)
    shared_at = pl.multiple_of(16 + 80 * c, 16)
    for i in range(8):
        piece = r.s1[i, pl.ds(shared_at, 16), :].astype(F32)
        for row in range(2):
            r.asmf[pl.ds(64 + 2 * i + row, 2, stride=16), :] = piece[2 * row : 2 * row + 2]
        r.asmf[96 + i : 97 + i, :] = piece[4:5]
    r.wio[here, 64:112, :] = r.asmf[64:112, :].astype(BF16)
    for k in (1, 2, 3):
        copy_to("wa", wo_view(here), wo_view(here), a_peer(k)).start()
    for k in (1, 2, 3):
        copy_to("wb", wo_view(here), wo_view(here), b_peer(k)).start()

    for k in (1, 2, 3):
        at = ring(z, -k)
        await_recv("tk", r.img.at[at, c], k - 1)
        copy_to("tf", r.img.at[at, c], r.img.at[at, c], sibling).start()
    sends_end("tf", r.img.at[:, 0])
    for k in (1, 2, 3):
        copy_to("ct", r.cot.at[ring(z, k)], r.cotb.at[z], z_peer(k)).start()
    sends_end("ct", r.cotb.at[pl.ds(0, 3)])
    await_recv("tf", r.img.at[:, 1 - c])

    for i in range(8):
        rows = r.img[i // 2, i % 2].astype(F32)
        for k in range(4):
            at = 4 * i + k
            pos = first_c[at : at + 1] * cos_f + second_c[at : at + 1] * sin_f
            r.sh[32 * at : 32 * at + 32, :] = (rows[32 * k : 32 * k + 32] + pos).astype(BF16)
    image = r.img[...].reshape(1024, 256)

    await_recv("fa", r.ff.at[c, pl.ds(0, 3)])
    for i in (1, 2, 3):
        at = group(ring(a, -i), b)
        for k in (1, 2, 3):
            copy_to("fc", ff_view(at), ff_view(at), b_peer(k)).start()
    for i in range(4):
        at = group(ring(a, -i), b)
        copy_to("fw", ff_view(at), ff_view(at), sibling).start()
    await_recv("wa", r.wio.at[pl.ds(0, 3), pl.ds(64, 48)])
    for i in (1, 2, 3):
        at = group(ring(a, -i), b)
        for k in (1, 2, 3):
            copy_to("wb", wo_view(at), wo_view(at), b_peer(k)).start()
    sends_end("fa", r.ff.at[c, pl.ds(0, 3)])
    sends_end("fb", r.ff.at[c, pl.ds(0, 3)])
    sends_end("fc", r.ff.at[c, pl.ds(0, 9)])
    sends_end("fw", r.ff.at[c])
    sends_end("wa", r.wio.at[pl.ds(0, 3), pl.ds(64, 48)])
    sends_end("wb", r.wio.at[pl.ds(0, 12), pl.ds(64, 48)])

    r.sht[...] = r.sh[...].T
    r.imgt[...] = image.T

    await_recv("wi", r.wio.at[pl.ds(0, 15), pl.ds(0, 64)])
    biases = jnp.zeros((16, 128), F32)
    for i in range(16):
        biases = biases + r.wio[i, 48:64, :].astype(F32)

    def w_part(k):
        return r.wio[:, 16 * k : 16 * k + 16, :].reshape(256, 128)

    queries = (dot(r.sh[...], w_part(0)) + biases[0:1]).astype(BF16)
    keys = dot(r.sh[...], w_part(1)).astype(BF16)
    values = (dot(image, w_part(2)) + biases[1:2]).astype(BF16)
    r.qq[...] = queries
    r.vv[...] = values
    r.kt[...] = keys.T
    r.vt[...] = values.T
    r.qt[0:128, :] = queries.T
    ones_row = iota((128, 1024), 0) == 0
    r.qt[128:256, :] = jnp.where(ones_row, 1.0, 0.0).astype(BF16)

    length = r.lens[z]

    zero = jnp.zeros((), BF16)
    head_of_lane = lax.div(iota((1024, 128), 1), HD)
    hidden_key = (iota((1024, 128), 0) >= length) & (iota((1024, 128), 1) == 0)
    bias = jnp.where(hidden_key, -1e30, 0.0).astype(BF16)
    for head in range(4):
        r.kx[head, :, 0:128] = jnp.where(head_of_lane == head, keys, zero)
        r.kx[head, :, 128:256] = bias

    for head in range(4):
        peak = None
        for k in range(0, 1024, 512):
            part = jnp.max(dot(r.kx[head, k : k + 512, :], r.qt[...]), axis=0, keepdims=True)
            peak = part if peak is None else jnp.maximum(peak, part)
        scores = dot(r.kx[head], r.qt[...])
        weights = jnp.exp2(scores * EXP2_SCALE - peak * EXP2_SCALE).astype(BF16)
        r.ee[head] = weights
        rows = slice(head * HD, head * HD + HD)
        left = jnp.concatenate([r.vt[rows, :], jnp.ones((16, 1024), BF16)], axis=0)
        mixed = dot(left, weights)
        inverse = 1.0 / mixed[HD : HD + 1]
        r.ot[rows, :] = mixed[0:HD] * inverse
        r.ri[head : head + 1, :] = inverse
        if head == 2:
            await_recv("fb", r.ff.at[c, pl.ds(0, 3)])
            for k in (1, 2, 3):
                at = group(a, ring(b, -k))
                copy_to("fw", ff_view(at), ff_view(at), sibling).start()

    r.mx[...] = r.ot[...].T.astype(BF16).reshape(4, 2, 128, 128)
    copy_to("mx", r.mx.at[:, 1 - c], r.mr, sibling).start()
    sends_end("mx", r.mr)

    await_recv("fc", r.ff.at[c, pl.ds(0, 9)])
    for i in (1, 2, 3):
        for k in (1, 2, 3):
            at = group(ring(a, -i), ring(b, -k))
            copy_to("fw", ff_view(at), ff_view(at), sibling).start()

    await_recv("wb", r.wio.at[pl.ds(0, 12), pl.ds(64, 48)])
    rows = r.wio[:, 96:112, :].reshape(256, 128)
    spot_row, spot_lane = iota((256, 256), 0), iota((256, 256), 1)
    pick = spot_row == 16 * lax.div(spot_lane, 16) + lax.div(lax.rem(spot_lane, 16), 2)
    spread = dot_tn(rows, jnp.where(pick, 1.0, 0.0).astype(BF16))
    even_lane = lax.rem(iota((1, 256), 1), 2) == 0
    for i in range(8):
        r.vecs[i : i + 1, :] = jnp.where(
            even_lane, spread[2 * i : 2 * i + 1], spread[2 * i + 1 : 2 * i + 2])
    tile = iota((128, 256), 0) == 16 + lax.rem(iota((128, 256), 1), 16)
    wide = dot(rows, jnp.where(tile, 1.0, 0.0).astype(BF16))
    keep = lax.rem(spot_row, 32) == (
        16 * lax.div(spot_lane, 128) + lax.rem(lax.div(spot_lane, 16), 8))
    wide = jnp.where(keep, wide, 0.0).reshape(8, 32, 256)
    r.vecs[8:16, :] = jnp.sum(wide, axis=1)

    for head in range(4):
        r.vx[head, :, 0:128] = jnp.where(head_of_lane == head, r.vv[...], zero)
        r.vx[head, :, 128:256] = jnp.where(
            lax.div(iota((1024, 128), 1), 2) == head, 1.0, 0.0).astype(BF16)
        r.qm[head] = jnp.where(head_of_lane == head, r.qq[...], zero)

    def w_out_rows(half):
        low = r.wio[pl.ds(8 * half, 8), 64:80, :].reshape(128, 128)
        high = r.wio[pl.ds(8 * half, 8), 80:96, :].reshape(128, 128)
        return jnp.concatenate([low, high], axis=1)

    def vec(name):
        return r.vecs[ROW[name] : ROW[name] + 1, :]

    mixed_own = r.mx[:, c].reshape(512, 128)
    branch = dot(mixed_own, w_out_rows(c))
    await_recv("mx", r.mr)
    mixed_other = r.mr[...].reshape(512, 128)
    branch = branch + dot(mixed_other, w_out_rows(1 - c))
    first_sum = r.img[:, c].reshape(512, 256).astype(F32) + branch + vec("b_out")
    hidden, unit, inverse = norm_forward(first_sum, vec("gain1"), vec("shift1"))
    r.unit1[...] = unit
    r.inv1[...] = inverse
    r.hid[...] = hidden
    hidden_low = hidden.astype(BF16)
    r.hlow[...] = hidden_low
    r.hlt[...] = hidden_low.T

    await_recv("fw", r.ff.at[1 - c])

    def up_block(j):
        parts = [r.ff[0, :, 16 * k : 16 * k + 16, :].reshape(256, 256) for k in (2 * j, 2 * j + 1)]
        return jnp.concatenate(parts, axis=1)

    def down_block(j):
        return r.ff[1, 4 * j : 4 * j + 4, :, :].reshape(512, 256)

    r.acc[...] = r.hid[...] + vec("b_down")
    for j in range(4):
        up_shift = jnp.concatenate(
            [r.vecs[8 + 2 * j : 9 + 2 * j, :], r.vecs[9 + 2 * j : 10 + 2 * j, :]], axis=1)
        up = dot(r.hlow[...], up_block(j)) + up_shift
        square = up * up
        gate = 0.5 + 0.5 * jnp.tanh(up * (GELU_SCALE + GELU_SCALE * 0.044715 * square))
        active = up * gate
        slope = 2 * GELU_SCALE + 6 * 0.044715 * GELU_SCALE * square
        r.dgl[j] = (gate + active * (1.0 - gate) * slope).astype(BF16)
        active = active.astype(BF16)
        r.act[j] = active
        r.acc[...] += dot(active, down_block(j))

    out, unit, inverse = norm_forward(r.acc[...], vec("gain2"), vec("shift2"))
    r.lob[...] = out.astype(BF16).reshape(4, 128, 256)
    for k in (1, 2, 3):
        copy_to("lo", r.lob.at[ring(z, k)], r.lor.at[z], z_peer(k)).start()
    sends_end("lo", r.lob.at[pl.ds(0, 3)])
    own_copies = [pltpu.make_async_copy(r.lob.at[z], r.lor.at[z], r.own_s.at[0])]
    own_copies[0].start()

    await_recv("ct", r.cotb.at[pl.ds(0, 3)])
    d_out = r.cotb[...].reshape(512, 256).astype(F32)
    r.gv[ROW["gain2"] : ROW["gain2"] + 1, :] = column_sum(d_out * unit)
    r.gv[ROW["shift2"] : ROW["shift2"] + 1, :] = column_sum(d_out)
    d_second = norm_backward(d_out, unit, inverse, vec("gain2"))
    d_ffn = d_second.astype(BF16)
    r.dffn[...] = d_ffn
    r.gv[ROW["b_down"] : ROW["b_down"] + 1, :] = column_sum(d_ffn.astype(F32))
    r.acc[...] = d_second

    for j in range(4):
        d_active = dot_nt(r.dffn[...], down_block(j))
        d_up = (d_active * r.dgl[j].astype(F32)).astype(BF16)
        g_down = dot_tn(r.act[j], r.dffn[...])
        r.gp[1, 4 * j : 4 * j + 4] = g_down.astype(BF16).reshape(4, 128, 256)
        g_up = dot(r.hlt[...], d_up).astype(BF16)
        sums = column_sum(d_up.astype(F32))
        for k in range(2):
            at, lanes = 2 * j + k, slice(256 * k, 256 * k + 256)
            r.gp[0, :, 16 * at : 16 * at + 16, :] = g_up[:, lanes].reshape(16, 16, 256)
            r.gv[8 + at : 9 + at, :] = sums[:, lanes]
        r.acc[...] += dot_nt(d_up, up_block(j))

        @pl.when(c == 0)
        def _():
            part = pl.ds(4 * j, 4)
            copy_to("gs", r.gp.at[1, part], r.gs.at[part], sibling).start()

        @pl.when(c == 1)
        def _():
            part = pl.ds(32 * j, 32)
            copy_to("gs", r.gp.at[0, :, part], r.gs.at[:, part], sibling).start()

    sends_end("gs", r.gs)

    d_hidden = r.acc[...]
    unit = r.unit1[...]
    r.gv[ROW["gain1"] : ROW["gain1"] + 1, :] = column_sum(d_hidden * unit)
    r.gv[ROW["shift1"] : ROW["shift1"] + 1, :] = column_sum(d_hidden)
    d_first = norm_backward(d_hidden, unit, r.inv1[...], vec("gain1"))
    r.dfirst[...] = d_first
    d_branch = d_first.astype(BF16)
    r.gv[ROW["b_out"] : ROW["b_out"] + 1, :] = column_sum(d_branch.astype(F32))
    r.dms[...] = dot_nt(d_branch, w_out_rows(1 - c)).astype(BF16).reshape(4, 128, 128)
    copy_to("dm", r.dms, r.dmx.at[:, c], sibling).start()
    sends_end("dm", r.dms)
    r.dmx[:, c] = dot_nt(d_branch, w_out_rows(c)).astype(BF16).reshape(4, 128, 128)

    def spot(g):
        return g * (1 - c) + (4 * lax.rem(g, 4) + lax.div(g, 4)) * c

    for half, mixed in ((c, r.mx[:, c].reshape(512, 128)), (1 - c, r.mr[...].reshape(512, 128))):
        g_out = dot_tn(mixed, d_branch).astype(BF16)
        for i in range(8):
            at = spot(8 * half + i)
            r.gwo[at, 0:16, :] = g_out[16 * i : 16 * i + 16, 0:128]
            r.gwo[at, 16:32, :] = g_out[16 * i : 16 * i + 16, 128:256]
    r.gv[0:2, :] = jnp.zeros((2, 256), F32)
    r.v0[...] = r.gv[...]

    await_recv("gs", r.gs)

    def add_cores(i, carry):
        at = group(lax.div(i, 4), lax.rem(i, 4))
        r.rs[i] = (r.gp[c, at].astype(F32) + r.gs[at].astype(F32)).astype(BF16)
        return carry

    lax.fori_loop(0, 16, add_cores, 0)

    for k in (1, 2, 3):
        part, to = pl.ds(4 * ring(a, k), 4), a_peer(k)
        copy_to("r1", r.rs.at[part], r.r1.at[k - 1], to).start()
        copy_to("g1", r.gwo.at[part], r.wo1.at[k - 1], to).start()
        copy_to("v1", r.v0, r.vr1.at[k - 1], to).start()
    sends_end("r1", r.r1)
    sends_end("g1", r.wo1)
    sends_end("v1", r.vr1)

    await_recv("dm", r.dmx.at[:, 1 - c])
    d_mixed_t = r.dmx[...].reshape(1024, 128).astype(F32).T
    extra = []
    for head in range(4):
        rows = slice(32 * head, 32 * head + 32)
        scaled = d_mixed_t[rows] * r.ri[head : head + 1, :]
        r.dot_[rows, :] = scaled.astype(BF16)
        inner = -column_sum(scaled * r.ot[rows, :])
        high = inner.astype(BF16).astype(F32)
        extra += [high, inner - high]
    extra.append(jnp.zeros((8, 1024), F32))
    r.dot_[128:144, :] = jnp.concatenate(extra, axis=0).astype(BF16)
    r.dot_[144:256, :] = jnp.zeros((112, 1024), BF16)
    r.doo[...] = r.dot_[0:128, :].T

    for head in range(4):
        d_probs = dot(r.vx[head], r.dot_[...])
        d_scores = r.ee[head] * d_probs.astype(BF16)
        r.ds[head % 2] = d_scores
        rows = slice(head * HD, head * HD + HD)
        r.dqt[rows, :] = dot(r.kt[rows, :], d_scores)
        do_masked = jnp.where(head_of_lane == head, r.doo[...], zero)
        for k in range(0, 1024, 256):
            d_key = dot(r.ds[head % 2, k : k + 256, :], r.qm[head])
            d_value = dot(r.ee[head, k : k + 256, :], do_masked)
            if head == 0:
                r.dk[k : k + 256, :] = d_key
                r.dv[k : k + 256, :] = d_value
            else:
                r.dk[k : k + 256, :] += d_key
                r.dv[k : k + 256, :] += d_value

    d_queries = (r.dqt[...] * SCORE_SCALE).T.astype(BF16)
    d_keys = (r.dk[...] * SCORE_SCALE).astype(BF16)
    d_values = r.dv[...].astype(BF16)
    for k, (left, right) in enumerate(((r.sht, d_queries), (r.sht, d_keys), (r.imgt, d_values))):
        g_part = dot(left[...], right).astype(BF16)
        for i in range(16):
            r.gio[i, 16 * k : 16 * k + 16, :] = g_part[16 * i : 16 * i + 16, :]
    ones = jnp.ones((1024, 128), BF16)
    sums = jnp.where(
        iota((128, 128), 1) < 64, dot_tn(d_queries, ones), dot_tn(d_values, ones)).astype(BF16)
    for i in range(8):
        r.gio[8 * c + i, 48:64, :] = sums[16 * i : 16 * i + 16, :]
        r.gio[8 * (1 - c) + i, 48:64, :] = jnp.zeros((16, 128), BF16)
    for k in range(1, 16):
        copy_to("q1", r.gio.at[ring(gx, k, 16)], r.q1.at[gx], gx_peer(k)).start()
    sends_end("q1", r.q1.at[pl.ds(0, 15)])

    d_tokens = (
        dot_nt(d_queries, w_part(0)) + dot_nt(d_keys, w_part(1)) + dot_nt(d_values, w_part(2)))
    r.gt[...] = d_tokens.astype(BF16).reshape(4, 2, 128, 256)
    copy_to("gt", r.gt.at[:, 1 - c], r.gtr, sibling).start()
    sends_end("gt", r.gtr)

    await_recv("r1", r.r1)
    await_recv("g1", r.wo1)
    await_recv("v1", r.vr1)

    def add_first(i, carry):
        total = r.rs[4 * a + i].astype(F32)
        small = r.gwo[4 * a + i].astype(F32)
        for k in range(3):
            total = total + r.r1[k, i].astype(F32)
            small = small + r.wo1[k, i].astype(F32)
        r.s2[i] = total.astype(BF16)
        r.wos[i] = small.astype(BF16)
        return carry

    lax.fori_loop(0, 4, add_first, 0)
    r.v1[...] = r.v0[...] + r.vr1[0] + r.vr1[1] + r.vr1[2]
    for k in (1, 2, 3):
        part, to = ring(b, k), b_peer(k)
        copy_to("r2", r.s2.at[part], r.r2.at[k - 1], to).start()
        copy_to("g2", r.wos.at[part], r.wo2.at[k - 1], to).start()
        copy_to("v2", r.v1, r.vr2.at[k - 1], to).start()
    sends_end("r2", r.r2)
    sends_end("g2", r.wo2)
    sends_end("v2", r.vr2)

    await_recv("gt", r.gtr)
    full = (
        r.dfirst[...]
        + r.gt[:, c].reshape(512, 256).astype(F32)
        + r.gtr[...].reshape(512, 256).astype(F32))
    r.gob[...] = full.astype(BF16).reshape(4, 128, 256)
    for k in (1, 2, 3):
        copy_to("go", r.gob.at[ring(z, k)], r.gor.at[z], z_peer(k)).start()
    sends_end("go", r.gob.at[pl.ds(0, 3)])

    await_recv("r2", r.r2)
    await_recv("g2", r.wo2)
    await_recv("v2", r.vr2)
    total = r.s2[b].astype(F32)
    small = r.wos[b].astype(F32)
    for k in range(3):
        total = total + r.r2[k].astype(F32)
        small = small + r.wo2[k].astype(F32)
    r.fin[0] = total[:, 0:128]
    r.fin[1] = total[:, 128:256]
    r.fwo[...] = small
    r.v2[...] = r.v1[...] + r.vr2[0] + r.vr2[1] + r.vr2[2]
    r.p3f[...] = jnp.zeros((8, 48, 128), F32)

    @pl.when(c == 0)
    def _():
        for i in range(8):
            for half in range(2):
                for row in range(2):
                    at = 16 * half + 8 * row
                    r.p3f[i, at : at + 8, :] = r.fin.at[half][
                        pl.ds(2 * i + row, 8, stride=16), :]

    @pl.when(c == 1)
    def _():
        for i in range(8):
            for half in range(2):
                r.p3f[i, 16 * half : 16 * half + 16, :] = r.fin[half, 16 * i : 16 * i + 16, :]

    for i in range(8):
        for row in range(2):
            at = 32 + 8 * row
            r.p3f[i, at : at + 2, :] = r.fwo[pl.ds(2 * i + row, 2, stride=16), :]
    r.p3[...] = r.p3f[...].astype(BF16)
    for k in range(1, 8):
        copy_to("p3", r.p3.at[ring(gy, k, 8)], r.r3.at[gy], gy_peer(k)).start()
        copy_to("v3", r.v2, r.vr3.at[gy], gy_peer(k)).start()
    sends_end("p3", r.p3.at[pl.ds(0, 7)])
    sends_end("v3", r.vr3.at[pl.ds(0, 7)])

    await_recv("q1", r.q1.at[pl.ds(0, 15)])
    total = r.gio[gx].astype(F32)
    for k in range(1, 16):
        total = total + r.q1[ring(gx, -k, 16)].astype(F32)
    r.fio[...] = total
    r.p4f[...] = jnp.zeros((8, 16, 128), F32)
    for i in range(8):
        for row in range(2):
            at = 8 * row
            r.p4f[i, at : at + 4, :] = r.fio[pl.ds(2 * i + row, 4, stride=16), :]
    r.p4[...] = r.p4f[...].astype(BF16)
    for k in range(1, 8):
        copy_to("p4", r.p4.at[ring(gy, k, 8)], r.r4.at[gy], gy_peer(k)).start()
    sends_end("p4", r.p4.at[pl.ds(0, 7)])

    own_copies += [
        pltpu.make_async_copy(r.gob.at[z], r.gor.at[z], r.own_s.at[1]),
        pltpu.make_async_copy(r.p3.at[gy], r.r3.at[gy], r.own_s.at[2]),
        pltpu.make_async_copy(r.p4.at[gy], r.r4.at[gy], r.own_s.at[3]),
        pltpu.make_async_copy(r.v2, r.vr3.at[gy], r.own_s.at[4]),
    ]
    for copy in own_copies[1:]:
        copy.start()
    await_recv("lo", r.lor.at[pl.ds(0, 3)])
    await_recv("go", r.gor.at[pl.ds(0, 3)])
    await_recv("p3", r.r3.at[pl.ds(0, 7)])
    await_recv("v3", r.vr3.at[pl.ds(0, 7)])
    await_recv("p4", r.r4.at[pl.ds(0, 7)])
    for copy in own_copies:
        copy.wait()
    for make in closing:
        make().wait_send()


def unpack(*refs):
    r = Refs()
    for name, ref in zip(tuple(PACKED) + OUTPUTS, refs):
        setattr(r, name, ref)
    gx, gy = lax.axis_index("gx"), lax.axis_index("gy")
    place = 2 * (8 * gx + gy)
    up_place = 128 * lax.rem(gx, 2) + 16 * gy
    r.layer_out[...] = r.lor[...]
    r.grad_tokens[...] = r.gor[...].astype(F32)
    core0 = jnp.zeros((48, 128), F32)
    core1 = jnp.zeros((48, 128), F32)
    into0 = jnp.zeros((16, 128), F32)
    into1 = jnp.zeros((16, 128), F32)
    total = jnp.zeros((16, 256), F32)
    for i in range(4):
        core0 = core0 + r.r3[2 * i].astype(F32)
        core1 = core1 + r.r3[2 * i + 1].astype(F32)
        into0 = into0 + r.r4[2 * i].astype(F32)
        into1 = into1 + r.r4[2 * i + 1].astype(F32)
        total = total + r.vr3[2 * i] + r.vr3[2 * i + 1]
    r.g_w_down[:, 0:128] = core1[0:16]
    r.g_w_down[:, 128:256] = core1[16:32]
    w_out = core0 + core1
    for row in range(2):
        out_row = slice(row, row + 1)
        for j in range(8):
            for half in range(2):
                at = 16 * half + 8 * row + j
                lanes = 256 * j + 128 * half
                r.g_w_up[out_row, lanes : lanes + 128] = core0[at : at + 1]
        for k in range(3):
            at = 8 * row + k
            r.g_w_in[out_row, 256 * k : 256 * k + 128] = into0[at : at + 1]
            r.g_w_in[out_row, 256 * k + 128 : 256 * k + 256] = into1[at : at + 1]
        at = 32 + 8 * row
        r.g_w_out[out_row, 0:128] = w_out[at : at + 1]
        r.g_w_out[out_row, 128:256] = w_out[at + 1 : at + 2]
    biases = into0 + into1
    for name, lane in (("b_q", 0), ("b_v", 64)):
        pair = jnp.concatenate(
            [biases[3:4, lane : lane + 1], biases[11:12, lane : lane + 1]], axis=1)
        getattr(r, "g_" + name)[...] = pair.reshape(2)
    moved = pltpu.roll(total, lax.rem(256 - place, 256), axis=1)
    for name in SMALL[2:]:
        row = ROW[name]
        getattr(r, "g_" + name)[...] = moved[row : row + 1, 0:2].reshape(2)
    up_total = column_sum(jnp.where(iota((8, 256), 0) == lax.div(gx, 2), total[8:16], 0.0))
    up_total = jnp.broadcast_to(up_total, (8, 256))
    up_total = pltpu.roll(up_total, lax.rem(256 - up_place, 256), axis=1)
    r.g_b_up[...] = up_total[0:1, 0:16].reshape(16)


def body(
    tokens, lengths, w_in, b_q, b_v, w_out, b_out, gain_first, shift_first, w_up, b_up,
    w_down, b_down, gain_second, shift_second, cotangent,
):
    column = np.arange(D)
    freq = np.power(10000.0, -(2.0 * (column // 2)) / D).astype(np.float32)[None, :]
    args = (
        tokens, cotangent, lengths, jnp.asarray(freq), w_in, w_out, w_up, w_down,
        b_q, b_v, b_out, gain_first, shift_first, b_down, gain_second, shift_second, b_up,
    )
    vmem = pl.BlockSpec(memory_space=pltpu.VMEM)
    anywhere = pl.BlockSpec(memory_space=pl.ANY)
    in_specs = [anywhere] * len(args)
    in_specs[2] = pl.BlockSpec(memory_space=pltpu.SMEM)
    shape = jax.ShapeDtypeStruct
    vector = shape((2,), F32)
    scratch = [pltpu.VMEM(args[INPUTS.index(name)].shape, args[INPUTS.index(name)].dtype)
               for name in LOADED]
    scratch += [pltpu.VMEM(dims, kind) for dims, kind in SCRATCH.values()]
    scratch += [pltpu.SemaphoreType.DMA((count,)) for count in SEMS.values()]
    packed = pl.pallas_call(
        kernel,
        out_shape=tuple(shape(dims, kind) for dims, kind in PACKED.values()),
        in_specs=in_specs,
        out_specs=tuple([anywhere] * len(PACKED)),
        scratch_shapes=scratch,
        compiler_params=pltpu.CompilerParams(
            collective_id=0, has_side_effects=True, vmem_limit_bytes=VMEM_LIMIT),
        name="encoder_layer",
    )(*args)
    out_shape = (
        shape((4, 128, 256), BF16), shape((4, 128, 256), F32), shape((2, 768), F32),
        vector, vector, shape((2, 256), F32), vector, vector, vector,
        shape((2, 2048), F32), shape((16,), F32), shape((16, 256), F32),
        vector, vector, vector,
    )
    return pl.pallas_call(
        unpack,
        out_shape=out_shape,
        in_specs=[vmem] * len(packed),
        out_specs=tuple([vmem] * len(out_shape)),
        name="unpack_results",
    )(*packed)


def solution(mesh):
    both = ("gx", "gy")
    rows, vector, whole = P(both, None), P(both), P("gx", "gy", None)
    return jax.shard_map(
        body,
        mesh=mesh,
        in_specs=(
            whole, P("gx"), rows, vector, vector, rows, vector, vector, vector, rows, vector,
            rows, vector, vector, vector, whole,
        ),
        out_specs=(
            whole, whole, rows, vector, vector, rows, vector, vector, vector, rows, vector,
            rows, vector, vector, vector,
        ),
        check_vma=False,
    )
```

```python
import math

import jax
import jax.numpy as jnp
import numpy as np
from jax import lax
from jax.experimental import pallas as pl
from jax.experimental.pallas import tpu as pltpu
from jax.sharding import PartitionSpec as P

MESH = pl.DeviceIdType.MESH
F32 = jnp.float32
BF16 = jnp.bfloat16

D = 256
HD = 32
VMEM_LIMIT = 56 * 2**20
EPSILON = 1e-05
GELU_SCALE = math.sqrt(2.0 / math.pi)
SCORE_SCALE = 1.0 / math.sqrt(HD)
EXP2_SCALE = SCORE_SCALE * math.log2(math.e)


def dot(left, right):
    return jnp.dot(left, right, preferred_element_type=F32)


def dot_nt(left, right):
    return lax.dot_general(left, right, (((1,), (1,)), ((), ())), preferred_element_type=F32)


def dot_tn(left, right):
    return lax.dot_general(left, right, (((0,), (0,)), ((), ())), preferred_element_type=F32)


def iota(shape, dim):
    return lax.broadcasted_iota(jnp.int32, shape, dim)


def column_sum(values):
    return jnp.sum(values, axis=0, keepdims=True)


def norm_forward(values, gain, shift):
    centre = jnp.mean(values, axis=-1, keepdims=True)
    moved = values - centre
    spread = jnp.mean(moved * moved, axis=-1, keepdims=True)
    inverse = lax.rsqrt(spread + EPSILON)
    unit = moved * inverse
    return unit * gain + shift, unit, inverse


def norm_backward(d_out, unit, inverse, gain):
    d_unit = d_out * gain
    mean_d = jnp.mean(d_unit, axis=-1, keepdims=True)
    mean_du = jnp.mean(d_unit * unit, axis=-1, keepdims=True)
    return inverse * (d_unit - mean_d - unit * mean_du)


SCRATCH = dict(
    pf=((112, 128), F32),
    s1=((8, 112, 128), BF16),
    asmf=((384, 128), F32),
    img=((4, 2, 128, 256), BF16),
    cotb=((4, 128, 256), BF16),
    wio=((16, 112, 128), BF16),
    ff=((2, 16, 128, 256), BF16),
    vecs=((16, 256), F32),
    sh=((1024, 256), BF16),
    sht=((256, 1024), BF16),
    imgt=((256, 1024), BF16),
    kx=((4, 1024, 256), BF16),
    vx=((4, 1024, 256), BF16),
    qm=((4, 1024, 128), BF16),
    vv=((1024, 128), BF16),
    qq=((1024, 128), BF16),
    kt=((128, 1024), BF16),
    vt=((128, 1024), BF16),
    qt=((256, 1024), BF16),
    ee=((4, 1024, 1024), BF16),
    ot=((128, 1024), F32),
    ri=((8, 1024), F32),
    mx=((4, 2, 128, 128), BF16),
    mr=((4, 128, 128), BF16),
    hid=((512, 256), F32),
    hlow=((512, 256), BF16),
    hlt=((256, 512), BF16),
    unit1=((512, 256), F32),
    inv1=((512, 1), F32),
    act=((4, 512, 512), BF16),
    dgl=((4, 512, 512), BF16),
    acc=((512, 256), F32),
    lob=((4, 128, 256), BF16),
    dffn=((512, 256), BF16),
    gp=((2, 16, 128, 256), BF16),
    gs=((16, 128, 256), BF16),
    rs=((16, 128, 256), BF16),
    r1=((3, 4, 128, 256), BF16),
    s2=((4, 128, 256), BF16),
    r2=((3, 128, 256), BF16),
    fin=((2, 128, 128), F32),
    gv=((16, 256), F32),
    dfirst=((512, 256), F32),
    dms=((4, 128, 128), BF16),
    dmx=((4, 2, 128, 128), BF16),
    dot_=((256, 1024), BF16),
    doo=((1024, 128), BF16),
    ds=((2, 1024, 1024), BF16),
    dqt=((128, 1024), F32),
    dk=((1024, 128), F32),
    dv=((1024, 128), F32),
    gwo=((16, 32, 128), BF16),
    wo1=((3, 4, 32, 128), BF16),
    wos=((4, 32, 128), BF16),
    wo2=((3, 32, 128), BF16),
    fwo=((32, 128), F32),
    gio=((16, 64, 128), BF16),
    q1=((16, 64, 128), BF16),
    fio=((64, 128), F32),
    v0=((16, 256), F32),
    vr1=((3, 16, 256), F32),
    v1=((16, 256), F32),
    vr2=((3, 16, 256), F32),
    gt=((4, 2, 128, 256), BF16),
    gtr=((4, 128, 256), BF16),
    gob=((4, 128, 256), BF16),
    p3f=((8, 48, 128), F32),
    p3=((8, 48, 128), BF16),
    p4f=((8, 16, 128), F32),
    p4=((8, 16, 128), BF16),
)

GROUPS = (
    "s1", "s2", "tk", "tf", "ct", "ia", "ib", "wa", "wb", "fa", "fb", "fc", "fw", "mx", "dm", "lo",
    "gs", "r1", "r2", "g1", "g2", "v1", "v2", "q1", "gt", "go", "p3", "p4",
)
SEMS = dict(in_s=16, own_s=4, tk_r=3, fc_r=3)
for group_name in GROUPS:
    SEMS.setdefault(group_name + "_s", 1)
    SEMS.setdefault(group_name + "_r", 1)

INPUTS = (
    "tok", "cot", "lens", "freq", "w_in", "w_out", "w_up", "w_down",
    "b_q", "b_v", "b_out", "gain1", "shift1", "b_down", "gain2", "shift2", "b_up",
)
OUTPUTS = (
    "layer_out", "grad_tokens", "g_w_in", "g_b_q", "g_b_v", "g_w_out", "g_b_out",
    "g_gain1", "g_shift1", "g_w_up", "g_b_up", "g_w_down", "g_b_down", "g_gain2", "g_shift2",
)
PACKED = dict(
    lor=((4, 128, 256), BF16),
    gor=((4, 128, 256), BF16),
    r3=((8, 48, 128), BF16),
    r4=((8, 16, 128), BF16),
)
LOADED = INPUTS[3:]
SMALL = ("b_q", "b_v", "b_out", "gain1", "shift1", "b_down", "gain2", "shift2")
ROW = {name: row for row, name in enumerate(SMALL)}


class Refs:
    pass


def kernel(*refs):
    r = Refs()
    held = tuple("v_" + name for name in LOADED)
    names = INPUTS + tuple(PACKED) + held + tuple(SCRATCH) + tuple(SEMS)
    for name, ref in zip(names, refs):
        setattr(r, name, ref)

    gx, gy = lax.axis_index("gx"), lax.axis_index("gy")
    x, y = lax.div(gx, 4), lax.rem(gx, 4)
    z, c = lax.div(gy, 2), lax.rem(gy, 2)
    a = x * (1 - c) + y * c
    b = y * (1 - c) + x * c

    def group(a_at, b_at):
        return a_at * (4 - 3 * c) + b_at * (1 + 3 * c)

    def ring(at, step, size=4):
        return lax.rem(at + (step % size), size)

    def a_peer(step):
        return (group(ring(a, step), b), gy)

    def b_peer(step):
        return (group(a, ring(b, step)), gy)

    def gx_peer(step):
        return (ring(gx, step, 16), gy)

    def z_peer(step):
        return (gx, 2 * ring(z, step) + c)

    def gy_peer(step):
        return (gx, ring(gy, step, 8))

    sibling = (gx, 2 * z + 1 - c)
    here = group(a, b)

    def remote(src, dst, send, recv, device):
        return pltpu.make_async_remote_copy(
            src_ref=src, dst_ref=dst, send_sem=send, recv_sem=recv,
            device_id=device, device_id_type=MESH,
        )

    closing = []

    def sem(name):
        return getattr(r, name).at[0]

    def copy_to(name, src, dst, device, recv=None):
        return remote(src, dst, sem(name + "_s"), recv or sem(name + "_r"), device)

    def sends_end(name, ref):
        closing.append(lambda: remote(ref, ref, sem(name + "_s"), sem(name + "_s"), sibling))

    def await_recv(name, ref, at=0):
        done = getattr(r, name + "_r").at[at]
        remote(ref, ref, done, done, sibling).wait_recv()

    loads = [
        pltpu.make_async_copy(getattr(r, name), getattr(r, "v_" + name), r.in_s.at[i])
        for i, name in enumerate(LOADED)
    ]
    loads.append(pltpu.make_async_copy(r.tok.at[z], r.img.at[z, c], r.in_s.at[14]))
    loads.append(pltpu.make_async_copy(r.cot.at[z], r.cotb.at[z], r.in_s.at[15]))

    barrier = pltpu.get_barrier_semaphore()
    peers = [gy_peer(k) for k in (4, 5, 3, 2, 6, 1, 7)]
    peers += [a_peer(k) for k in (2, 1, 3)] + [b_peer(k) for k in (2, 1, 3)]
    for peer in peers:
        pl.semaphore_signal(barrier, inc=1, device_id=peer, device_id_type=MESH)
    for load in loads:
        load.start()
    for load in loads:
        load.wait()

    rows = r.v_w_in[...].astype(F32)
    for row in range(2):
        for k in range(6):
            at = 6 * row + k
            r.pf[at : at + 1, :] = rows[row : row + 1, k * 128 : (k + 1) * 128]
    lane = iota((1, 256), 1)
    place = 2 * (8 * gx + gy)
    for i, name in enumerate(("b_q", "b_v")):
        pair = getattr(r, "v_" + name)[...].astype(F32).reshape(1, 2)
        row = jnp.where(lane == place, pair[:, 0:1], 0.0)
        row = jnp.where(lane == place + 1, pair[:, 1:2], row)
        r.pf[12 + 2 * i : 13 + 2 * i, :] = row[:, 0:128]
        r.pf[13 + 2 * i : 14 + 2 * i, :] = row[:, 128:256]
    r.s1[gy, 0:16, :] = r.pf[0:16, :].astype(BF16)

    rows = r.v_w_out[...].astype(F32)
    r.pf[16:32, :] = jnp.zeros((16, 128), F32)
    for row in range(2):
        for k in range(2):
            at = 16 + 2 * row + k
            r.pf[at : at + 1, :] = rows[row : row + 1, k * 128 : (k + 1) * 128]
    thin = iota((1, 128), 1)
    packed = jnp.zeros((1, 128), F32)
    for i, name in enumerate(SMALL):
        pair = getattr(r, "v_" + name)[...].astype(F32).reshape(1, 2)
        packed = jnp.where(thin == 2 * i, pair[:, 0:1], packed)
        packed = jnp.where(thin == 2 * i + 1, pair[:, 1:2], packed)
    up_bias = r.v_b_up[...].astype(F32).reshape(1, 16)
    for k in range(16):
        packed = jnp.where(thin == 16 + k, up_bias[:, k : k + 1], packed)
    r.pf[20:21, :] = packed
    rows = r.v_w_up[...].astype(F32)
    for row in range(2):
        for k in range(16):
            at = 32 + 16 * row + k
            r.pf[at : at + 1, :] = rows[row : row + 1, k * 128 : (k + 1) * 128]
    r.s1[gy, 16:64, :] = r.pf[16:64, :].astype(BF16)
    r.s1[gy, 64:80, :] = r.v_w_down[:, 0:128]
    r.s1[gy, 80:96, :] = r.v_w_down[:, 128:256]
    r.s1[gy, 96:112, :] = r.pf[16:32, :].astype(BF16)

    pl.semaphore_wait(barrier, 13)

    def first_part(at):
        return r.s1.at[at, pl.ds(0, 16)]

    def second_part(at, core):
        return r.s1.at[at, pl.ds(pl.multiple_of(16 + 48 * core, 16), 48)]

    for k in range(1, 8):
        copy_to("s1", first_part(gy), first_part(gy), gy_peer(k)).start()
    sends_end("s1", r.s1.at[pl.ds(0, 7), pl.ds(0, 16)])
    for k in range(1, 8):
        part = second_part(gy, lax.rem(gy + k, 2))
        copy_to("s2", part, part, gy_peer(k)).start()
    sends_end("s2", r.s1.at[pl.ds(0, 7), pl.ds(0, 48)])
    for k in (1, 2, 3):
        copy_to("tk", r.tok.at[ring(z, k)], r.img.at[z, c], z_peer(k), r.tk_r.at[k - 1]).start()
    sends_end("tk", r.cotb.at[pl.ds(0, 3)])
    copy_to("tf", r.img.at[z, c], r.img.at[z, c], sibling).start()

    freq = r.v_freq[...]
    even = lax.rem(iota((1, 256), 1), 2) == 0
    fine = iota((32, 256), 0).astype(F32) * freq
    coarse = iota((32, 256), 0).astype(F32) * 32.0 * freq
    sin_f, cos_f = jnp.sin(fine), jnp.cos(fine)
    sin_c, cos_c = jnp.sin(coarse), jnp.cos(coarse)
    first_c = jnp.where(even, sin_c, cos_c)
    second_c = jnp.where(even, cos_c, -sin_c)

    await_recv("s1", r.s1.at[pl.ds(0, 7), pl.ds(0, 16)])
    bias_low, bias_high = jnp.zeros((1, 128), F32), jnp.zeros((1, 128), F32)
    share0, share1 = (1 - c).astype(F32), c.astype(F32)
    for i in range(8):
        piece = r.s1[i, 0:16, :].astype(F32)
        for row in range(2):
            r.asmf[pl.ds(2 * i + row, 6, stride=16), :] = piece[row * 6 : row * 6 + 6]
        bias_low = bias_low + piece[12:13] * share0 + piece[13:14] * share1
        bias_high = bias_high + piece[14:15] * share0 + piece[15:16] * share1
    for k in range(3):
        rows = r.asmf[pl.ds(pl.multiple_of(32 * k + 16 * c, 16), 16), :]
        r.wio[here, 16 * k : 16 * k + 16, :] = rows.astype(BF16)
    r.wio[here, 48:64, :] = jnp.concatenate(
        [bias_low, bias_high, jnp.zeros((14, 128), F32)], axis=0).astype(BF16)

    def wi_view(at):
        return r.wio.at[at, pl.ds(0, 64)]

    for k in (1, 2, 3):
        copy_to("ia", wi_view(here), wi_view(here), a_peer(k)).start()
    for k in (1, 2, 3):
        copy_to("ib", wi_view(here), wi_view(here), b_peer(k)).start()

    await_recv("s2", r.s1.at[pl.ds(0, 7), pl.ds(0, 48)])

    def wo_view(at):
        return r.wio.at[at, pl.ds(64, 48)]

    def ff_view(at):
        return r.ff.at[c, at]

    @pl.when(c == 0)
    def _():
        for i in range(8):
            piece = r.s1[i, 32:64, :].astype(F32)
            for row in range(2):
                r.asmf[pl.ds(128 + 2 * i + row, 16, stride=16), :] = (
                    piece[16 * row : 16 * row + 16])
        for j in range(8):
            for half in range(2):
                at = 128 + 16 * (2 * j + half)
                r.ff[0, here, 16 * j : 16 * j + 16, 128 * half : 128 * half + 128] = (
                    r.asmf[at : at + 16, :].astype(BF16))

    @pl.when(c == 1)
    def _():
        for i in range(8):
            for half in range(2):
                r.ff[1, here, 16 * i : 16 * i + 16, 128 * half : 128 * half + 128] = (
                    r.s1[i, 64 + 16 * half : 80 + 16 * half, :])

    for k in (1, 2, 3):
        copy_to("fa", ff_view(here), ff_view(here), a_peer(k)).start()
    for k in (1, 2, 3):
        copy_to("fb", ff_view(here), ff_view(here), b_peer(k)).start()

    r.asmf[96:112, :] = jnp.zeros((16, 128), F32)
    shared_at = pl.multiple_of(16 + 80 * c, 16)
    for i in range(8):
        piece = r.s1[i, pl.ds(shared_at, 16), :].astype(F32)
        for row in range(2):
            r.asmf[pl.ds(64 + 2 * i + row, 2, stride=16), :] = piece[2 * row : 2 * row + 2]
        r.asmf[96 + i : 97 + i, :] = piece[4:5]
    r.wio[here, 64:112, :] = r.asmf[64:112, :].astype(BF16)
    for k in (1, 2, 3):
        copy_to("wa", wo_view(here), wo_view(here), a_peer(k)).start()

    for k in (1, 2, 3):
        at = ring(z, -k)
        await_recv("tk", r.img.at[at, c], k - 1)
        copy_to("tf", r.img.at[at, c], r.img.at[at, c], sibling).start()
    sends_end("tf", r.img.at[:, 0])
    for k in (1, 2, 3):
        copy_to("ct", r.cot.at[ring(z, k)], r.cotb.at[z], z_peer(k)).start()
    sends_end("ct", r.cotb.at[pl.ds(0, 3)])
    await_recv("ia", r.wio.at[pl.ds(0, 3), pl.ds(0, 64)])
    for i in (1, 2, 3):
        at = group(ring(a, -i), b)
        for k in (1, 2, 3):
            copy_to("ib", wi_view(at), wi_view(at), b_peer(k)).start()
    sends_end("ia", r.wio.at[pl.ds(0, 3), pl.ds(0, 64)])
    sends_end("ib", r.wio.at[pl.ds(0, 12), pl.ds(0, 64)])
    await_recv("tf", r.img.at[:, 1 - c])

    for i in range(8):
        rows = r.img[i // 2, i % 2].astype(F32)
        for k in range(4):
            at = 4 * i + k
            pos = first_c[at : at + 1] * cos_f + second_c[at : at + 1] * sin_f
            r.sh[32 * at : 32 * at + 32, :] = (rows[32 * k : 32 * k + 32] + pos).astype(BF16)
    image = r.img[...].reshape(1024, 256)

    r.sht[...] = r.sh[...].T
    r.imgt[...] = image.T

    await_recv("fa", r.ff.at[c, pl.ds(0, 3)])
    for i in (1, 2, 3):
        at = group(ring(a, -i), b)
        for k in (1, 2, 3):
            copy_to("fc", ff_view(at), ff_view(at), b_peer(k), r.fc_r.at[k - 1]).start()
    for i in range(4):
        at = group(ring(a, -i), b)
        copy_to("fw", ff_view(at), ff_view(at), sibling).start()
    for k in (1, 2, 3):
        copy_to("wb", wo_view(here), wo_view(here), b_peer(k)).start()
    await_recv("wa", r.wio.at[pl.ds(0, 3), pl.ds(64, 48)])
    for i in (1, 2, 3):
        at = group(ring(a, -i), b)
        for k in (1, 2, 3):
            copy_to("wb", wo_view(at), wo_view(at), b_peer(k)).start()
    sends_end("fa", r.ff.at[c, pl.ds(0, 3)])
    sends_end("fb", r.ff.at[c, pl.ds(0, 3)])
    sends_end("fc", r.ff.at[c, pl.ds(0, 9)])
    sends_end("fw", r.ff.at[c])
    sends_end("wa", r.wio.at[pl.ds(0, 3), pl.ds(64, 48)])
    sends_end("wb", r.wio.at[pl.ds(0, 12), pl.ds(64, 48)])

    await_recv("ib", r.wio.at[pl.ds(0, 12), pl.ds(0, 64)])
    biases = jnp.zeros((16, 128), F32)
    for i in range(16):
        biases = biases + r.wio[i, 48:64, :].astype(F32)

    def w_part(k):
        return r.wio[:, 16 * k : 16 * k + 16, :].reshape(256, 128)

    queries = (dot(r.sh[...], w_part(0)) + biases[0:1]).astype(BF16)
    keys = dot(r.sh[...], w_part(1)).astype(BF16)
    values = (dot(image, w_part(2)) + biases[1:2]).astype(BF16)
    r.qq[...] = queries
    r.vv[...] = values
    r.kt[...] = keys.T
    r.vt[...] = values.T
    r.qt[0:128, :] = queries.T
    ones_row = iota((128, 1024), 0) == 0
    r.qt[128:256, :] = jnp.where(ones_row, 1.0, 0.0).astype(BF16)

    length = r.lens[z]

    zero = jnp.zeros((), BF16)
    head_of_lane = lax.div(iota((1024, 128), 1), HD)
    hidden_key = (iota((1024, 128), 0) >= length) & (iota((1024, 128), 1) == 0)
    bias = jnp.where(hidden_key, -1e30, 0.0).astype(BF16)
    for head in range(4):
        r.kx[head, :, 0:128] = jnp.where(head_of_lane == head, keys, zero)
        r.kx[head, :, 128:256] = bias

    for head in range(4):
        peak = None
        for k in range(0, 1024, 512):
            part = jnp.max(dot(r.kx[head, k : k + 512, :], r.qt[...]), axis=0, keepdims=True)
            peak = part if peak is None else jnp.maximum(peak, part)
        scores = dot(r.kx[head], r.qt[...])
        weights = jnp.exp2(scores * EXP2_SCALE - peak * EXP2_SCALE).astype(BF16)
        r.ee[head] = weights
        rows = slice(head * HD, head * HD + HD)
        left = jnp.concatenate([r.vt[rows, :], jnp.ones((16, 1024), BF16)], axis=0)
        mixed = dot(left, weights)
        inverse = 1.0 / mixed[HD : HD + 1]
        r.ot[rows, :] = mixed[0:HD] * inverse
        r.ri[head : head + 1, :] = inverse
        if head == 2:
            await_recv("fb", r.ff.at[c, pl.ds(0, 3)])
            for k in (1, 2, 3):
                at = group(a, ring(b, -k))
                copy_to("fw", ff_view(at), ff_view(at), sibling).start()

    r.mx[...] = r.ot[...].T.astype(BF16).reshape(4, 2, 128, 128)
    copy_to("mx", r.mx.at[:, 1 - c], r.mr, sibling).start()
    sends_end("mx", r.mr)

    for k in (1, 3, 2):
        await_recv("fc", r.ff.at[c, pl.ds(0, 3)], k - 1)
        for i in (1, 2, 3):
            at = group(ring(a, -i), ring(b, -k))
            copy_to("fw", ff_view(at), ff_view(at), sibling).start()

    await_recv("wb", r.wio.at[pl.ds(0, 12), pl.ds(64, 48)])
    rows = r.wio[:, 96:112, :].reshape(256, 128)
    spot_row, spot_lane = iota((256, 256), 0), iota((256, 256), 1)
    pick = spot_row == 16 * lax.div(spot_lane, 16) + lax.div(lax.rem(spot_lane, 16), 2)
    spread = dot_tn(rows, jnp.where(pick, 1.0, 0.0).astype(BF16))
    even_lane = lax.rem(iota((1, 256), 1), 2) == 0
    for i in range(8):
        r.vecs[i : i + 1, :] = jnp.where(
            even_lane, spread[2 * i : 2 * i + 1], spread[2 * i + 1 : 2 * i + 2])
    tile = iota((128, 256), 0) == 16 + lax.rem(iota((128, 256), 1), 16)
    wide = dot(rows, jnp.where(tile, 1.0, 0.0).astype(BF16))
    keep = lax.rem(spot_row, 32) == (
        16 * lax.div(spot_lane, 128) + lax.rem(lax.div(spot_lane, 16), 8))
    wide = jnp.where(keep, wide, 0.0).reshape(8, 32, 256)
    r.vecs[8:16, :] = jnp.sum(wide, axis=1)

    for head in range(4):
        r.vx[head, :, 0:128] = jnp.where(head_of_lane == head, r.vv[...], zero)
        r.vx[head, :, 128:256] = jnp.where(
            lax.div(iota((1024, 128), 1), 2) == head, 1.0, 0.0).astype(BF16)
        r.qm[head] = jnp.where(head_of_lane == head, r.qq[...], zero)

    def w_out_rows(half):
        low = r.wio[pl.ds(8 * half, 8), 64:80, :].reshape(128, 128)
        high = r.wio[pl.ds(8 * half, 8), 80:96, :].reshape(128, 128)
        return jnp.concatenate([low, high], axis=1)

    def vec(name):
        return r.vecs[ROW[name] : ROW[name] + 1, :]

    mixed_own = r.mx[:, c].reshape(512, 128)
    branch = dot(mixed_own, w_out_rows(c))
    await_recv("mx", r.mr)
    mixed_other = r.mr[...].reshape(512, 128)
    branch = branch + dot(mixed_other, w_out_rows(1 - c))
    first_sum = r.img[:, c].reshape(512, 256).astype(F32) + branch + vec("b_out")
    hidden, unit, inverse = norm_forward(first_sum, vec("gain1"), vec("shift1"))
    r.unit1[...] = unit
    r.inv1[...] = inverse
    r.hid[...] = hidden
    hidden_low = hidden.astype(BF16)
    r.hlow[...] = hidden_low
    r.hlt[...] = hidden_low.T

    await_recv("fw", r.ff.at[1 - c])

    def up_block(j):
        parts = [r.ff[0, :, 16 * k : 16 * k + 16, :].reshape(256, 256) for k in (2 * j, 2 * j + 1)]
        return jnp.concatenate(parts, axis=1)

    def down_block(j):
        return r.ff[1, 4 * j : 4 * j + 4, :, :].reshape(512, 256)

    r.acc[...] = r.hid[...] + vec("b_down")
    for j in range(4):
        up_shift = jnp.concatenate(
            [r.vecs[8 + 2 * j : 9 + 2 * j, :], r.vecs[9 + 2 * j : 10 + 2 * j, :]], axis=1)
        up = dot(r.hlow[...], up_block(j)) + up_shift
        square = up * up
        gate = 0.5 + 0.5 * jnp.tanh(up * (GELU_SCALE + GELU_SCALE * 0.044715 * square))
        active = up * gate
        slope = 2 * GELU_SCALE + 6 * 0.044715 * GELU_SCALE * square
        r.dgl[j] = (gate + active * (1.0 - gate) * slope).astype(BF16)
        active = active.astype(BF16)
        r.act[j] = active
        r.acc[...] += dot(active, down_block(j))

    out, unit, inverse = norm_forward(r.acc[...], vec("gain2"), vec("shift2"))
    r.lob[...] = out.astype(BF16).reshape(4, 128, 256)
    for k in (1, 2, 3):
        copy_to("lo", r.lob.at[ring(z, k)], r.lor.at[z], z_peer(k)).start()
    sends_end("lo", r.lob.at[pl.ds(0, 3)])
    own_copies = [pltpu.make_async_copy(r.lob.at[z], r.lor.at[z], r.own_s.at[0])]
    own_copies[0].start()

    await_recv("ct", r.cotb.at[pl.ds(0, 3)])
    d_out = r.cotb[...].reshape(512, 256).astype(F32)
    r.gv[ROW["gain2"] : ROW["gain2"] + 1, :] = column_sum(d_out * unit)
    r.gv[ROW["shift2"] : ROW["shift2"] + 1, :] = column_sum(d_out)
    d_second = norm_backward(d_out, unit, inverse, vec("gain2"))
    d_ffn = d_second.astype(BF16)
    r.dffn[...] = d_ffn
    r.gv[ROW["b_down"] : ROW["b_down"] + 1, :] = column_sum(d_ffn.astype(F32))
    r.acc[...] = d_second

    for j in range(4):
        d_active = dot_nt(r.dffn[...], down_block(j))
        d_up = (d_active * r.dgl[j].astype(F32)).astype(BF16)
        g_down = dot_tn(r.act[j], r.dffn[...])
        r.gp[1, 4 * j : 4 * j + 4] = g_down.astype(BF16).reshape(4, 128, 256)
        g_up = dot(r.hlt[...], d_up).astype(BF16)
        sums = column_sum(d_up.astype(F32))
        for k in range(2):
            at, lanes = 2 * j + k, slice(256 * k, 256 * k + 256)
            r.gp[0, :, 16 * at : 16 * at + 16, :] = g_up[:, lanes].reshape(16, 16, 256)
            r.gv[8 + at : 9 + at, :] = sums[:, lanes]
        r.acc[...] += dot_nt(d_up, up_block(j))

        @pl.when(c == 0)
        def _():
            part = pl.ds(4 * j, 4)
            copy_to("gs", r.gp.at[1, part], r.gs.at[part], sibling).start()

        @pl.when(c == 1)
        def _():
            part = pl.ds(32 * j, 32)
            copy_to("gs", r.gp.at[0, :, part], r.gs.at[:, part], sibling).start()

    sends_end("gs", r.gs)

    d_hidden = r.acc[...]
    unit = r.unit1[...]
    r.gv[ROW["gain1"] : ROW["gain1"] + 1, :] = column_sum(d_hidden * unit)
    r.gv[ROW["shift1"] : ROW["shift1"] + 1, :] = column_sum(d_hidden)
    d_first = norm_backward(d_hidden, unit, r.inv1[...], vec("gain1"))
    r.dfirst[...] = d_first
    d_branch = d_first.astype(BF16)
    r.gv[ROW["b_out"] : ROW["b_out"] + 1, :] = column_sum(d_branch.astype(F32))
    r.dms[...] = dot_nt(d_branch, w_out_rows(1 - c)).astype(BF16).reshape(4, 128, 128)
    copy_to("dm", r.dms, r.dmx.at[:, c], sibling).start()
    sends_end("dm", r.dms)
    r.dmx[:, c] = dot_nt(d_branch, w_out_rows(c)).astype(BF16).reshape(4, 128, 128)

    def spot(g):
        return g * (1 - c) + (4 * lax.rem(g, 4) + lax.div(g, 4)) * c

    for half, mixed in ((c, r.mx[:, c].reshape(512, 128)), (1 - c, r.mr[...].reshape(512, 128))):
        g_out = dot_tn(mixed, d_branch).astype(BF16)
        for i in range(8):
            at = spot(8 * half + i)
            r.gwo[at, 0:16, :] = g_out[16 * i : 16 * i + 16, 0:128]
            r.gwo[at, 16:32, :] = g_out[16 * i : 16 * i + 16, 128:256]
    r.gv[0:2, :] = jnp.zeros((2, 256), F32)
    r.v0[...] = r.gv[...]

    await_recv("gs", r.gs)

    def add_cores(i, carry):
        at = group(lax.div(i, 4), lax.rem(i, 4))
        r.rs[i] = (r.gp[c, at].astype(F32) + r.gs[at].astype(F32)).astype(BF16)
        return carry

    lax.fori_loop(0, 16, add_cores, 0)

    for k in (1, 2, 3):
        part, to = pl.ds(4 * ring(a, k), 4), a_peer(k)
        copy_to("r1", r.rs.at[part], r.r1.at[k - 1], to).start()
        copy_to("g1", r.gwo.at[part], r.wo1.at[k - 1], to).start()
        copy_to("v1", r.v0, r.vr1.at[k - 1], to).start()
    sends_end("r1", r.r1)
    sends_end("g1", r.wo1)
    sends_end("v1", r.vr1)

    await_recv("dm", r.dmx.at[:, 1 - c])
    d_mixed_t = r.dmx[...].reshape(1024, 128).astype(F32).T
    extra = []
    for head in range(4):
        rows = slice(32 * head, 32 * head + 32)
        scaled = d_mixed_t[rows] * r.ri[head : head + 1, :]
        r.dot_[rows, :] = scaled.astype(BF16)
        inner = -column_sum(scaled * r.ot[rows, :])
        high = inner.astype(BF16).astype(F32)
        extra += [high, inner - high]
    extra.append(jnp.zeros((8, 1024), F32))
    r.dot_[128:144, :] = jnp.concatenate(extra, axis=0).astype(BF16)
    r.dot_[144:256, :] = jnp.zeros((112, 1024), BF16)
    r.doo[...] = r.dot_[0:128, :].T

    for head in range(4):
        d_probs = dot(r.vx[head], r.dot_[...])
        d_scores = r.ee[head] * d_probs.astype(BF16)
        r.ds[head % 2] = d_scores
        rows = slice(head * HD, head * HD + HD)
        r.dqt[rows, :] = dot(r.kt[rows, :], d_scores)
        do_masked = jnp.where(head_of_lane == head, r.doo[...], zero)
        for k in range(0, 1024, 256):
            d_key = dot(r.ds[head % 2, k : k + 256, :], r.qm[head])
            d_value = dot(r.ee[head, k : k + 256, :], do_masked)
            if head == 0:
                r.dk[k : k + 256, :] = d_key
                r.dv[k : k + 256, :] = d_value
            else:
                r.dk[k : k + 256, :] += d_key
                r.dv[k : k + 256, :] += d_value

    await_recv("r1", r.r1)
    await_recv("g1", r.wo1)
    await_recv("v1", r.vr1)

    def add_first(i, carry):
        total = r.rs[4 * a + i].astype(F32)
        small = r.gwo[4 * a + i].astype(F32)
        for k in range(3):
            total = total + r.r1[k, i].astype(F32)
            small = small + r.wo1[k, i].astype(F32)
        r.s2[i] = total.astype(BF16)
        r.wos[i] = small.astype(BF16)
        return carry

    lax.fori_loop(0, 4, add_first, 0)
    r.v1[...] = r.v0[...] + r.vr1[0] + r.vr1[1] + r.vr1[2]
    for k in (1, 2, 3):
        part, to = ring(b, k), b_peer(k)
        copy_to("r2", r.s2.at[part], r.r2.at[k - 1], to).start()
        copy_to("g2", r.wos.at[part], r.wo2.at[k - 1], to).start()
        copy_to("v2", r.v1, r.vr2.at[k - 1], to).start()
    sends_end("r2", r.r2)
    sends_end("g2", r.wo2)
    sends_end("v2", r.vr2)

    d_queries = (r.dqt[...] * SCORE_SCALE).T.astype(BF16)
    d_keys = (r.dk[...] * SCORE_SCALE).astype(BF16)
    d_values = r.dv[...].astype(BF16)
    for k, (left, right) in enumerate(((r.sht, d_queries), (r.sht, d_keys), (r.imgt, d_values))):
        g_part = dot(left[...], right).astype(BF16)
        for i in range(16):
            r.gio[i, 16 * k : 16 * k + 16, :] = g_part[16 * i : 16 * i + 16, :]
    ones = jnp.ones((1024, 128), BF16)
    sums = jnp.where(
        iota((128, 128), 1) < 64, dot_tn(d_queries, ones), dot_tn(d_values, ones)).astype(BF16)
    for i in range(8):
        r.gio[8 * c + i, 48:64, :] = sums[16 * i : 16 * i + 16, :]
        r.gio[8 * (1 - c) + i, 48:64, :] = jnp.zeros((16, 128), BF16)
    for k in range(1, 16):
        copy_to("q1", r.gio.at[ring(gx, k, 16)], r.q1.at[gx], gx_peer(k)).start()
    sends_end("q1", r.q1.at[pl.ds(0, 15)])

    d_tokens = (
        dot_nt(d_queries, w_part(0)) + dot_nt(d_keys, w_part(1)) + dot_nt(d_values, w_part(2)))
    r.gt[...] = d_tokens.astype(BF16).reshape(4, 2, 128, 256)
    copy_to("gt", r.gt.at[:, 1 - c], r.gtr, sibling).start()
    sends_end("gt", r.gtr)

    await_recv("gt", r.gtr)
    full = (
        r.dfirst[...]
        + r.gt[:, c].reshape(512, 256).astype(F32)
        + r.gtr[...].reshape(512, 256).astype(F32))
    r.gob[...] = full.astype(BF16).reshape(4, 128, 256)
    for k in (1, 2, 3):
        copy_to("go", r.gob.at[ring(z, k)], r.gor.at[z], z_peer(k)).start()
    sends_end("go", r.gob.at[pl.ds(0, 3)])

    await_recv("r2", r.r2)
    await_recv("g2", r.wo2)
    await_recv("v2", r.vr2)
    total = r.s2[b].astype(F32)
    small = r.wos[b].astype(F32)
    for k in range(3):
        total = total + r.r2[k].astype(F32)
        small = small + r.wo2[k].astype(F32)
    r.fin[0] = total[:, 0:128]
    r.fin[1] = total[:, 128:256]
    r.fwo[...] = small
    r.p3f[...] = jnp.zeros((8, 48, 128), F32)

    @pl.when(c == 0)
    def _():
        for i in range(8):
            for half in range(2):
                for row in range(2):
                    at = 16 * half + 8 * row
                    r.p3f[i, at : at + 8, :] = r.fin.at[half][
                        pl.ds(2 * i + row, 8, stride=16), :]

    @pl.when(c == 1)
    def _():
        for i in range(8):
            for half in range(2):
                r.p3f[i, 16 * half : 16 * half + 16, :] = r.fin[half, 16 * i : 16 * i + 16, :]

    for i in range(8):
        for row in range(2):
            at = 32 + 8 * row
            r.p3f[i, at : at + 2, :] = r.fwo[pl.ds(2 * i + row, 2, stride=16), :]
    sums = r.v1[...] + r.vr2[0] + r.vr2[1] + r.vr2[2]
    own_lanes = pltpu.roll(sums[0:8], lax.rem(256 - 16 * gx, 256), axis=1)[:, 0:128]
    up_sums = column_sum(jnp.where(iota((8, 256), 0) == lax.div(gx, 2), sums[8:16], 0.0))
    right = lax.rem(gx, 2).astype(F32)
    up_sums = up_sums[:, 0:128] * (1.0 - right) + up_sums[:, 128:256] * right
    for i in range(8):
        r.p3f[i, 34:40, :] = own_lanes[2:8]
        r.p3f[i, 42:43, :] = up_sums
    r.p3[...] = r.p3f[...].astype(BF16)
    for k in range(1, 8):
        copy_to("p3", r.p3.at[ring(gy, k, 8)], r.r3.at[gy], gy_peer(k)).start()
    sends_end("p3", r.p3.at[pl.ds(0, 7)])

    await_recv("q1", r.q1.at[pl.ds(0, 15)])
    total = r.gio[gx].astype(F32)
    for k in range(1, 16):
        total = total + r.q1[ring(gx, -k, 16)].astype(F32)
    r.fio[...] = total
    r.p4f[...] = jnp.zeros((8, 16, 128), F32)
    for i in range(8):
        for row in range(2):
            at = 8 * row
            r.p4f[i, at : at + 4, :] = r.fio[pl.ds(2 * i + row, 4, stride=16), :]
    r.p4[...] = r.p4f[...].astype(BF16)
    for k in range(1, 8):
        copy_to("p4", r.p4.at[ring(gy, k, 8)], r.r4.at[gy], gy_peer(k)).start()
    sends_end("p4", r.p4.at[pl.ds(0, 7)])

    own_copies += [
        pltpu.make_async_copy(r.gob.at[z], r.gor.at[z], r.own_s.at[1]),
        pltpu.make_async_copy(r.p3.at[gy], r.r3.at[gy], r.own_s.at[2]),
        pltpu.make_async_copy(r.p4.at[gy], r.r4.at[gy], r.own_s.at[3]),
    ]
    for copy in own_copies[1:]:
        copy.start()
    await_recv("lo", r.lor.at[pl.ds(0, 3)])
    await_recv("go", r.gor.at[pl.ds(0, 3)])
    await_recv("p3", r.r3.at[pl.ds(0, 7)])
    await_recv("p4", r.r4.at[pl.ds(0, 7)])
    for copy in own_copies:
        copy.wait()
    for make in closing:
        make().wait_send()


def unpack(*refs):
    r = Refs()
    for name, ref in zip(tuple(PACKED) + OUTPUTS, refs):
        setattr(r, name, ref)
    gy = lax.axis_index("gy")
    r.layer_out[...] = r.lor[...]
    r.grad_tokens[...] = r.gor[...].astype(F32)
    core0 = jnp.zeros((48, 128), F32)
    core1 = jnp.zeros((48, 128), F32)
    into0 = jnp.zeros((16, 128), F32)
    into1 = jnp.zeros((16, 128), F32)
    for i in range(4):
        core0 = core0 + r.r3[2 * i].astype(F32)
        core1 = core1 + r.r3[2 * i + 1].astype(F32)
        into0 = into0 + r.r4[2 * i].astype(F32)
        into1 = into1 + r.r4[2 * i + 1].astype(F32)
    r.g_w_down[:, 0:128] = core1[0:16]
    r.g_w_down[:, 128:256] = core1[16:32]
    w_out = core0 + core1
    for row in range(2):
        out_row = slice(row, row + 1)
        for j in range(8):
            for half in range(2):
                at = 16 * half + 8 * row + j
                lanes = 256 * j + 128 * half
                r.g_w_up[out_row, lanes : lanes + 128] = core0[at : at + 1]
        for k in range(3):
            at = 8 * row + k
            r.g_w_in[out_row, 256 * k : 256 * k + 128] = into0[at : at + 1]
            r.g_w_in[out_row, 256 * k + 128 : 256 * k + 256] = into1[at : at + 1]
        at = 32 + 8 * row
        r.g_w_out[out_row, 0:128] = w_out[at : at + 1]
        r.g_w_out[out_row, 128:256] = w_out[at + 1 : at + 2]
    biases = into0 + into1
    for name, lane in (("b_q", 0), ("b_v", 64)):
        pair = jnp.concatenate(
            [biases[3:4, lane : lane + 1], biases[11:12, lane : lane + 1]], axis=1)
        getattr(r, "g_" + name)[...] = pair.reshape(2)
    moved = pltpu.roll(w_out[32:48], lax.rem(128 - 2 * gy, 128), axis=1)
    for name in SMALL[2:]:
        row = ROW[name]
        getattr(r, "g_" + name)[...] = moved[row : row + 1, 0:2].reshape(2)
    moved = pltpu.roll(w_out[40:48], lax.rem(128 - 16 * gy, 128), axis=1)
    r.g_b_up[...] = moved[2:3, 0:16].reshape(16)


def body(
    tokens, lengths, w_in, b_q, b_v, w_out, b_out, gain_first, shift_first, w_up, b_up,
    w_down, b_down, gain_second, shift_second, cotangent,
):
    column = np.arange(D)
    freq = np.power(10000.0, -(2.0 * (column // 2)) / D).astype(np.float32)[None, :]
    args = (
        tokens, cotangent, lengths, jnp.asarray(freq), w_in, w_out, w_up, w_down,
        b_q, b_v, b_out, gain_first, shift_first, b_down, gain_second, shift_second, b_up,
    )
    vmem = pl.BlockSpec(memory_space=pltpu.VMEM)
    anywhere = pl.BlockSpec(memory_space=pl.ANY)
    in_specs = [anywhere] * len(args)
    in_specs[2] = pl.BlockSpec(memory_space=pltpu.SMEM)
    shape = jax.ShapeDtypeStruct
    vector = shape((2,), F32)
    scratch = [pltpu.VMEM(args[INPUTS.index(name)].shape, args[INPUTS.index(name)].dtype)
               for name in LOADED]
    scratch += [pltpu.VMEM(dims, kind) for dims, kind in SCRATCH.values()]
    scratch += [pltpu.SemaphoreType.DMA((count,)) for count in SEMS.values()]
    packed = pl.pallas_call(
        kernel,
        out_shape=tuple(shape(dims, kind) for dims, kind in PACKED.values()),
        in_specs=in_specs,
        out_specs=tuple([anywhere] * len(PACKED)),
        scratch_shapes=scratch,
        compiler_params=pltpu.CompilerParams(
            collective_id=0, has_side_effects=True, vmem_limit_bytes=VMEM_LIMIT),
        name="encoder_layer",
    )(*args)
    out_shape = (
        shape((4, 128, 256), BF16), shape((4, 128, 256), F32), shape((2, 768), F32),
        vector, vector, shape((2, 256), F32), vector, vector, vector,
        shape((2, 2048), F32), shape((16,), F32), shape((16, 256), F32),
        vector, vector, vector,
    )
    return pl.pallas_call(
        unpack,
        out_shape=out_shape,
        in_specs=[vmem] * len(packed),
        out_specs=tuple([vmem] * len(out_shape)),
        name="unpack_results",
    )(*packed)


def solution(mesh):
    both = ("gx", "gy")
    rows, vector, whole = P(both, None), P(both), P("gx", "gy", None)
    return jax.shard_map(
        body,
        mesh=mesh,
        in_specs=(
            whole, P("gx"), rows, vector, vector, rows, vector, vector, vector, rows, vector,
            rows, vector, vector, vector, whole,
        ),
        out_specs=(
            whole, whole, rows, vector, vector, rows, vector, vector, vector, rows, vector,
            rows, vector, vector, vector,
        ),
        check_vma=False,
    )
```

```python
import math

import jax
import jax.numpy as jnp
import numpy as np
from jax import lax
from jax.experimental import pallas as pl
from jax.experimental.pallas import tpu as pltpu
from jax.sharding import PartitionSpec as P

MESH = pl.DeviceIdType.MESH
F32 = jnp.float32
BF16 = jnp.bfloat16

D = 256
HD = 32
VMEM_LIMIT = 56 * 2**20
EPSILON = 1e-05
GELU_SCALE = math.sqrt(2.0 / math.pi)
SCORE_SCALE = 1.0 / math.sqrt(HD)
EXP2_SCALE = SCORE_SCALE * math.log2(math.e)


def dot(left, right):
    return jnp.dot(left, right, preferred_element_type=F32)


def dot_nt(left, right):
    return lax.dot_general(left, right, (((1,), (1,)), ((), ())), preferred_element_type=F32)


def dot_tn(left, right):
    return lax.dot_general(left, right, (((0,), (0,)), ((), ())), preferred_element_type=F32)


def iota(shape, dim):
    return lax.broadcasted_iota(jnp.int32, shape, dim)


def column_sum(values):
    return jnp.sum(values, axis=0, keepdims=True)


def norm_forward(values, gain, shift):
    centre = jnp.mean(values, axis=-1, keepdims=True)
    moved = values - centre
    spread = jnp.mean(moved * moved, axis=-1, keepdims=True)
    inverse = lax.rsqrt(spread + EPSILON)
    unit = moved * inverse
    return unit * gain + shift, unit, inverse


def norm_backward(d_out, unit, inverse, gain):
    d_unit = d_out * gain
    mean_d = jnp.mean(d_unit, axis=-1, keepdims=True)
    mean_du = jnp.mean(d_unit * unit, axis=-1, keepdims=True)
    return inverse * (d_unit - mean_d - unit * mean_du)


SCRATCH = dict(
    pf=((112, 128), F32),
    s1=((8, 112, 128), BF16),
    asmf=((384, 128), F32),
    img=((4, 2, 128, 256), BF16),
    cotb=((4, 128, 256), BF16),
    wio=((16, 112, 128), BF16),
    ff=((2, 16, 128, 256), BF16),
    vecs=((16, 256), F32),
    sh=((1024, 256), BF16),
    sht=((256, 1024), BF16),
    imgt=((256, 1024), BF16),
    kx=((4, 1024, 256), BF16),
    vx=((4, 1024, 256), BF16),
    qm=((4, 1024, 128), BF16),
    vv=((1024, 128), BF16),
    qq=((1024, 128), BF16),
    kt=((128, 1024), BF16),
    vt=((128, 1024), BF16),
    qt=((256, 1024), BF16),
    ee=((4, 1024, 1024), BF16),
    ot=((128, 1024), F32),
    ri=((8, 1024), F32),
    mx=((4, 2, 128, 128), BF16),
    mr=((4, 128, 128), BF16),
    hid=((512, 256), F32),
    hlow=((512, 256), BF16),
    hlt=((256, 512), BF16),
    unit1=((512, 256), F32),
    inv1=((512, 1), F32),
    act=((4, 512, 512), BF16),
    dgl=((4, 512, 512), BF16),
    acc=((512, 256), F32),
    lob=((4, 128, 256), BF16),
    dffn=((512, 256), BF16),
    gp=((2, 16, 128, 256), BF16),
    gs=((16, 128, 256), BF16),
    rs=((16, 128, 256), BF16),
    r1=((3, 4, 128, 256), BF16),
    s2=((4, 128, 256), BF16),
    r2=((3, 128, 256), BF16),
    fin=((2, 128, 128), F32),
    gv=((16, 256), F32),
    dfirst=((512, 256), F32),
    dms=((4, 128, 128), BF16),
    dmx=((4, 2, 128, 128), BF16),
    dot_=((256, 1024), BF16),
    doo=((1024, 128), BF16),
    ds=((2, 1024, 1024), BF16),
    dqt=((128, 1024), F32),
    dk=((1024, 128), F32),
    dv=((1024, 128), F32),
    gwo=((16, 32, 128), BF16),
    wo1=((3, 4, 32, 128), BF16),
    wos=((4, 32, 128), BF16),
    wo2=((3, 32, 128), BF16),
    fwo=((32, 128), F32),
    gio=((16, 64, 128), BF16),
    q1=((16, 64, 128), BF16),
    fio=((64, 128), F32),
    v0=((16, 256), F32),
    vr1=((3, 16, 256), F32),
    v1=((16, 256), F32),
    vr2=((3, 16, 256), F32),
    gt=((4, 2, 128, 256), BF16),
    gtr=((4, 128, 256), BF16),
    gob=((4, 128, 256), BF16),
    p3f=((8, 48, 128), F32),
    p3=((8, 48, 128), BF16),
    p4f=((8, 16, 128), F32),
    p4=((8, 16, 128), BF16),
)

GROUPS = (
    "s1", "s2", "tk", "tf", "ct", "ia", "ib", "wa", "wb", "fa", "fb", "fc", "fw", "mx", "dm", "lo",
    "gs", "r1", "r2", "g1", "g2", "v1", "v2", "q1", "gt", "go", "p3", "p4",
)
SEMS = dict(in_s=16, own_s=4, tk_r=3, fc_r=3, gs_r=2)
for group_name in GROUPS:
    SEMS.setdefault(group_name + "_s", 1)
    SEMS.setdefault(group_name + "_r", 1)

INPUTS = (
    "tok", "cot", "lens", "freq", "w_in", "w_out", "w_up", "w_down",
    "b_q", "b_v", "b_out", "gain1", "shift1", "b_down", "gain2", "shift2", "b_up",
)
OUTPUTS = (
    "layer_out", "grad_tokens", "g_w_in", "g_b_q", "g_b_v", "g_w_out", "g_b_out",
    "g_gain1", "g_shift1", "g_w_up", "g_b_up", "g_w_down", "g_b_down", "g_gain2", "g_shift2",
)
PACKED = dict(
    lor=((4, 128, 256), BF16),
    gor=((4, 128, 256), BF16),
    r3=((8, 48, 128), BF16),
    r4=((8, 16, 128), BF16),
)
LOADED = INPUTS[3:]
SMALL = ("b_q", "b_v", "b_out", "gain1", "shift1", "b_down", "gain2", "shift2")
ROW = {name: row for row, name in enumerate(SMALL)}


class Refs:
    pass


def kernel(*refs):
    r = Refs()
    held = tuple("v_" + name for name in LOADED)
    names = INPUTS + tuple(PACKED) + held + tuple(SCRATCH) + tuple(SEMS)
    for name, ref in zip(names, refs):
        setattr(r, name, ref)

    gx, gy = lax.axis_index("gx"), lax.axis_index("gy")
    x, y = lax.div(gx, 4), lax.rem(gx, 4)
    z, c = lax.div(gy, 2), lax.rem(gy, 2)
    a = x * (1 - c) + y * c
    b = y * (1 - c) + x * c

    def group(a_at, b_at):
        return a_at * (4 - 3 * c) + b_at * (1 + 3 * c)

    def ring(at, step, size=4):
        return lax.rem(at + (step % size), size)

    def a_peer(step):
        return (group(ring(a, step), b), gy)

    def b_peer(step):
        return (group(a, ring(b, step)), gy)

    def gx_peer(step):
        return (ring(gx, step, 16), gy)

    def z_peer(step):
        return (gx, 2 * ring(z, step) + c)

    def gy_peer(step):
        return (gx, ring(gy, step, 8))

    sibling = (gx, 2 * z + 1 - c)
    here = group(a, b)

    def remote(src, dst, send, recv, device):
        return pltpu.make_async_remote_copy(
            src_ref=src, dst_ref=dst, send_sem=send, recv_sem=recv,
            device_id=device, device_id_type=MESH,
        )

    closing = []

    def sem(name):
        return getattr(r, name).at[0]

    def copy_to(name, src, dst, device, recv=None):
        return remote(src, dst, sem(name + "_s"), recv or sem(name + "_r"), device)

    def sends_end(name, ref):
        closing.append(lambda: remote(ref, ref, sem(name + "_s"), sem(name + "_s"), sibling))

    def await_recv(name, ref, at=0):
        done = getattr(r, name + "_r").at[at]
        remote(ref, ref, done, done, sibling).wait_recv()

    loads = [
        pltpu.make_async_copy(getattr(r, name), getattr(r, "v_" + name), r.in_s.at[i])
        for i, name in enumerate(LOADED)
    ]
    loads.append(pltpu.make_async_copy(r.tok.at[z], r.img.at[z, c], r.in_s.at[14]))
    loads.append(pltpu.make_async_copy(r.cot.at[z], r.cotb.at[z], r.in_s.at[15]))

    barrier = pltpu.get_barrier_semaphore()
    peers = [gy_peer(k) for k in (4, 5, 3, 2, 6, 1, 7)]
    peers += [a_peer(k) for k in (2, 1, 3)] + [b_peer(k) for k in (2, 1, 3)]
    for peer in peers:
        pl.semaphore_signal(barrier, inc=1, device_id=peer, device_id_type=MESH)
    for load in loads:
        load.start()
    for load in loads:
        load.wait()

    rows = r.v_w_in[...].astype(F32)
    for row in range(2):
        for k in range(6):
            at = 6 * row + k
            r.pf[at : at + 1, :] = rows[row : row + 1, k * 128 : (k + 1) * 128]
    lane = iota((1, 256), 1)
    place = 2 * (8 * gx + gy)
    for i, name in enumerate(("b_q", "b_v")):
        pair = getattr(r, "v_" + name)[...].astype(F32).reshape(1, 2)
        row = jnp.where(lane == place, pair[:, 0:1], 0.0)
        row = jnp.where(lane == place + 1, pair[:, 1:2], row)
        r.pf[12 + 2 * i : 13 + 2 * i, :] = row[:, 0:128]
        r.pf[13 + 2 * i : 14 + 2 * i, :] = row[:, 128:256]
    r.s1[gy, 0:16, :] = r.pf[0:16, :].astype(BF16)

    rows = r.v_w_out[...].astype(F32)
    r.pf[16:32, :] = jnp.zeros((16, 128), F32)
    for row in range(2):
        for k in range(2):
            at = 16 + 2 * row + k
            r.pf[at : at + 1, :] = rows[row : row + 1, k * 128 : (k + 1) * 128]
    thin = iota((1, 128), 1)
    packed = jnp.zeros((1, 128), F32)
    for i, name in enumerate(SMALL):
        pair = getattr(r, "v_" + name)[...].astype(F32).reshape(1, 2)
        packed = jnp.where(thin == 2 * i, pair[:, 0:1], packed)
        packed = jnp.where(thin == 2 * i + 1, pair[:, 1:2], packed)
    up_bias = r.v_b_up[...].astype(F32).reshape(1, 16)
    for k in range(16):
        packed = jnp.where(thin == 16 + k, up_bias[:, k : k + 1], packed)
    r.pf[20:21, :] = packed
    rows = r.v_w_up[...].astype(F32)
    for row in range(2):
        for k in range(16):
            at = 32 + 16 * row + k
            r.pf[at : at + 1, :] = rows[row : row + 1, k * 128 : (k + 1) * 128]
    r.s1[gy, 16:64, :] = r.pf[16:64, :].astype(BF16)
    r.s1[gy, 64:80, :] = r.v_w_down[:, 0:128]
    r.s1[gy, 80:96, :] = r.v_w_down[:, 128:256]
    r.s1[gy, 96:112, :] = r.pf[16:32, :].astype(BF16)

    pl.semaphore_wait(barrier, 13)

    def first_part(at):
        return r.s1.at[at, pl.ds(0, 16)]

    def second_part(at, core):
        return r.s1.at[at, pl.ds(pl.multiple_of(16 + 48 * core, 16), 48)]

    for k in range(1, 8):
        copy_to("s1", first_part(gy), first_part(gy), gy_peer(k)).start()
    sends_end("s1", r.s1.at[pl.ds(0, 7), pl.ds(0, 16)])
    for k in range(1, 8):
        part = second_part(gy, lax.rem(gy + k, 2))
        copy_to("s2", part, part, gy_peer(k)).start()
    sends_end("s2", r.s1.at[pl.ds(0, 7), pl.ds(0, 48)])
    for k in (1, 2, 3):
        copy_to("tk", r.tok.at[ring(z, k)], r.img.at[z, c], z_peer(k), r.tk_r.at[k - 1]).start()
    sends_end("tk", r.cotb.at[pl.ds(0, 3)])
    copy_to("tf", r.img.at[z, c], r.img.at[z, c], sibling).start()

    freq = r.v_freq[...]
    even = lax.rem(iota((1, 256), 1), 2) == 0
    fine = iota((32, 256), 0).astype(F32) * freq
    coarse = iota((32, 256), 0).astype(F32) * 32.0 * freq
    sin_f, cos_f = jnp.sin(fine), jnp.cos(fine)
    sin_c, cos_c = jnp.sin(coarse), jnp.cos(coarse)
    first_c = jnp.where(even, sin_c, cos_c)
    second_c = jnp.where(even, cos_c, -sin_c)

    await_recv("s1", r.s1.at[pl.ds(0, 7), pl.ds(0, 16)])
    bias_low, bias_high = jnp.zeros((1, 128), F32), jnp.zeros((1, 128), F32)
    share0, share1 = (1 - c).astype(F32), c.astype(F32)
    for i in range(8):
        piece = r.s1[i, 0:16, :].astype(F32)
        for row in range(2):
            r.asmf[pl.ds(2 * i + row, 6, stride=16), :] = piece[row * 6 : row * 6 + 6]
        bias_low = bias_low + piece[12:13] * share0 + piece[13:14] * share1
        bias_high = bias_high + piece[14:15] * share0 + piece[15:16] * share1
    for k in range(3):
        rows = r.asmf[pl.ds(pl.multiple_of(32 * k + 16 * c, 16), 16), :]
        r.wio[here, 16 * k : 16 * k + 16, :] = rows.astype(BF16)
    r.wio[here, 48:64, :] = jnp.concatenate(
        [bias_low, bias_high, jnp.zeros((14, 128), F32)], axis=0).astype(BF16)

    def wi_view(at):
        return r.wio.at[at, pl.ds(0, 64)]

    for k in (1, 2, 3):
        copy_to("ia", wi_view(here), wi_view(here), a_peer(k)).start()
    for k in (1, 2, 3):
        copy_to("ib", wi_view(here), wi_view(here), b_peer(k)).start()

    await_recv("s2", r.s1.at[pl.ds(0, 7), pl.ds(0, 48)])

    def wo_view(at):
        return r.wio.at[at, pl.ds(64, 48)]

    def ff_view(at):
        return r.ff.at[c, at]

    @pl.when(c == 0)
    def _():
        for i in range(8):
            piece = r.s1[i, 32:64, :].astype(F32)
            for row in range(2):
                r.asmf[pl.ds(128 + 2 * i + row, 16, stride=16), :] = (
                    piece[16 * row : 16 * row + 16])
        for j in range(8):
            for half in range(2):
                at = 128 + 16 * (2 * j + half)
                r.ff[0, here, 16 * j : 16 * j + 16, 128 * half : 128 * half + 128] = (
                    r.asmf[at : at + 16, :].astype(BF16))

    @pl.when(c == 1)
    def _():
        for i in range(8):
            for half in range(2):
                r.ff[1, here, 16 * i : 16 * i + 16, 128 * half : 128 * half + 128] = (
                    r.s1[i, 64 + 16 * half : 80 + 16 * half, :])

    for k in (1, 2, 3):
        copy_to("fa", ff_view(here), ff_view(here), a_peer(k)).start()

    r.asmf[96:112, :] = jnp.zeros((16, 128), F32)
    shared_at = pl.multiple_of(16 + 80 * c, 16)
    for i in range(8):
        piece = r.s1[i, pl.ds(shared_at, 16), :].astype(F32)
        for row in range(2):
            r.asmf[pl.ds(64 + 2 * i + row, 2, stride=16), :] = piece[2 * row : 2 * row + 2]
        r.asmf[96 + i : 97 + i, :] = piece[4:5]
    r.wio[here, 64:112, :] = r.asmf[64:112, :].astype(BF16)
    for k in (1, 2, 3):
        copy_to("wa", wo_view(here), wo_view(here), a_peer(k)).start()

    for k in (1, 2, 3):
        at = ring(z, -k)
        await_recv("tk", r.img.at[at, c], k - 1)
        copy_to("tf", r.img.at[at, c], r.img.at[at, c], sibling).start()
    sends_end("tf", r.img.at[:, 0])
    for k in (1, 2, 3):
        copy_to("ct", r.cot.at[ring(z, k)], r.cotb.at[z], z_peer(k)).start()
    sends_end("ct", r.cotb.at[pl.ds(0, 3)])
    await_recv("ia", r.wio.at[pl.ds(0, 3), pl.ds(0, 64)])
    for i in (1, 2, 3):
        at = group(ring(a, -i), b)
        for k in (1, 2, 3):
            copy_to("ib", wi_view(at), wi_view(at), b_peer(k)).start()
    for k in (1, 2, 3):
        copy_to("fb", ff_view(here), ff_view(here), b_peer(k)).start()
    sends_end("ia", r.wio.at[pl.ds(0, 3), pl.ds(0, 64)])
    sends_end("ib", r.wio.at[pl.ds(0, 12), pl.ds(0, 64)])
    await_recv("tf", r.img.at[:, 1 - c])

    for i in range(8):
        rows = r.img[i // 2, i % 2].astype(F32)
        for k in range(4):
            at = 4 * i + k
            pos = first_c[at : at + 1] * cos_f + second_c[at : at + 1] * sin_f
            r.sh[32 * at : 32 * at + 32, :] = (rows[32 * k : 32 * k + 32] + pos).astype(BF16)
    image = r.img[...].reshape(1024, 256)

    r.sht[...] = r.sh[...].T
    r.imgt[...] = image.T

    await_recv("fa", r.ff.at[c, pl.ds(0, 3)])
    for i in (1, 2, 3):
        at = group(ring(a, -i), b)
        for k in (1, 2, 3):
            copy_to("fc", ff_view(at), ff_view(at), b_peer(k), r.fc_r.at[k - 1]).start()
    for i in range(4):
        at = group(ring(a, -i), b)
        copy_to("fw", ff_view(at), ff_view(at), sibling).start()
    for k in (1, 2, 3):
        copy_to("wb", wo_view(here), wo_view(here), b_peer(k)).start()
    await_recv("wa", r.wio.at[pl.ds(0, 3), pl.ds(64, 48)])
    for i in (1, 2, 3):
        at = group(ring(a, -i), b)
        for k in (1, 2, 3):
            copy_to("wb", wo_view(at), wo_view(at), b_peer(k)).start()
    sends_end("fa", r.ff.at[c, pl.ds(0, 3)])
    sends_end("fb", r.ff.at[c, pl.ds(0, 3)])
    sends_end("fc", r.ff.at[c, pl.ds(0, 9)])
    sends_end("fw", r.ff.at[c])
    sends_end("wa", r.wio.at[pl.ds(0, 3), pl.ds(64, 48)])
    sends_end("wb", r.wio.at[pl.ds(0, 12), pl.ds(64, 48)])

    await_recv("ib", r.wio.at[pl.ds(0, 12), pl.ds(0, 64)])
    biases = jnp.zeros((16, 128), F32)
    for i in range(16):
        biases = biases + r.wio[i, 48:64, :].astype(F32)

    def w_part(k):
        return r.wio[:, 16 * k : 16 * k + 16, :].reshape(256, 128)

    queries = (dot(r.sh[...], w_part(0)) + biases[0:1]).astype(BF16)
    keys = dot(r.sh[...], w_part(1)).astype(BF16)
    values = (dot(image, w_part(2)) + biases[1:2]).astype(BF16)
    r.qq[...] = queries
    r.vv[...] = values
    r.kt[...] = keys.T
    r.vt[...] = values.T
    r.qt[0:128, :] = queries.T
    ones_row = iota((128, 1024), 0) == 0
    r.qt[128:256, :] = jnp.where(ones_row, 1.0, 0.0).astype(BF16)

    length = r.lens[z]

    zero = jnp.zeros((), BF16)
    head_of_lane = lax.div(iota((1024, 128), 1), HD)
    hidden_key = (iota((1024, 128), 0) >= length) & (iota((1024, 128), 1) == 0)
    bias = jnp.where(hidden_key, -1e30, 0.0).astype(BF16)
    for head in range(4):
        r.kx[head, :, 0:128] = jnp.where(head_of_lane == head, keys, zero)
        r.kx[head, :, 128:256] = bias

    for head in range(4):
        peak = None
        for k in range(0, 1024, 512):
            part = jnp.max(dot(r.kx[head, k : k + 512, :], r.qt[...]), axis=0, keepdims=True)
            peak = part if peak is None else jnp.maximum(peak, part)
        scores = dot(r.kx[head], r.qt[...])
        weights = jnp.exp2(scores * EXP2_SCALE - peak * EXP2_SCALE).astype(BF16)
        r.ee[head] = weights
        rows = slice(head * HD, head * HD + HD)
        left = jnp.concatenate([r.vt[rows, :], jnp.ones((16, 1024), BF16)], axis=0)
        mixed = dot(left, weights)
        inverse = 1.0 / mixed[HD : HD + 1]
        r.ot[rows, :] = mixed[0:HD] * inverse
        r.ri[head : head + 1, :] = inverse
        if head == 2:
            await_recv("fb", r.ff.at[c, pl.ds(0, 3)])
            for k in (1, 2, 3):
                at = group(a, ring(b, -k))
                copy_to("fw", ff_view(at), ff_view(at), sibling).start()

    r.mx[...] = r.ot[...].T.astype(BF16).reshape(4, 2, 128, 128)
    copy_to("mx", r.mx.at[:, 1 - c], r.mr, sibling).start()
    sends_end("mx", r.mr)

    for k in (1, 3, 2):
        await_recv("fc", r.ff.at[c, pl.ds(0, 3)], k - 1)
        for i in (1, 2, 3):
            at = group(ring(a, -i), ring(b, -k))
            copy_to("fw", ff_view(at), ff_view(at), sibling).start()

    await_recv("wb", r.wio.at[pl.ds(0, 12), pl.ds(64, 48)])
    rows = r.wio[:, 96:112, :].reshape(256, 128)
    spot_row, spot_lane = iota((256, 256), 0), iota((256, 256), 1)
    pick = spot_row == 16 * lax.div(spot_lane, 16) + lax.div(lax.rem(spot_lane, 16), 2)
    spread = dot_tn(rows, jnp.where(pick, 1.0, 0.0).astype(BF16))
    even_lane = lax.rem(iota((1, 256), 1), 2) == 0
    for i in range(8):
        r.vecs[i : i + 1, :] = jnp.where(
            even_lane, spread[2 * i : 2 * i + 1], spread[2 * i + 1 : 2 * i + 2])
    tile = iota((128, 256), 0) == 16 + lax.rem(iota((128, 256), 1), 16)
    wide = dot(rows, jnp.where(tile, 1.0, 0.0).astype(BF16))
    keep = lax.rem(spot_row, 32) == (
        16 * lax.div(spot_lane, 128) + lax.rem(lax.div(spot_lane, 16), 8))
    wide = jnp.where(keep, wide, 0.0).reshape(8, 32, 256)
    r.vecs[8:16, :] = jnp.sum(wide, axis=1)

    for head in range(4):
        r.vx[head, :, 0:128] = jnp.where(head_of_lane == head, r.vv[...], zero)
        r.vx[head, :, 128:256] = jnp.where(
            lax.div(iota((1024, 128), 1), 2) == head, 1.0, 0.0).astype(BF16)
        r.qm[head] = jnp.where(head_of_lane == head, r.qq[...], zero)

    def w_out_rows(half):
        low = r.wio[pl.ds(8 * half, 8), 64:80, :].reshape(128, 128)
        high = r.wio[pl.ds(8 * half, 8), 80:96, :].reshape(128, 128)
        return jnp.concatenate([low, high], axis=1)

    def vec(name):
        return r.vecs[ROW[name] : ROW[name] + 1, :]

    mixed_own = r.mx[:, c].reshape(512, 128)
    branch = dot(mixed_own, w_out_rows(c))
    await_recv("mx", r.mr)
    mixed_other = r.mr[...].reshape(512, 128)
    branch = branch + dot(mixed_other, w_out_rows(1 - c))
    first_sum = r.img[:, c].reshape(512, 256).astype(F32) + branch + vec("b_out")
    hidden, unit, inverse = norm_forward(first_sum, vec("gain1"), vec("shift1"))
    r.unit1[...] = unit
    r.inv1[...] = inverse
    r.hid[...] = hidden
    hidden_low = hidden.astype(BF16)
    r.hlow[...] = hidden_low
    r.hlt[...] = hidden_low.T

    await_recv("fw", r.ff.at[1 - c])

    def up_block(j):
        parts = [r.ff[0, :, 16 * k : 16 * k + 16, :].reshape(256, 256) for k in (2 * j, 2 * j + 1)]
        return jnp.concatenate(parts, axis=1)

    def down_block(j):
        return r.ff[1, 4 * j : 4 * j + 4, :, :].reshape(512, 256)

    r.acc[...] = r.hid[...] + vec("b_down")
    for j in range(4):
        up_shift = jnp.concatenate(
            [r.vecs[8 + 2 * j : 9 + 2 * j, :], r.vecs[9 + 2 * j : 10 + 2 * j, :]], axis=1)
        up = dot(r.hlow[...], up_block(j)) + up_shift
        square = up * up
        gate = 0.5 + 0.5 * jnp.tanh(up * (GELU_SCALE + GELU_SCALE * 0.044715 * square))
        active = up * gate
        slope = 2 * GELU_SCALE + 6 * 0.044715 * GELU_SCALE * square
        r.dgl[j] = (gate + active * (1.0 - gate) * slope).astype(BF16)
        active = active.astype(BF16)
        r.act[j] = active
        r.acc[...] += dot(active, down_block(j))

    out, unit, inverse = norm_forward(r.acc[...], vec("gain2"), vec("shift2"))
    r.lob[...] = out.astype(BF16).reshape(4, 128, 256)
    for k in (1, 2, 3):
        copy_to("lo", r.lob.at[ring(z, k)], r.lor.at[z], z_peer(k)).start()
    sends_end("lo", r.lob.at[pl.ds(0, 3)])
    own_copies = [pltpu.make_async_copy(r.lob.at[z], r.lor.at[z], r.own_s.at[0])]
    own_copies[0].start()

    await_recv("ct", r.cotb.at[pl.ds(0, 3)])
    d_out = r.cotb[...].reshape(512, 256).astype(F32)
    r.gv[ROW["gain2"] : ROW["gain2"] + 1, :] = column_sum(d_out * unit)
    r.gv[ROW["shift2"] : ROW["shift2"] + 1, :] = column_sum(d_out)
    d_second = norm_backward(d_out, unit, inverse, vec("gain2"))
    d_ffn = d_second.astype(BF16)
    r.dffn[...] = d_ffn
    r.gv[ROW["b_down"] : ROW["b_down"] + 1, :] = column_sum(d_ffn.astype(F32))
    r.acc[...] = d_second

    def first_sums(half):
        await_recv("gs", r.gs.at[pl.ds(0, 8)], half)

        @pl.when(c == 0)
        def _():
            rows = pl.ds(64 * half, 64)

            def add(g, carry):
                r.rs[g, rows] = (
                    r.gp[0, g, rows].astype(F32) + r.gs[g, rows].astype(F32)).astype(BF16)
                return carry

            lax.fori_loop(0, 16, add, 0)
            for k in (2, 1, 3):
                copy_to(
                    "r1", r.rs.at[pl.ds(4 * ring(a, k), 4), rows], r.r1.at[k - 1, :, rows],
                    a_peer(k)).start()

        @pl.when(c == 1)
        def _():
            def add(i, carry):
                at, to = 8 * half + i, 4 * lax.rem(i, 4) + 2 * half + lax.div(i, 4)
                r.rs[to] = (r.gp[1, at].astype(F32) + r.gs[at].astype(F32)).astype(BF16)
                return carry

            lax.fori_loop(0, 8, add, 0)
            part = pl.ds(2 * half, 2)
            for k in (2, 1, 3):
                copy_to(
                    "r1", r.rs.at[pl.ds(4 * ring(a, k) + 2 * half, 2)], r.r1.at[k - 1, part],
                    a_peer(k)).start()

    for j in range(4):
        d_active = dot_nt(r.dffn[...], down_block(j))
        d_up = (d_active * r.dgl[j].astype(F32)).astype(BF16)
        g_down = dot_tn(r.act[j], r.dffn[...])
        r.gp[1, 4 * j : 4 * j + 4] = g_down.astype(BF16).reshape(4, 128, 256)
        g_up = dot(r.hlt[...], d_up).astype(BF16)
        sums = column_sum(d_up.astype(F32))
        for k in range(2):
            at, lanes = 2 * j + k, slice(256 * k, 256 * k + 256)
            r.gp[0, :, 16 * at : 16 * at + 16, :] = g_up[:, lanes].reshape(16, 16, 256)
            r.gv[8 + at : 9 + at, :] = sums[:, lanes]
        r.acc[...] += dot_nt(d_up, up_block(j))

        @pl.when(c == 0)
        def _():
            part = pl.ds(4 * j, 4)
            copy_to("gs", r.gp.at[1, part], r.gs.at[part], sibling, r.gs_r.at[j // 2]).start()

        @pl.when(c == 1)
        def _():
            part = pl.ds(32 * j, 32)
            copy_to("gs", r.gp.at[0, :, part], r.gs.at[:, part], sibling, r.gs_r.at[j // 2]).start()

    sends_end("gs", r.gs)
    first_sums(0)

    d_hidden = r.acc[...]
    unit = r.unit1[...]
    r.gv[ROW["gain1"] : ROW["gain1"] + 1, :] = column_sum(d_hidden * unit)
    r.gv[ROW["shift1"] : ROW["shift1"] + 1, :] = column_sum(d_hidden)
    d_first = norm_backward(d_hidden, unit, r.inv1[...], vec("gain1"))
    r.dfirst[...] = d_first
    d_branch = d_first.astype(BF16)
    r.gv[ROW["b_out"] : ROW["b_out"] + 1, :] = column_sum(d_branch.astype(F32))
    r.dms[...] = dot_nt(d_branch, w_out_rows(1 - c)).astype(BF16).reshape(4, 128, 128)
    copy_to("dm", r.dms, r.dmx.at[:, c], sibling).start()
    sends_end("dm", r.dms)
    r.dmx[:, c] = dot_nt(d_branch, w_out_rows(c)).astype(BF16).reshape(4, 128, 128)

    def spot(g):
        return g * (1 - c) + (4 * lax.rem(g, 4) + lax.div(g, 4)) * c

    for half, mixed in ((c, r.mx[:, c].reshape(512, 128)), (1 - c, r.mr[...].reshape(512, 128))):
        g_out = dot_tn(mixed, d_branch).astype(BF16)
        for i in range(8):
            at = spot(8 * half + i)
            r.gwo[at, 0:16, :] = g_out[16 * i : 16 * i + 16, 0:128]
            r.gwo[at, 16:32, :] = g_out[16 * i : 16 * i + 16, 128:256]
    r.gv[0:2, :] = jnp.zeros((2, 256), F32)
    r.v0[...] = r.gv[...]

    first_sums(1)
    for k in (2, 1, 3):
        part, to = pl.ds(4 * ring(a, k), 4), a_peer(k)
        copy_to("g1", r.gwo.at[part], r.wo1.at[k - 1], to).start()
        copy_to("v1", r.v0, r.vr1.at[k - 1], to).start()
    sends_end("r1", r.r1)
    sends_end("g1", r.wo1)
    sends_end("v1", r.vr1)

    await_recv("dm", r.dmx.at[:, 1 - c])
    d_mixed_t = r.dmx[...].reshape(1024, 128).astype(F32).T
    extra = []
    for head in range(4):
        rows = slice(32 * head, 32 * head + 32)
        scaled = d_mixed_t[rows] * r.ri[head : head + 1, :]
        r.dot_[rows, :] = scaled.astype(BF16)
        inner = -column_sum(scaled * r.ot[rows, :])
        high = inner.astype(BF16).astype(F32)
        extra += [high, inner - high]
    extra.append(jnp.zeros((8, 1024), F32))
    r.dot_[128:144, :] = jnp.concatenate(extra, axis=0).astype(BF16)
    r.dot_[144:256, :] = jnp.zeros((112, 1024), BF16)
    r.doo[...] = r.dot_[0:128, :].T

    for head in range(4):
        d_probs = dot(r.vx[head], r.dot_[...])
        d_scores = r.ee[head] * d_probs.astype(BF16)
        r.ds[head % 2] = d_scores
        rows = slice(head * HD, head * HD + HD)
        r.dqt[rows, :] = dot(r.kt[rows, :], d_scores)
        if head == 3:
            await_recv("r1", r.r1)
            await_recv("g1", r.wo1)
            await_recv("v1", r.vr1)

            def add_first(i, carry):
                total = r.rs[4 * a + i].astype(F32)
                small = r.gwo[4 * a + i].astype(F32)
                for k in range(3):
                    total = total + r.r1[k, i].astype(F32)
                    small = small + r.wo1[k, i].astype(F32)
                r.s2[i] = total.astype(BF16)
                r.wos[i] = small.astype(BF16)
                return carry

            lax.fori_loop(0, 4, add_first, 0)
            r.v1[...] = r.v0[...] + r.vr1[0] + r.vr1[1] + r.vr1[2]
            for k in (1, 2, 3):
                part, to = ring(b, k), b_peer(k)
                copy_to("r2", r.s2.at[part], r.r2.at[k - 1], to).start()
                copy_to("g2", r.wos.at[part], r.wo2.at[k - 1], to).start()
                copy_to("v2", r.v1, r.vr2.at[k - 1], to).start()
            sends_end("r2", r.r2)
            sends_end("g2", r.wo2)
            sends_end("v2", r.vr2)

        do_masked = jnp.where(head_of_lane == head, r.doo[...], zero)
        for k in range(0, 1024, 256):
            d_key = dot(r.ds[head % 2, k : k + 256, :], r.qm[head])
            d_value = dot(r.ee[head, k : k + 256, :], do_masked)
            if head == 0:
                r.dk[k : k + 256, :] = d_key
                r.dv[k : k + 256, :] = d_value
            else:
                r.dk[k : k + 256, :] += d_key
                r.dv[k : k + 256, :] += d_value

    d_queries = (r.dqt[...] * SCORE_SCALE).T.astype(BF16)
    d_keys = (r.dk[...] * SCORE_SCALE).astype(BF16)
    d_values = r.dv[...].astype(BF16)
    for k, (left, right) in enumerate(((r.sht, d_queries), (r.sht, d_keys), (r.imgt, d_values))):
        g_part = dot(left[...], right).astype(BF16)
        for i in range(16):
            r.gio[i, 16 * k : 16 * k + 16, :] = g_part[16 * i : 16 * i + 16, :]
    ones = jnp.ones((1024, 128), BF16)
    sums = jnp.where(
        iota((128, 128), 1) < 64, dot_tn(d_queries, ones), dot_tn(d_values, ones)).astype(BF16)
    for i in range(8):
        r.gio[8 * c + i, 48:64, :] = sums[16 * i : 16 * i + 16, :]
        r.gio[8 * (1 - c) + i, 48:64, :] = jnp.zeros((16, 128), BF16)
    for k in range(1, 16):
        copy_to("q1", r.gio.at[ring(gx, k, 16)], r.q1.at[gx], gx_peer(k)).start()
    sends_end("q1", r.q1.at[pl.ds(0, 15)])

    d_tokens = (
        dot_nt(d_queries, w_part(0)) + dot_nt(d_keys, w_part(1)) + dot_nt(d_values, w_part(2)))
    r.gt[...] = d_tokens.astype(BF16).reshape(4, 2, 128, 256)
    copy_to("gt", r.gt.at[:, 1 - c], r.gtr, sibling).start()
    sends_end("gt", r.gtr)

    await_recv("gt", r.gtr)
    full = (
        r.dfirst[...]
        + r.gt[:, c].reshape(512, 256).astype(F32)
        + r.gtr[...].reshape(512, 256).astype(F32))
    r.gob[...] = full.astype(BF16).reshape(4, 128, 256)
    for k in (1, 2, 3):
        copy_to("go", r.gob.at[ring(z, k)], r.gor.at[z], z_peer(k)).start()
    sends_end("go", r.gob.at[pl.ds(0, 3)])

    await_recv("r2", r.r2)
    await_recv("g2", r.wo2)
    await_recv("v2", r.vr2)
    total = r.s2[b].astype(F32)
    small = r.wos[b].astype(F32)
    for k in range(3):
        total = total + r.r2[k].astype(F32)
        small = small + r.wo2[k].astype(F32)
    r.fin[0] = total[:, 0:128]
    r.fin[1] = total[:, 128:256]
    r.fwo[...] = small
    r.p3f[...] = jnp.zeros((8, 48, 128), F32)

    @pl.when(c == 0)
    def _():
        for i in range(8):
            for half in range(2):
                for row in range(2):
                    at = 16 * half + 8 * row
                    r.p3f[i, at : at + 8, :] = r.fin.at[half][
                        pl.ds(2 * i + row, 8, stride=16), :]

    @pl.when(c == 1)
    def _():
        for i in range(8):
            for half in range(2):
                r.p3f[i, 16 * half : 16 * half + 16, :] = r.fin[half, 16 * i : 16 * i + 16, :]

    for i in range(8):
        for row in range(2):
            at = 32 + 8 * row
            r.p3f[i, at : at + 2, :] = r.fwo[pl.ds(2 * i + row, 2, stride=16), :]
    sums = r.v1[...] + r.vr2[0] + r.vr2[1] + r.vr2[2]
    own_lanes = pltpu.roll(sums[0:8], lax.rem(256 - 16 * gx, 256), axis=1)[:, 0:128]
    up_sums = column_sum(jnp.where(iota((8, 256), 0) == lax.div(gx, 2), sums[8:16], 0.0))
    right = lax.rem(gx, 2).astype(F32)
    up_sums = up_sums[:, 0:128] * (1.0 - right) + up_sums[:, 128:256] * right
    for i in range(8):
        r.p3f[i, 34:40, :] = own_lanes[2:8]
        r.p3f[i, 42:43, :] = up_sums
    r.p3[...] = r.p3f[...].astype(BF16)
    for k in range(1, 8):
        copy_to("p3", r.p3.at[ring(gy, k, 8)], r.r3.at[gy], gy_peer(k)).start()
    sends_end("p3", r.p3.at[pl.ds(0, 7)])

    await_recv("q1", r.q1.at[pl.ds(0, 15)])
    total = r.gio[gx].astype(F32)
    for k in range(1, 16):
        total = total + r.q1[ring(gx, -k, 16)].astype(F32)
    r.fio[...] = total
    r.p4f[...] = jnp.zeros((8, 16, 128), F32)
    for i in range(8):
        for row in range(2):
            at = 8 * row
            r.p4f[i, at : at + 4, :] = r.fio[pl.ds(2 * i + row, 4, stride=16), :]
    r.p4[...] = r.p4f[...].astype(BF16)
    for k in range(1, 8):
        copy_to("p4", r.p4.at[ring(gy, k, 8)], r.r4.at[gy], gy_peer(k)).start()
    sends_end("p4", r.p4.at[pl.ds(0, 7)])

    own_copies += [
        pltpu.make_async_copy(r.gob.at[z], r.gor.at[z], r.own_s.at[1]),
        pltpu.make_async_copy(r.p3.at[gy], r.r3.at[gy], r.own_s.at[2]),
        pltpu.make_async_copy(r.p4.at[gy], r.r4.at[gy], r.own_s.at[3]),
    ]
    for copy in own_copies[1:]:
        copy.start()
    await_recv("lo", r.lor.at[pl.ds(0, 3)])
    await_recv("go", r.gor.at[pl.ds(0, 3)])
    await_recv("p3", r.r3.at[pl.ds(0, 7)])
    await_recv("p4", r.r4.at[pl.ds(0, 7)])
    for copy in own_copies:
        copy.wait()
    for make in closing:
        make().wait_send()


def unpack(*refs):
    r = Refs()
    for name, ref in zip(tuple(PACKED) + OUTPUTS, refs):
        setattr(r, name, ref)
    gy = lax.axis_index("gy")
    r.layer_out[...] = r.lor[...]
    r.grad_tokens[...] = r.gor[...].astype(F32)
    core0 = jnp.zeros((48, 128), F32)
    core1 = jnp.zeros((48, 128), F32)
    into0 = jnp.zeros((16, 128), F32)
    into1 = jnp.zeros((16, 128), F32)
    for i in range(4):
        core0 = core0 + r.r3[2 * i].astype(F32)
        core1 = core1 + r.r3[2 * i + 1].astype(F32)
        into0 = into0 + r.r4[2 * i].astype(F32)
        into1 = into1 + r.r4[2 * i + 1].astype(F32)
    r.g_w_down[:, 0:128] = core1[0:16]
    r.g_w_down[:, 128:256] = core1[16:32]
    w_out = core0 + core1
    for row in range(2):
        out_row = slice(row, row + 1)
        for j in range(8):
            for half in range(2):
                at = 16 * half + 8 * row + j
                lanes = 256 * j + 128 * half
                r.g_w_up[out_row, lanes : lanes + 128] = core0[at : at + 1]
        for k in range(3):
            at = 8 * row + k
            r.g_w_in[out_row, 256 * k : 256 * k + 128] = into0[at : at + 1]
            r.g_w_in[out_row, 256 * k + 128 : 256 * k + 256] = into1[at : at + 1]
        at = 32 + 8 * row
        r.g_w_out[out_row, 0:128] = w_out[at : at + 1]
        r.g_w_out[out_row, 128:256] = w_out[at + 1 : at + 2]
    biases = into0 + into1
    for name, lane in (("b_q", 0), ("b_v", 64)):
        pair = jnp.concatenate(
            [biases[3:4, lane : lane + 1], biases[11:12, lane : lane + 1]], axis=1)
        getattr(r, "g_" + name)[...] = pair.reshape(2)
    moved = pltpu.roll(w_out[32:48], lax.rem(128 - 2 * gy, 128), axis=1)
    for name in SMALL[2:]:
        row = ROW[name]
        getattr(r, "g_" + name)[...] = moved[row : row + 1, 0:2].reshape(2)
    moved = pltpu.roll(w_out[40:48], lax.rem(128 - 16 * gy, 128), axis=1)
    r.g_b_up[...] = moved[2:3, 0:16].reshape(16)


def body(
    tokens, lengths, w_in, b_q, b_v, w_out, b_out, gain_first, shift_first, w_up, b_up,
    w_down, b_down, gain_second, shift_second, cotangent,
):
    column = np.arange(D)
    freq = np.power(10000.0, -(2.0 * (column // 2)) / D).astype(np.float32)[None, :]
    args = (
        tokens, cotangent, lengths, jnp.asarray(freq), w_in, w_out, w_up, w_down,
        b_q, b_v, b_out, gain_first, shift_first, b_down, gain_second, shift_second, b_up,
    )
    vmem = pl.BlockSpec(memory_space=pltpu.VMEM)
    anywhere = pl.BlockSpec(memory_space=pl.ANY)
    in_specs = [anywhere] * len(args)
    in_specs[2] = pl.BlockSpec(memory_space=pltpu.SMEM)
    shape = jax.ShapeDtypeStruct
    vector = shape((2,), F32)
    scratch = [pltpu.VMEM(args[INPUTS.index(name)].shape, args[INPUTS.index(name)].dtype)
               for name in LOADED]
    scratch += [pltpu.VMEM(dims, kind) for dims, kind in SCRATCH.values()]
    scratch += [pltpu.SemaphoreType.DMA((count,)) for count in SEMS.values()]
    packed = pl.pallas_call(
        kernel,
        out_shape=tuple(shape(dims, kind) for dims, kind in PACKED.values()),
        in_specs=in_specs,
        out_specs=tuple([anywhere] * len(PACKED)),
        scratch_shapes=scratch,
        compiler_params=pltpu.CompilerParams(
            collective_id=0, has_side_effects=True, vmem_limit_bytes=VMEM_LIMIT),
        name="encoder_layer",
    )(*args)
    out_shape = (
        shape((4, 128, 256), BF16), shape((4, 128, 256), F32), shape((2, 768), F32),
        vector, vector, shape((2, 256), F32), vector, vector, vector,
        shape((2, 2048), F32), shape((16,), F32), shape((16, 256), F32),
        vector, vector, vector,
    )
    return pl.pallas_call(
        unpack,
        out_shape=out_shape,
        in_specs=[vmem] * len(packed),
        out_specs=tuple([vmem] * len(out_shape)),
        name="unpack_results",
    )(*packed)


def solution(mesh):
    both = ("gx", "gy")
    rows, vector, whole = P(both, None), P(both), P("gx", "gy", None)
    return jax.shard_map(
        body,
        mesh=mesh,
        in_specs=(
            whole, P("gx"), rows, vector, vector, rows, vector, vector, vector, rows, vector,
            rows, vector, vector, vector, whole,
        ),
        out_specs=(
            whole, whole, rows, vector, vector, rows, vector, vector, vector, rows, vector,
            rows, vector, vector, vector,
        ),
        check_vma=False,
    )
```

```python
import math

import jax
import jax.numpy as jnp
import numpy as np
from jax import lax
from jax.experimental import pallas as pl
from jax.experimental.pallas import tpu as pltpu
from jax.sharding import PartitionSpec as P

MESH = pl.DeviceIdType.MESH
F32 = jnp.float32
BF16 = jnp.bfloat16

D = 256
HD = 32
VMEM_LIMIT = 56 * 2**20
EPSILON = 1e-05
GELU_SCALE = math.sqrt(2.0 / math.pi)
SCORE_SCALE = 1.0 / math.sqrt(HD)
EXP2_SCALE = SCORE_SCALE * math.log2(math.e)


def dot(left, right):
    return jnp.dot(left, right, preferred_element_type=F32)


def dot_nt(left, right):
    return lax.dot_general(left, right, (((1,), (1,)), ((), ())), preferred_element_type=F32)


def dot_tn(left, right):
    return lax.dot_general(left, right, (((0,), (0,)), ((), ())), preferred_element_type=F32)


def iota(shape, dim):
    return lax.broadcasted_iota(jnp.int32, shape, dim)


def column_sum(values):
    return jnp.sum(values, axis=0, keepdims=True)


def norm_forward(values, gain, shift):
    centre = jnp.mean(values, axis=-1, keepdims=True)
    moved = values - centre
    spread = jnp.mean(moved * moved, axis=-1, keepdims=True)
    inverse = lax.rsqrt(spread + EPSILON)
    unit = moved * inverse
    return unit * gain + shift, unit, inverse


def norm_backward(d_out, unit, inverse, gain):
    d_unit = d_out * gain
    mean_d = jnp.mean(d_unit, axis=-1, keepdims=True)
    mean_du = jnp.mean(d_unit * unit, axis=-1, keepdims=True)
    return inverse * (d_unit - mean_d - unit * mean_du)


SCRATCH = dict(
    pf=((112, 128), F32),
    s1=((8, 112, 128), BF16),
    asmf=((384, 128), F32),
    img=((4, 2, 128, 256), BF16),
    cotb=((4, 128, 256), BF16),
    wio=((16, 112, 128), BF16),
    ff=((2, 16, 128, 256), BF16),
    vecs=((16, 256), F32),
    sh=((1024, 256), BF16),
    sht=((256, 1024), BF16),
    imgt=((256, 1024), BF16),
    kx=((4, 1024, 256), BF16),
    vx=((4, 1024, 256), BF16),
    qm=((4, 1024, 128), BF16),
    vv=((1024, 128), BF16),
    qq=((1024, 128), BF16),
    kt=((128, 1024), BF16),
    vt=((128, 1024), BF16),
    qt=((256, 1024), BF16),
    ee=((4, 1024, 1024), BF16),
    ot=((128, 1024), F32),
    ri=((8, 1024), F32),
    mx=((4, 2, 128, 128), BF16),
    mr=((4, 128, 128), BF16),
    hid=((512, 256), F32),
    hlow=((512, 256), BF16),
    hlt=((256, 512), BF16),
    unit1=((512, 256), F32),
    inv1=((512, 1), F32),
    act=((4, 512, 512), BF16),
    dgl=((4, 512, 512), BF16),
    acc=((512, 256), F32),
    lob=((4, 128, 256), BF16),
    dffn=((512, 256), BF16),
    gp=((2, 16, 128, 256), BF16),
    gs=((16, 128, 256), BF16),
    rs=((16, 128, 256), BF16),
    r1=((3, 4, 128, 256), BF16),
    s2=((4, 128, 256), BF16),
    r2=((3, 128, 256), BF16),
    fin=((2, 128, 128), F32),
    gv=((16, 256), F32),
    dfirst=((512, 256), F32),
    dms=((4, 128, 128), BF16),
    dmx=((4, 2, 128, 128), BF16),
    dot_=((256, 1024), BF16),
    doo=((1024, 128), BF16),
    ds=((2, 1024, 1024), BF16),
    dqt=((128, 1024), F32),
    dk=((1024, 128), F32),
    dv=((1024, 128), F32),
    gwo=((16, 32, 128), BF16),
    wo1=((3, 4, 32, 128), BF16),
    wos=((4, 32, 128), BF16),
    wo2=((3, 32, 128), BF16),
    fwo=((32, 128), F32),
    gio=((16, 64, 128), BF16),
    q1=((16, 64, 128), BF16),
    fio=((64, 128), F32),
    v0=((16, 256), F32),
    vr1=((3, 16, 256), F32),
    v1=((16, 256), F32),
    vr2=((3, 16, 256), F32),
    gt=((4, 2, 128, 256), BF16),
    gtr=((4, 128, 256), BF16),
    gob=((4, 128, 256), BF16),
    p3f=((8, 48, 128), F32),
    p3=((8, 48, 128), BF16),
    p4f=((8, 16, 128), F32),
    p4=((8, 16, 128), BF16),
)

GROUPS = (
    "s1", "s2", "tk", "tf", "ct", "ia", "ib", "wa", "wb", "fa", "fb", "fc", "fw", "mx", "dm", "lo",
    "gs", "r1", "r2", "g1", "g2", "v1", "v2", "q1", "gt", "go", "p3", "p4",
)
SEMS = dict(in_s=16, own_s=4, tk_r=3, fc_r=3, gs_r=2, fa_r=3, ia_r=3)
for group_name in GROUPS:
    SEMS.setdefault(group_name + "_s", 1)
    SEMS.setdefault(group_name + "_r", 1)

INPUTS = (
    "tok", "cot", "lens", "freq", "w_in", "w_out", "w_up", "w_down",
    "b_q", "b_v", "b_out", "gain1", "shift1", "b_down", "gain2", "shift2", "b_up",
)
OUTPUTS = (
    "layer_out", "grad_tokens", "g_w_in", "g_b_q", "g_b_v", "g_w_out", "g_b_out",
    "g_gain1", "g_shift1", "g_w_up", "g_b_up", "g_w_down", "g_b_down", "g_gain2", "g_shift2",
)
PACKED = dict(
    lor=((4, 128, 256), BF16),
    gor=((4, 128, 256), BF16),
    r3=((8, 48, 128), BF16),
    r4=((8, 16, 128), BF16),
)
LOADED = INPUTS[3:]
SMALL = ("b_q", "b_v", "b_out", "gain1", "shift1", "b_down", "gain2", "shift2")
ROW = {name: row for row, name in enumerate(SMALL)}


class Refs:
    pass


def kernel(*refs):
    r = Refs()
    held = tuple("v_" + name for name in LOADED)
    names = INPUTS + tuple(PACKED) + held + tuple(SCRATCH) + tuple(SEMS)
    for name, ref in zip(names, refs):
        setattr(r, name, ref)

    gx, gy = lax.axis_index("gx"), lax.axis_index("gy")
    x, y = lax.div(gx, 4), lax.rem(gx, 4)
    z, c = lax.div(gy, 2), lax.rem(gy, 2)
    a = x * (1 - c) + y * c
    b = y * (1 - c) + x * c

    def group(a_at, b_at):
        return a_at * (4 - 3 * c) + b_at * (1 + 3 * c)

    def ring(at, step, size=4):
        return lax.rem(at + (step % size), size)

    def a_peer(step):
        return (group(ring(a, step), b), gy)

    def b_peer(step):
        return (group(a, ring(b, step)), gy)

    def gx_peer(step):
        return (ring(gx, step, 16), gy)

    def z_peer(step):
        return (gx, 2 * ring(z, step) + c)

    def gy_peer(step):
        return (gx, ring(gy, step, 8))

    sibling = (gx, 2 * z + 1 - c)
    here = group(a, b)

    def remote(src, dst, send, recv, device):
        return pltpu.make_async_remote_copy(
            src_ref=src, dst_ref=dst, send_sem=send, recv_sem=recv,
            device_id=device, device_id_type=MESH,
        )

    closing = []

    def sem(name):
        return getattr(r, name).at[0]

    def copy_to(name, src, dst, device, recv=None):
        return remote(src, dst, sem(name + "_s"), recv or sem(name + "_r"), device)

    def sends_end(name, ref):
        closing.append(lambda: remote(ref, ref, sem(name + "_s"), sem(name + "_s"), sibling))

    def await_recv(name, ref, at=0):
        done = getattr(r, name + "_r").at[at]
        remote(ref, ref, done, done, sibling).wait_recv()

    loads = [
        pltpu.make_async_copy(getattr(r, name), getattr(r, "v_" + name), r.in_s.at[i])
        for i, name in enumerate(LOADED)
    ]
    loads.append(pltpu.make_async_copy(r.tok.at[z], r.img.at[z, c], r.in_s.at[14]))
    loads.append(pltpu.make_async_copy(r.cot.at[z], r.cotb.at[z], r.in_s.at[15]))

    barrier = pltpu.get_barrier_semaphore()
    peers = [gy_peer(k) for k in (4, 5, 3, 2, 6, 1, 7)]
    peers += [a_peer(k) for k in (2, 1, 3)] + [b_peer(k) for k in (2, 1, 3)]
    for peer in peers:
        pl.semaphore_signal(barrier, inc=1, device_id=peer, device_id_type=MESH)
    for load in loads:
        load.start()
    for load in loads:
        load.wait()

    rows = r.v_w_in[...].astype(F32)
    for row in range(2):
        for k in range(6):
            at = 6 * row + k
            r.pf[at : at + 1, :] = rows[row : row + 1, k * 128 : (k + 1) * 128]
    lane = iota((1, 256), 1)
    place = 2 * (8 * gx + gy)
    for i, name in enumerate(("b_q", "b_v")):
        pair = getattr(r, "v_" + name)[...].astype(F32).reshape(1, 2)
        row = jnp.where(lane == place, pair[:, 0:1], 0.0)
        row = jnp.where(lane == place + 1, pair[:, 1:2], row)
        r.pf[12 + 2 * i : 13 + 2 * i, :] = row[:, 0:128]
        r.pf[13 + 2 * i : 14 + 2 * i, :] = row[:, 128:256]
    r.s1[gy, 0:16, :] = r.pf[0:16, :].astype(BF16)

    rows = r.v_w_out[...].astype(F32)
    r.pf[16:32, :] = jnp.zeros((16, 128), F32)
    for row in range(2):
        for k in range(2):
            at = 16 + 2 * row + k
            r.pf[at : at + 1, :] = rows[row : row + 1, k * 128 : (k + 1) * 128]
    thin = iota((1, 128), 1)
    packed = jnp.zeros((1, 128), F32)
    for i, name in enumerate(SMALL):
        pair = getattr(r, "v_" + name)[...].astype(F32).reshape(1, 2)
        packed = jnp.where(thin == 2 * i, pair[:, 0:1], packed)
        packed = jnp.where(thin == 2 * i + 1, pair[:, 1:2], packed)
    up_bias = r.v_b_up[...].astype(F32).reshape(1, 16)
    for k in range(16):
        packed = jnp.where(thin == 16 + k, up_bias[:, k : k + 1], packed)
    r.pf[20:21, :] = packed
    rows = r.v_w_up[...].astype(F32)
    for row in range(2):
        for k in range(16):
            at = 32 + 16 * row + k
            r.pf[at : at + 1, :] = rows[row : row + 1, k * 128 : (k + 1) * 128]
    r.s1[gy, 16:64, :] = r.pf[16:64, :].astype(BF16)
    r.s1[gy, 64:80, :] = r.v_w_down[:, 0:128]
    r.s1[gy, 80:96, :] = r.v_w_down[:, 128:256]
    r.s1[gy, 96:112, :] = r.pf[16:32, :].astype(BF16)

    pl.semaphore_wait(barrier, 13)

    def first_part(at):
        return r.s1.at[at, pl.ds(0, 16)]

    def second_part(at, core):
        return r.s1.at[at, pl.ds(pl.multiple_of(16 + 48 * core, 16), 48)]

    for k in (4, 5, 3, 2, 6, 1, 7):
        copy_to("s1", first_part(gy), first_part(gy), gy_peer(k)).start()
    sends_end("s1", r.s1.at[pl.ds(0, 7), pl.ds(0, 16)])
    for k in (4, 5, 3, 2, 6, 1, 7):
        part = second_part(gy, lax.rem(gy + k, 2))
        copy_to("s2", part, part, gy_peer(k)).start()
    sends_end("s2", r.s1.at[pl.ds(0, 7), pl.ds(0, 48)])
    for k in (2, 1, 3):
        copy_to("tk", r.tok.at[ring(z, k)], r.img.at[z, c], z_peer(k), r.tk_r.at[k - 1]).start()
    sends_end("tk", r.cotb.at[pl.ds(0, 3)])
    copy_to("tf", r.img.at[z, c], r.img.at[z, c], sibling).start()

    freq = r.v_freq[...]
    even = lax.rem(iota((1, 256), 1), 2) == 0
    fine = iota((32, 256), 0).astype(F32) * freq
    coarse = iota((32, 256), 0).astype(F32) * 32.0 * freq
    sin_f, cos_f = jnp.sin(fine), jnp.cos(fine)
    sin_c, cos_c = jnp.sin(coarse), jnp.cos(coarse)
    first_c = jnp.where(even, sin_c, cos_c)
    second_c = jnp.where(even, cos_c, -sin_c)

    await_recv("s1", r.s1.at[pl.ds(0, 7), pl.ds(0, 16)])
    bias_low, bias_high = jnp.zeros((1, 128), F32), jnp.zeros((1, 128), F32)
    share0, share1 = (1 - c).astype(F32), c.astype(F32)
    for i in range(8):
        piece = r.s1[i, 0:16, :].astype(F32)
        for row in range(2):
            r.asmf[pl.ds(2 * i + row, 6, stride=16), :] = piece[row * 6 : row * 6 + 6]
        bias_low = bias_low + piece[12:13] * share0 + piece[13:14] * share1
        bias_high = bias_high + piece[14:15] * share0 + piece[15:16] * share1
    for k in range(3):
        rows = r.asmf[pl.ds(pl.multiple_of(32 * k + 16 * c, 16), 16), :]
        r.wio[here, 16 * k : 16 * k + 16, :] = rows.astype(BF16)
    r.wio[here, 48:64, :] = jnp.concatenate(
        [bias_low, bias_high, jnp.zeros((14, 128), F32)], axis=0).astype(BF16)

    def wi_view(at):
        return r.wio.at[at, pl.ds(0, 64)]

    for k in (2, 1, 3):
        copy_to("ia", wi_view(here), wi_view(here), a_peer(k), r.ia_r.at[k - 1]).start()
    for k in (2, 1, 3):
        copy_to("ib", wi_view(here), wi_view(here), b_peer(k)).start()

    await_recv("s2", r.s1.at[pl.ds(0, 7), pl.ds(0, 48)])

    def wo_view(at):
        return r.wio.at[at, pl.ds(64, 48)]

    def ff_view(at):
        return r.ff.at[c, at]

    @pl.when(c == 0)
    def _():
        for i in range(8):
            piece = r.s1[i, 32:64, :].astype(F32)
            for row in range(2):
                r.asmf[pl.ds(128 + 2 * i + row, 16, stride=16), :] = (
                    piece[16 * row : 16 * row + 16])
        for j in range(8):
            for half in range(2):
                at = 128 + 16 * (2 * j + half)
                r.ff[0, here, 16 * j : 16 * j + 16, 128 * half : 128 * half + 128] = (
                    r.asmf[at : at + 16, :].astype(BF16))

    @pl.when(c == 1)
    def _():
        for i in range(8):
            for half in range(2):
                r.ff[1, here, 16 * i : 16 * i + 16, 128 * half : 128 * half + 128] = (
                    r.s1[i, 64 + 16 * half : 80 + 16 * half, :])

    for k in (2, 1, 3):
        copy_to("fa", ff_view(here), ff_view(here), a_peer(k), r.fa_r.at[k - 1]).start()

    r.asmf[96:112, :] = jnp.zeros((16, 128), F32)
    shared_at = pl.multiple_of(16 + 80 * c, 16)
    for i in range(8):
        piece = r.s1[i, pl.ds(shared_at, 16), :].astype(F32)
        for row in range(2):
            r.asmf[pl.ds(64 + 2 * i + row, 2, stride=16), :] = piece[2 * row : 2 * row + 2]
        r.asmf[96 + i : 97 + i, :] = piece[4:5]
    r.wio[here, 64:112, :] = r.asmf[64:112, :].astype(BF16)
    for k in (2, 1, 3):
        copy_to("wa", wo_view(here), wo_view(here), a_peer(k)).start()

    for k in (2, 1, 3):
        at = ring(z, -k)
        await_recv("tk", r.img.at[at, c], k - 1)
        copy_to("tf", r.img.at[at, c], r.img.at[at, c], sibling).start()
    sends_end("tf", r.img.at[:, 0])
    for k in (2, 1, 3):
        copy_to("ct", r.cot.at[ring(z, k)], r.cotb.at[z], z_peer(k)).start()
    sends_end("ct", r.cotb.at[pl.ds(0, 3)])
    for i in (1, 3, 2):
        at = group(ring(a, -i), b)
        await_recv("ia", wi_view(at), i - 1)
        for k in (2, 1, 3):
            copy_to("ib", wi_view(at), wi_view(at), b_peer(k)).start()
    for k in (2, 1, 3):
        copy_to("fb", ff_view(here), ff_view(here), b_peer(k)).start()
    sends_end("ia", r.wio.at[pl.ds(0, 3), pl.ds(0, 64)])
    sends_end("ib", r.wio.at[pl.ds(0, 12), pl.ds(0, 64)])
    await_recv("tf", r.img.at[:, 1 - c])

    for i in range(8):
        rows = r.img[i // 2, i % 2].astype(F32)
        for k in range(4):
            at = 4 * i + k
            pos = first_c[at : at + 1] * cos_f + second_c[at : at + 1] * sin_f
            r.sh[32 * at : 32 * at + 32, :] = (rows[32 * k : 32 * k + 32] + pos).astype(BF16)
    image = r.img[...].reshape(1024, 256)

    r.sht[...] = r.sh[...].T
    r.imgt[...] = image.T

    for i in (1, 3, 2):
        at = group(ring(a, -i), b)
        await_recv("fa", ff_view(at), i - 1)
        for k in (2, 1, 3):
            copy_to("fc", ff_view(at), ff_view(at), b_peer(k), r.fc_r.at[k - 1]).start()
    for i in range(4):
        at = group(ring(a, -i), b)
        copy_to("fw", ff_view(at), ff_view(at), sibling).start()
    for k in (2, 1, 3):
        copy_to("wb", wo_view(here), wo_view(here), b_peer(k)).start()
    await_recv("wa", r.wio.at[pl.ds(0, 3), pl.ds(64, 48)])
    for i in (1, 2, 3):
        at = group(ring(a, -i), b)
        for k in (2, 1, 3):
            copy_to("wb", wo_view(at), wo_view(at), b_peer(k)).start()
    sends_end("fa", r.ff.at[c, pl.ds(0, 3)])
    sends_end("fb", r.ff.at[c, pl.ds(0, 3)])
    sends_end("fc", r.ff.at[c, pl.ds(0, 9)])
    sends_end("fw", r.ff.at[c])
    sends_end("wa", r.wio.at[pl.ds(0, 3), pl.ds(64, 48)])
    sends_end("wb", r.wio.at[pl.ds(0, 12), pl.ds(64, 48)])

    await_recv("ib", r.wio.at[pl.ds(0, 12), pl.ds(0, 64)])
    biases = jnp.zeros((16, 128), F32)
    for i in range(16):
        biases = biases + r.wio[i, 48:64, :].astype(F32)

    def w_part(k):
        return r.wio[:, 16 * k : 16 * k + 16, :].reshape(256, 128)

    queries = (dot(r.sh[...], w_part(0)) + biases[0:1]).astype(BF16)
    keys = dot(r.sh[...], w_part(1)).astype(BF16)
    values = (dot(image, w_part(2)) + biases[1:2]).astype(BF16)
    r.qq[...] = queries
    r.vv[...] = values
    r.kt[...] = keys.T
    r.vt[...] = values.T
    r.qt[0:128, :] = queries.T
    ones_row = iota((128, 1024), 0) == 0
    r.qt[128:256, :] = jnp.where(ones_row, 1.0, 0.0).astype(BF16)

    length = r.lens[z]

    zero = jnp.zeros((), BF16)
    head_of_lane = lax.div(iota((1024, 128), 1), HD)
    hidden_key = (iota((1024, 128), 0) >= length) & (iota((1024, 128), 1) == 0)
    bias = jnp.where(hidden_key, -1e30, 0.0).astype(BF16)
    for head in range(4):
        r.kx[head, :, 0:128] = jnp.where(head_of_lane == head, keys, zero)
        r.kx[head, :, 128:256] = bias

    for head in range(4):
        peak = None
        for k in range(0, 1024, 512):
            part = jnp.max(dot(r.kx[head, k : k + 512, :], r.qt[...]), axis=0, keepdims=True)
            peak = part if peak is None else jnp.maximum(peak, part)
        scores = dot(r.kx[head], r.qt[...])
        weights = jnp.exp2(scores * EXP2_SCALE - peak * EXP2_SCALE).astype(BF16)
        r.ee[head] = weights
        rows = slice(head * HD, head * HD + HD)
        left = jnp.concatenate([r.vt[rows, :], jnp.ones((16, 1024), BF16)], axis=0)
        mixed = dot(left, weights)
        inverse = 1.0 / mixed[HD : HD + 1]
        r.ot[rows, :] = mixed[0:HD] * inverse
        r.ri[head : head + 1, :] = inverse
        if head == 2:
            await_recv("fb", r.ff.at[c, pl.ds(0, 3)])
            for k in (2, 1, 3):
                at = group(a, ring(b, -k))
                copy_to("fw", ff_view(at), ff_view(at), sibling).start()

    r.mx[...] = r.ot[...].T.astype(BF16).reshape(4, 2, 128, 128)
    copy_to("mx", r.mx.at[:, 1 - c], r.mr, sibling).start()
    sends_end("mx", r.mr)

    for k in (1, 3, 2):
        await_recv("fc", r.ff.at[c, pl.ds(0, 3)], k - 1)
        for i in (1, 2, 3):
            at = group(ring(a, -i), ring(b, -k))
            copy_to("fw", ff_view(at), ff_view(at), sibling).start()

    await_recv("wb", r.wio.at[pl.ds(0, 12), pl.ds(64, 48)])
    rows = r.wio[:, 96:112, :].reshape(256, 128)
    spot_row, spot_lane = iota((256, 256), 0), iota((256, 256), 1)
    pick = spot_row == 16 * lax.div(spot_lane, 16) + lax.div(lax.rem(spot_lane, 16), 2)
    spread = dot_tn(rows, jnp.where(pick, 1.0, 0.0).astype(BF16))
    even_lane = lax.rem(iota((1, 256), 1), 2) == 0
    for i in range(8):
        r.vecs[i : i + 1, :] = jnp.where(
            even_lane, spread[2 * i : 2 * i + 1], spread[2 * i + 1 : 2 * i + 2])
    tile = iota((128, 256), 0) == 16 + lax.rem(iota((128, 256), 1), 16)
    wide = dot(rows, jnp.where(tile, 1.0, 0.0).astype(BF16))
    keep = lax.rem(spot_row, 32) == (
        16 * lax.div(spot_lane, 128) + lax.rem(lax.div(spot_lane, 16), 8))
    wide = jnp.where(keep, wide, 0.0).reshape(8, 32, 256)
    r.vecs[8:16, :] = jnp.sum(wide, axis=1)

    for head in range(4):
        r.vx[head, :, 0:128] = jnp.where(head_of_lane == head, r.vv[...], zero)
        r.vx[head, :, 128:256] = jnp.where(
            lax.div(iota((1024, 128), 1), 2) == head, 1.0, 0.0).astype(BF16)
        r.qm[head] = jnp.where(head_of_lane == head, r.qq[...], zero)

    def w_out_rows(half):
        low = r.wio[pl.ds(8 * half, 8), 64:80, :].reshape(128, 128)
        high = r.wio[pl.ds(8 * half, 8), 80:96, :].reshape(128, 128)
        return jnp.concatenate([low, high], axis=1)

    def vec(name):
        return r.vecs[ROW[name] : ROW[name] + 1, :]

    mixed_own = r.mx[:, c].reshape(512, 128)
    branch = dot(mixed_own, w_out_rows(c))
    await_recv("mx", r.mr)
    mixed_other = r.mr[...].reshape(512, 128)
    branch = branch + dot(mixed_other, w_out_rows(1 - c))
    first_sum = r.img[:, c].reshape(512, 256).astype(F32) + branch + vec("b_out")
    hidden, unit, inverse = norm_forward(first_sum, vec("gain1"), vec("shift1"))
    r.unit1[...] = unit
    r.inv1[...] = inverse
    r.hid[...] = hidden
    hidden_low = hidden.astype(BF16)
    r.hlow[...] = hidden_low
    r.hlt[...] = hidden_low.T

    await_recv("fw", r.ff.at[1 - c])

    def up_block(j):
        parts = [r.ff[0, :, 16 * k : 16 * k + 16, :].reshape(256, 256) for k in (2 * j, 2 * j + 1)]
        return jnp.concatenate(parts, axis=1)

    def down_block(j):
        return r.ff[1, 4 * j : 4 * j + 4, :, :].reshape(512, 256)

    r.acc[...] = r.hid[...] + vec("b_down")
    for j in range(4):
        up_shift = jnp.concatenate(
            [r.vecs[8 + 2 * j : 9 + 2 * j, :], r.vecs[9 + 2 * j : 10 + 2 * j, :]], axis=1)
        up = dot(r.hlow[...], up_block(j)) + up_shift
        square = up * up
        gate = 0.5 + 0.5 * jnp.tanh(up * (GELU_SCALE + GELU_SCALE * 0.044715 * square))
        active = up * gate
        slope = 2 * GELU_SCALE + 6 * 0.044715 * GELU_SCALE * square
        r.dgl[j] = (gate + active * (1.0 - gate) * slope).astype(BF16)
        active = active.astype(BF16)
        r.act[j] = active
        r.acc[...] += dot(active, down_block(j))

    out, unit, inverse = norm_forward(r.acc[...], vec("gain2"), vec("shift2"))
    r.lob[...] = out.astype(BF16).reshape(4, 128, 256)
    for k in (2, 1, 3):
        copy_to("lo", r.lob.at[ring(z, k)], r.lor.at[z], z_peer(k)).start()
    sends_end("lo", r.lob.at[pl.ds(0, 3)])
    own_copies = [pltpu.make_async_copy(r.lob.at[z], r.lor.at[z], r.own_s.at[0])]
    own_copies[0].start()

    await_recv("ct", r.cotb.at[pl.ds(0, 3)])
    d_out = r.cotb[...].reshape(512, 256).astype(F32)
    r.gv[ROW["gain2"] : ROW["gain2"] + 1, :] = column_sum(d_out * unit)
    r.gv[ROW["shift2"] : ROW["shift2"] + 1, :] = column_sum(d_out)
    d_second = norm_backward(d_out, unit, inverse, vec("gain2"))
    d_ffn = d_second.astype(BF16)
    r.dffn[...] = d_ffn
    r.gv[ROW["b_down"] : ROW["b_down"] + 1, :] = column_sum(d_ffn.astype(F32))
    r.acc[...] = d_second

    def first_sums(half):
        await_recv("gs", r.gs.at[pl.ds(0, 8)], half)

        @pl.when(c == 0)
        def _():
            rows = pl.ds(64 * half, 64)

            def add(g, carry):
                r.rs[g, rows] = (
                    r.gp[0, g, rows].astype(F32) + r.gs[g, rows].astype(F32)).astype(BF16)
                return carry

            lax.fori_loop(0, 16, add, 0)
            for k in (2, 1, 3):
                copy_to(
                    "r1", r.rs.at[pl.ds(4 * ring(a, k), 4), rows], r.r1.at[k - 1, :, rows],
                    a_peer(k)).start()

        @pl.when(c == 1)
        def _():
            def add(i, carry):
                at, to = 8 * half + i, 4 * lax.rem(i, 4) + 2 * half + lax.div(i, 4)
                r.rs[to] = (r.gp[1, at].astype(F32) + r.gs[at].astype(F32)).astype(BF16)
                return carry

            lax.fori_loop(0, 8, add, 0)
            part = pl.ds(2 * half, 2)
            for k in (2, 1, 3):
                copy_to(
                    "r1", r.rs.at[pl.ds(4 * ring(a, k) + 2 * half, 2)], r.r1.at[k - 1, part],
                    a_peer(k)).start()

    for j in range(4):
        d_active = dot_nt(r.dffn[...], down_block(j))
        d_up = (d_active * r.dgl[j].astype(F32)).astype(BF16)
        g_down = dot_tn(r.act[j], r.dffn[...])
        r.gp[1, 4 * j : 4 * j + 4] = g_down.astype(BF16).reshape(4, 128, 256)
        g_up = dot(r.hlt[...], d_up).astype(BF16)
        sums = column_sum(d_up.astype(F32))
        for k in range(2):
            at, lanes = 2 * j + k, slice(256 * k, 256 * k + 256)
            r.gp[0, :, 16 * at : 16 * at + 16, :] = g_up[:, lanes].reshape(16, 16, 256)
            r.gv[8 + at : 9 + at, :] = sums[:, lanes]
        r.acc[...] += dot_nt(d_up, up_block(j))

        @pl.when(c == 0)
        def _():
            part = pl.ds(4 * j, 4)
            copy_to("gs", r.gp.at[1, part], r.gs.at[part], sibling, r.gs_r.at[j // 2]).start()

        @pl.when(c == 1)
        def _():
            part = pl.ds(32 * j, 32)
            copy_to("gs", r.gp.at[0, :, part], r.gs.at[:, part], sibling, r.gs_r.at[j // 2]).start()

    sends_end("gs", r.gs)
    first_sums(0)

    d_hidden = r.acc[...]
    unit = r.unit1[...]
    r.gv[ROW["gain1"] : ROW["gain1"] + 1, :] = column_sum(d_hidden * unit)
    r.gv[ROW["shift1"] : ROW["shift1"] + 1, :] = column_sum(d_hidden)
    d_first = norm_backward(d_hidden, unit, r.inv1[...], vec("gain1"))
    r.dfirst[...] = d_first
    d_branch = d_first.astype(BF16)
    r.gv[ROW["b_out"] : ROW["b_out"] + 1, :] = column_sum(d_branch.astype(F32))
    r.dms[...] = dot_nt(d_branch, w_out_rows(1 - c)).astype(BF16).reshape(4, 128, 128)
    copy_to("dm", r.dms, r.dmx.at[:, c], sibling).start()
    sends_end("dm", r.dms)
    r.dmx[:, c] = dot_nt(d_branch, w_out_rows(c)).astype(BF16).reshape(4, 128, 128)

    def spot(g):
        return g * (1 - c) + (4 * lax.rem(g, 4) + lax.div(g, 4)) * c

    for half, mixed in ((c, r.mx[:, c].reshape(512, 128)), (1 - c, r.mr[...].reshape(512, 128))):
        g_out = dot_tn(mixed, d_branch).astype(BF16)
        for i in range(8):
            at = spot(8 * half + i)
            r.gwo[at, 0:16, :] = g_out[16 * i : 16 * i + 16, 0:128]
            r.gwo[at, 16:32, :] = g_out[16 * i : 16 * i + 16, 128:256]
    r.gv[0:2, :] = jnp.zeros((2, 256), F32)
    r.v0[...] = r.gv[...]

    first_sums(1)
    for k in (2, 1, 3):
        part, to = pl.ds(4 * ring(a, k), 4), a_peer(k)
        copy_to("g1", r.gwo.at[part], r.wo1.at[k - 1], to).start()
        copy_to("v1", r.v0, r.vr1.at[k - 1], to).start()
    sends_end("r1", r.r1)
    sends_end("g1", r.wo1)
    sends_end("v1", r.vr1)

    await_recv("dm", r.dmx.at[:, 1 - c])
    d_mixed_t = r.dmx[...].reshape(1024, 128).astype(F32).T
    extra = []
    for head in range(4):
        rows = slice(32 * head, 32 * head + 32)
        scaled = d_mixed_t[rows] * r.ri[head : head + 1, :]
        r.dot_[rows, :] = scaled.astype(BF16)
        inner = -column_sum(scaled * r.ot[rows, :])
        high = inner.astype(BF16).astype(F32)
        extra += [high, inner - high]
    extra.append(jnp.zeros((8, 1024), F32))
    r.dot_[128:144, :] = jnp.concatenate(extra, axis=0).astype(BF16)
    r.dot_[144:256, :] = jnp.zeros((112, 1024), BF16)
    r.doo[...] = r.dot_[0:128, :].T

    for head in range(4):
        d_probs = dot(r.vx[head], r.dot_[...])
        d_scores = r.ee[head] * d_probs.astype(BF16)
        r.ds[head % 2] = d_scores
        rows = slice(head * HD, head * HD + HD)
        r.dqt[rows, :] = dot(r.kt[rows, :], d_scores)
        if head == 3:
            await_recv("r1", r.r1)
            await_recv("g1", r.wo1)
            await_recv("v1", r.vr1)

            def add_first(i, carry):
                total = r.rs[4 * a + i].astype(F32)
                small = r.gwo[4 * a + i].astype(F32)
                for k in range(3):
                    total = total + r.r1[k, i].astype(F32)
                    small = small + r.wo1[k, i].astype(F32)
                r.s2[i] = total.astype(BF16)
                r.wos[i] = small.astype(BF16)
                return carry

            lax.fori_loop(0, 4, add_first, 0)
            r.v1[...] = r.v0[...] + r.vr1[0] + r.vr1[1] + r.vr1[2]
            for k in (2, 1, 3):
                part, to = ring(b, k), b_peer(k)
                copy_to("r2", r.s2.at[part], r.r2.at[k - 1], to).start()
                copy_to("g2", r.wos.at[part], r.wo2.at[k - 1], to).start()
                copy_to("v2", r.v1, r.vr2.at[k - 1], to).start()
            sends_end("r2", r.r2)
            sends_end("g2", r.wo2)
            sends_end("v2", r.vr2)

        do_masked = jnp.where(head_of_lane == head, r.doo[...], zero)
        for k in range(0, 1024, 256):
            d_key = dot(r.ds[head % 2, k : k + 256, :], r.qm[head])
            d_value = dot(r.ee[head, k : k + 256, :], do_masked)
            if head == 0:
                r.dk[k : k + 256, :] = d_key
                r.dv[k : k + 256, :] = d_value
            else:
                r.dk[k : k + 256, :] += d_key
                r.dv[k : k + 256, :] += d_value

    d_queries = (r.dqt[...] * SCORE_SCALE).T.astype(BF16)
    d_keys = (r.dk[...] * SCORE_SCALE).astype(BF16)
    d_values = r.dv[...].astype(BF16)
    for k, (left, right) in enumerate(((r.sht, d_queries), (r.sht, d_keys), (r.imgt, d_values))):
        g_part = dot(left[...], right).astype(BF16)
        for i in range(16):
            r.gio[i, 16 * k : 16 * k + 16, :] = g_part[16 * i : 16 * i + 16, :]
    ones = jnp.ones((1024, 128), BF16)
    sums = jnp.where(
        iota((128, 128), 1) < 64, dot_tn(d_queries, ones), dot_tn(d_values, ones)).astype(BF16)
    for i in range(8):
        r.gio[8 * c + i, 48:64, :] = sums[16 * i : 16 * i + 16, :]
        r.gio[8 * (1 - c) + i, 48:64, :] = jnp.zeros((16, 128), BF16)
    for k in (10, 6, 14, 9, 11, 2, 8, 5, 7, 13, 15, 1, 3, 4, 12):
        copy_to("q1", r.gio.at[ring(gx, k, 16)], r.q1.at[gx], gx_peer(k)).start()
    sends_end("q1", r.q1.at[pl.ds(0, 15)])

    d_tokens = (
        dot_nt(d_queries, w_part(0)) + dot_nt(d_keys, w_part(1)) + dot_nt(d_values, w_part(2)))
    r.gt[...] = d_tokens.astype(BF16).reshape(4, 2, 128, 256)
    copy_to("gt", r.gt.at[:, 1 - c], r.gtr, sibling).start()
    sends_end("gt", r.gtr)

    await_recv("gt", r.gtr)
    full = (
        r.dfirst[...]
        + r.gt[:, c].reshape(512, 256).astype(F32)
        + r.gtr[...].reshape(512, 256).astype(F32))
    r.gob[...] = full.astype(BF16).reshape(4, 128, 256)
    for k in (2, 1, 3):
        copy_to("go", r.gob.at[ring(z, k)], r.gor.at[z], z_peer(k)).start()
    sends_end("go", r.gob.at[pl.ds(0, 3)])

    await_recv("r2", r.r2)
    await_recv("g2", r.wo2)
    await_recv("v2", r.vr2)
    total = r.s2[b].astype(F32)
    small = r.wos[b].astype(F32)
    for k in range(3):
        total = total + r.r2[k].astype(F32)
        small = small + r.wo2[k].astype(F32)
    r.fin[0] = total[:, 0:128]
    r.fin[1] = total[:, 128:256]
    r.fwo[...] = small
    r.p3f[...] = jnp.zeros((8, 48, 128), F32)

    @pl.when(c == 0)
    def _():
        for i in range(8):
            for half in range(2):
                for row in range(2):
                    at = 16 * half + 8 * row
                    r.p3f[i, at : at + 8, :] = r.fin.at[half][
                        pl.ds(2 * i + row, 8, stride=16), :]

    @pl.when(c == 1)
    def _():
        for i in range(8):
            for half in range(2):
                r.p3f[i, 16 * half : 16 * half + 16, :] = r.fin[half, 16 * i : 16 * i + 16, :]

    for i in range(8):
        for row in range(2):
            at = 32 + 8 * row
            r.p3f[i, at : at + 2, :] = r.fwo[pl.ds(2 * i + row, 2, stride=16), :]
    sums = r.v1[...] + r.vr2[0] + r.vr2[1] + r.vr2[2]
    own_lanes = pltpu.roll(sums[0:8], lax.rem(256 - 16 * gx, 256), axis=1)[:, 0:128]
    up_sums = column_sum(jnp.where(iota((8, 256), 0) == lax.div(gx, 2), sums[8:16], 0.0))
    right = lax.rem(gx, 2).astype(F32)
    up_sums = up_sums[:, 0:128] * (1.0 - right) + up_sums[:, 128:256] * right
    for i in range(8):
        r.p3f[i, 34:40, :] = own_lanes[2:8]
        r.p3f[i, 42:43, :] = up_sums
    r.p3[...] = r.p3f[...].astype(BF16)
    for k in (4, 5, 3, 2, 6, 1, 7):
        copy_to("p3", r.p3.at[ring(gy, k, 8)], r.r3.at[gy], gy_peer(k)).start()
    sends_end("p3", r.p3.at[pl.ds(0, 7)])

    await_recv("q1", r.q1.at[pl.ds(0, 15)])
    total = r.gio[gx].astype(F32)
    for k in range(1, 16):
        total = total + r.q1[ring(gx, -k, 16)].astype(F32)
    r.fio[...] = total
    r.p4f[...] = jnp.zeros((8, 16, 128), F32)
    for i in range(8):
        for row in range(2):
            at = 8 * row
            r.p4f[i, at : at + 4, :] = r.fio[pl.ds(2 * i + row, 4, stride=16), :]
    r.p4[...] = r.p4f[...].astype(BF16)
    for k in (4, 5, 3, 2, 6, 1, 7):
        copy_to("p4", r.p4.at[ring(gy, k, 8)], r.r4.at[gy], gy_peer(k)).start()
    sends_end("p4", r.p4.at[pl.ds(0, 7)])

    own_copies += [
        pltpu.make_async_copy(r.gob.at[z], r.gor.at[z], r.own_s.at[1]),
        pltpu.make_async_copy(r.p3.at[gy], r.r3.at[gy], r.own_s.at[2]),
        pltpu.make_async_copy(r.p4.at[gy], r.r4.at[gy], r.own_s.at[3]),
    ]
    for copy in own_copies[1:]:
        copy.start()
    await_recv("lo", r.lor.at[pl.ds(0, 3)])
    await_recv("go", r.gor.at[pl.ds(0, 3)])
    await_recv("p3", r.r3.at[pl.ds(0, 7)])
    await_recv("p4", r.r4.at[pl.ds(0, 7)])
    for copy in own_copies:
        copy.wait()
    for make in closing:
        make().wait_send()


def unpack(*refs):
    r = Refs()
    for name, ref in zip(tuple(PACKED) + OUTPUTS, refs):
        setattr(r, name, ref)
    gy = lax.axis_index("gy")
    r.layer_out[...] = r.lor[...]
    r.grad_tokens[...] = r.gor[...].astype(F32)
    core0 = jnp.zeros((48, 128), F32)
    core1 = jnp.zeros((48, 128), F32)
    into0 = jnp.zeros((16, 128), F32)
    into1 = jnp.zeros((16, 128), F32)
    for i in range(4):
        core0 = core0 + r.r3[2 * i].astype(F32)
        core1 = core1 + r.r3[2 * i + 1].astype(F32)
        into0 = into0 + r.r4[2 * i].astype(F32)
        into1 = into1 + r.r4[2 * i + 1].astype(F32)
    r.g_w_down[:, 0:128] = core1[0:16]
    r.g_w_down[:, 128:256] = core1[16:32]
    w_out = core0 + core1
    for row in range(2):
        out_row = slice(row, row + 1)
        for j in range(8):
            for half in range(2):
                at = 16 * half + 8 * row + j
                lanes = 256 * j + 128 * half
                r.g_w_up[out_row, lanes : lanes + 128] = core0[at : at + 1]
        for k in range(3):
            at = 8 * row + k
            r.g_w_in[out_row, 256 * k : 256 * k + 128] = into0[at : at + 1]
            r.g_w_in[out_row, 256 * k + 128 : 256 * k + 256] = into1[at : at + 1]
        at = 32 + 8 * row
        r.g_w_out[out_row, 0:128] = w_out[at : at + 1]
        r.g_w_out[out_row, 128:256] = w_out[at + 1 : at + 2]
    biases = into0 + into1
    for name, lane in (("b_q", 0), ("b_v", 64)):
        pair = jnp.concatenate(
            [biases[3:4, lane : lane + 1], biases[11:12, lane : lane + 1]], axis=1)
        getattr(r, "g_" + name)[...] = pair.reshape(2)
    moved = pltpu.roll(w_out[32:48], lax.rem(128 - 2 * gy, 128), axis=1)
    for name in SMALL[2:]:
        row = ROW[name]
        getattr(r, "g_" + name)[...] = moved[row : row + 1, 0:2].reshape(2)
    moved = pltpu.roll(w_out[40:48], lax.rem(128 - 16 * gy, 128), axis=1)
    r.g_b_up[...] = moved[2:3, 0:16].reshape(16)


def body(
    tokens, lengths, w_in, b_q, b_v, w_out, b_out, gain_first, shift_first, w_up, b_up,
    w_down, b_down, gain_second, shift_second, cotangent,
):
    column = np.arange(D)
    freq = np.power(10000.0, -(2.0 * (column // 2)) / D).astype(np.float32)[None, :]
    args = (
        tokens, cotangent, lengths, jnp.asarray(freq), w_in, w_out, w_up, w_down,
        b_q, b_v, b_out, gain_first, shift_first, b_down, gain_second, shift_second, b_up,
    )
    vmem = pl.BlockSpec(memory_space=pltpu.VMEM)
    anywhere = pl.BlockSpec(memory_space=pl.ANY)
    in_specs = [anywhere] * len(args)
    in_specs[2] = pl.BlockSpec(memory_space=pltpu.SMEM)
    shape = jax.ShapeDtypeStruct
    vector = shape((2,), F32)
    scratch = [pltpu.VMEM(args[INPUTS.index(name)].shape, args[INPUTS.index(name)].dtype)
               for name in LOADED]
    scratch += [pltpu.VMEM(dims, kind) for dims, kind in SCRATCH.values()]
    scratch += [pltpu.SemaphoreType.DMA((count,)) for count in SEMS.values()]
    packed = pl.pallas_call(
        kernel,
        out_shape=tuple(shape(dims, kind) for dims, kind in PACKED.values()),
        in_specs=in_specs,
        out_specs=tuple([anywhere] * len(PACKED)),
        scratch_shapes=scratch,
        compiler_params=pltpu.CompilerParams(
            collective_id=0, has_side_effects=True, vmem_limit_bytes=VMEM_LIMIT),
        name="encoder_layer",
    )(*args)
    out_shape = (
        shape((4, 128, 256), BF16), shape((4, 128, 256), F32), shape((2, 768), F32),
        vector, vector, shape((2, 256), F32), vector, vector, vector,
        shape((2, 2048), F32), shape((16,), F32), shape((16, 256), F32),
        vector, vector, vector,
    )
    return pl.pallas_call(
        unpack,
        out_shape=out_shape,
        in_specs=[vmem] * len(packed),
        out_specs=tuple([vmem] * len(out_shape)),
        name="unpack_results",
    )(*packed)


def solution(mesh):
    both = ("gx", "gy")
    rows, vector, whole = P(both, None), P(both), P("gx", "gy", None)
    return jax.shard_map(
        body,
        mesh=mesh,
        in_specs=(
            whole, P("gx"), rows, vector, vector, rows, vector, vector, vector, rows, vector,
            rows, vector, vector, vector, whole,
        ),
        out_specs=(
            whole, whole, rows, vector, vector, rows, vector, vector, vector, rows, vector,
            rows, vector, vector, vector,
        ),
        check_vma=False,
    )
```

```python
import math

import jax
import jax.numpy as jnp
import numpy as np
from jax import lax
from jax.experimental import pallas as pl
from jax.experimental.pallas import tpu as pltpu
from jax.sharding import PartitionSpec as P

MESH = pl.DeviceIdType.MESH
F32 = jnp.float32
BF16 = jnp.bfloat16

D = 256
HD = 32
VMEM_LIMIT = 56 * 2**20
EPSILON = 1e-05
GELU_SCALE = math.sqrt(2.0 / math.pi)
SCORE_SCALE = 1.0 / math.sqrt(HD)
EXP2_SCALE = SCORE_SCALE * math.log2(math.e)


def dot(left, right):
    return jnp.dot(left, right, preferred_element_type=F32)


def dot_nt(left, right):
    return lax.dot_general(left, right, (((1,), (1,)), ((), ())), preferred_element_type=F32)


def dot_tn(left, right):
    return lax.dot_general(left, right, (((0,), (0,)), ((), ())), preferred_element_type=F32)


def iota(shape, dim):
    return lax.broadcasted_iota(jnp.int32, shape, dim)


def column_sum(values):
    return jnp.sum(values, axis=0, keepdims=True)


def norm_forward(values, gain, shift):
    centre = jnp.mean(values, axis=-1, keepdims=True)
    moved = values - centre
    spread = jnp.mean(moved * moved, axis=-1, keepdims=True)
    inverse = lax.rsqrt(spread + EPSILON)
    unit = moved * inverse
    return unit * gain + shift, unit, inverse


def norm_backward(d_out, unit, inverse, gain):
    d_unit = d_out * gain
    mean_d = jnp.mean(d_unit, axis=-1, keepdims=True)
    mean_du = jnp.mean(d_unit * unit, axis=-1, keepdims=True)
    return inverse * (d_unit - mean_d - unit * mean_du)


SCRATCH = dict(
    pf=((112, 128), F32),
    s1=((8, 112, 128), BF16),
    asmf=((400, 128), F32),
    img=((4, 2, 128, 256), BF16),
    cotb=((4, 128, 256), BF16),
    wio=((16, 112, 128), BF16),
    ff=((2, 16, 128, 256), BF16),
    vecs=((16, 256), F32),
    sh=((1024, 256), BF16),
    sht=((256, 1024), BF16),
    imgt=((256, 1024), BF16),
    kx=((4, 1024, 256), BF16),
    vx=((4, 1024, 256), BF16),
    qm=((4, 1024, 128), BF16),
    vv=((1024, 128), BF16),
    qq=((1024, 128), BF16),
    kt=((128, 1024), BF16),
    vt=((128, 1024), BF16),
    qt=((256, 1024), BF16),
    ee=((4, 1024, 1024), BF16),
    ot=((128, 1024), F32),
    ri=((8, 1024), F32),
    mx=((4, 2, 128, 128), BF16),
    mr=((4, 128, 128), BF16),
    hid=((512, 256), F32),
    hlow=((512, 256), BF16),
    hlt=((256, 512), BF16),
    unit1=((512, 256), F32),
    inv1=((512, 1), F32),
    act=((4, 512, 512), BF16),
    dgl=((4, 512, 512), BF16),
    acc=((512, 256), F32),
    lob=((4, 128, 256), BF16),
    dffn=((512, 256), BF16),
    gp=((2, 16, 128, 256), BF16),
    gs=((16, 128, 256), BF16),
    rs=((16, 128, 256), BF16),
    r1=((3, 4, 128, 256), BF16),
    s2=((4, 128, 256), BF16),
    r2=((3, 128, 256), BF16),
    fin=((2, 144, 128), F32),
    gv=((16, 256), F32),
    dfirst=((512, 256), F32),
    dms=((4, 128, 128), BF16),
    dmx=((4, 2, 128, 128), BF16),
    dot_=((256, 1024), BF16),
    doo=((1024, 128), BF16),
    ds=((2, 1024, 1024), BF16),
    dqt=((128, 1024), F32),
    dk=((1024, 128), F32),
    dv=((1024, 128), F32),
    gwo=((16, 32, 128), BF16),
    wo1=((3, 4, 32, 128), BF16),
    wos=((4, 32, 128), BF16),
    wo2=((3, 32, 128), BF16),
    fwo=((144, 128), F32),
    gio=((16, 64, 128), BF16),
    q1=((16, 64, 128), BF16),
    fio=((144, 128), F32),
    v0=((16, 256), F32),
    vr1=((3, 16, 256), F32),
    v1=((16, 256), F32),
    vr2=((3, 16, 256), F32),
    gt=((4, 2, 128, 256), BF16),
    gtr=((4, 128, 256), BF16),
    gob=((4, 128, 256), BF16),
    p3f=((8, 48, 128), F32),
    p3=((8, 48, 128), BF16),
    p4f=((8, 16, 128), F32),
    p4=((8, 16, 128), BF16),
)

GROUPS = (
    "s1", "s2", "tk", "tf", "ct", "ia", "ib", "wa", "wb", "fa", "fb", "fc", "fw", "mx", "dm", "lo",
    "gs", "r1", "r2", "g1", "g2", "v1", "v2", "q1", "gt", "go", "p3", "p4",
)
SEMS = dict(in_s=16, own_s=4, tk_r=3, fc_r=3, gs_r=2, fa_r=3, ia_r=3)
for group_name in GROUPS:
    SEMS.setdefault(group_name + "_s", 1)
    SEMS.setdefault(group_name + "_r", 1)

INPUTS = (
    "tok", "cot", "lens", "freq", "w_in", "w_out", "w_up", "w_down",
    "b_q", "b_v", "b_out", "gain1", "shift1", "b_down", "gain2", "shift2", "b_up",
)
OUTPUTS = (
    "layer_out", "grad_tokens", "g_w_in", "g_b_q", "g_b_v", "g_w_out", "g_b_out",
    "g_gain1", "g_shift1", "g_w_up", "g_b_up", "g_w_down", "g_b_down", "g_gain2", "g_shift2",
)
PACKED = dict(
    lor=((4, 128, 256), BF16),
    gor=((4, 128, 256), BF16),
    r3=((8, 48, 128), BF16),
    r4=((8, 16, 128), BF16),
)
LOADED = INPUTS[3:]
SMALL = ("b_q", "b_v", "b_out", "gain1", "shift1", "b_down", "gain2", "shift2")
ROW = {name: row for row, name in enumerate(SMALL)}


class Refs:
    pass


def kernel(*refs):
    r = Refs()
    held = tuple("v_" + name for name in LOADED)
    names = INPUTS + tuple(PACKED) + held + tuple(SCRATCH) + tuple(SEMS)
    for name, ref in zip(names, refs):
        setattr(r, name, ref)

    gx, gy = lax.axis_index("gx"), lax.axis_index("gy")
    x, y = lax.div(gx, 4), lax.rem(gx, 4)
    z, c = lax.div(gy, 2), lax.rem(gy, 2)
    a = x * (1 - c) + y * c
    b = y * (1 - c) + x * c

    def group(a_at, b_at):
        return a_at * (4 - 3 * c) + b_at * (1 + 3 * c)

    def ring(at, step, size=4):
        return lax.rem(at + (step % size), size)

    def a_peer(step):
        return (group(ring(a, step), b), gy)

    def b_peer(step):
        return (group(a, ring(b, step)), gy)

    def gx_peer(step):
        return (ring(gx, step, 16), gy)

    def z_peer(step):
        return (gx, 2 * ring(z, step) + c)

    def gy_peer(step):
        return (gx, ring(gy, step, 8))

    sibling = (gx, 2 * z + 1 - c)
    here = group(a, b)

    def remote(src, dst, send, recv, device):
        return pltpu.make_async_remote_copy(
            src_ref=src, dst_ref=dst, send_sem=send, recv_sem=recv,
            device_id=device, device_id_type=MESH,
        )

    closing = []

    def sem(name):
        return getattr(r, name).at[0]

    def copy_to(name, src, dst, device, recv=None):
        return remote(src, dst, sem(name + "_s"), recv or sem(name + "_r"), device)

    def sends_end(name, ref):
        closing.append(lambda: remote(ref, ref, sem(name + "_s"), sem(name + "_s"), sibling))

    def await_recv(name, ref, at=0):
        done = getattr(r, name + "_r").at[at]
        remote(ref, ref, done, done, sibling).wait_recv()

    loads = [
        pltpu.make_async_copy(getattr(r, name), getattr(r, "v_" + name), r.in_s.at[i])
        for i, name in enumerate(LOADED)
    ]
    loads.append(pltpu.make_async_copy(r.tok.at[z], r.img.at[z, c], r.in_s.at[14]))
    loads.append(pltpu.make_async_copy(r.cot.at[z], r.cotb.at[z], r.in_s.at[15]))

    barrier = pltpu.get_barrier_semaphore()
    peers = [gy_peer(k) for k in (4, 5, 3, 2, 6, 1, 7)]
    peers += [a_peer(k) for k in (2, 1, 3)] + [b_peer(k) for k in (2, 1, 3)]
    for peer in peers:
        pl.semaphore_signal(barrier, inc=1, device_id=peer, device_id_type=MESH)
    for load in loads:
        load.start()
    for load in loads:
        load.wait()

    rows = r.v_w_in[...].astype(F32)
    for row in range(2):
        for k in range(6):
            at = 6 * row + k
            r.pf[at : at + 1, :] = rows[row : row + 1, k * 128 : (k + 1) * 128]
    lane = iota((1, 256), 1)
    place = 2 * (8 * gx + gy)
    for i, name in enumerate(("b_q", "b_v")):
        pair = getattr(r, "v_" + name)[...].astype(F32).reshape(1, 2)
        row = jnp.where(lane == place, pair[:, 0:1], 0.0)
        row = jnp.where(lane == place + 1, pair[:, 1:2], row)
        r.pf[12 + 2 * i : 13 + 2 * i, :] = row[:, 0:128]
        r.pf[13 + 2 * i : 14 + 2 * i, :] = row[:, 128:256]
    r.s1[gy, 0:16, :] = r.pf[0:16, :].astype(BF16)

    rows = r.v_w_out[...].astype(F32)
    r.pf[16:32, :] = jnp.zeros((16, 128), F32)
    for row in range(2):
        for k in range(2):
            at = 16 + 2 * row + k
            r.pf[at : at + 1, :] = rows[row : row + 1, k * 128 : (k + 1) * 128]
    thin = iota((1, 128), 1)
    packed = jnp.zeros((1, 128), F32)
    for i, name in enumerate(SMALL):
        pair = getattr(r, "v_" + name)[...].astype(F32).reshape(1, 2)
        packed = jnp.where(thin == 2 * i, pair[:, 0:1], packed)
        packed = jnp.where(thin == 2 * i + 1, pair[:, 1:2], packed)
    up_bias = r.v_b_up[...].astype(F32).reshape(1, 16)
    for k in range(16):
        packed = jnp.where(thin == 16 + k, up_bias[:, k : k + 1], packed)
    r.pf[20:21, :] = packed
    rows = r.v_w_up[...].astype(F32)
    for row in range(2):
        for k in range(16):
            at = 32 + 16 * row + k
            r.pf[at : at + 1, :] = rows[row : row + 1, k * 128 : (k + 1) * 128]
    r.s1[gy, 16:64, :] = r.pf[16:64, :].astype(BF16)
    r.s1[gy, 64:80, :] = r.v_w_down[:, 0:128]
    r.s1[gy, 80:96, :] = r.v_w_down[:, 128:256]
    r.s1[gy, 96:112, :] = r.pf[16:32, :].astype(BF16)

    pl.semaphore_wait(barrier, 13)

    def first_part(at):
        return r.s1.at[at, pl.ds(0, 16)]

    def second_part(at, core):
        return r.s1.at[at, pl.ds(pl.multiple_of(16 + 48 * core, 16), 48)]

    for k in (4, 5, 3, 2, 6, 1, 7):
        copy_to("s1", first_part(gy), first_part(gy), gy_peer(k)).start()
    sends_end("s1", r.s1.at[pl.ds(0, 7), pl.ds(0, 16)])
    for k in (4, 5, 3, 2, 6, 1, 7):
        part = second_part(gy, lax.rem(gy + k, 2))
        copy_to("s2", part, part, gy_peer(k)).start()
    sends_end("s2", r.s1.at[pl.ds(0, 7), pl.ds(0, 48)])
    for k in (2, 1, 3):
        copy_to("tk", r.tok.at[ring(z, k)], r.img.at[z, c], z_peer(k), r.tk_r.at[k - 1]).start()
    sends_end("tk", r.cotb.at[pl.ds(0, 3)])
    copy_to("tf", r.img.at[z, c], r.img.at[z, c], sibling).start()

    freq = r.v_freq[...]
    even = lax.rem(iota((1, 256), 1), 2) == 0
    fine = iota((32, 256), 0).astype(F32) * freq
    coarse = iota((32, 256), 0).astype(F32) * 32.0 * freq
    sin_f, cos_f = jnp.sin(fine), jnp.cos(fine)
    sin_c, cos_c = jnp.sin(coarse), jnp.cos(coarse)
    first_c = jnp.where(even, sin_c, cos_c)
    second_c = jnp.where(even, cos_c, -sin_c)

    await_recv("s1", r.s1.at[pl.ds(0, 7), pl.ds(0, 16)])
    bias_low, bias_high = jnp.zeros((1, 128), F32), jnp.zeros((1, 128), F32)
    share0, share1 = (1 - c).astype(F32), c.astype(F32)
    for i in range(8):
        piece = r.s1[i, 0:16, :].astype(F32)
        for row in range(2):
            r.asmf[pl.ds(2 * i + row, 6, stride=16), :] = piece[row * 6 : row * 6 + 6]
        bias_low = bias_low + piece[12:13] * share0 + piece[13:14] * share1
        bias_high = bias_high + piece[14:15] * share0 + piece[15:16] * share1
    for k in range(3):
        rows = r.asmf[pl.ds(pl.multiple_of(32 * k + 16 * c, 16), 16), :]
        r.wio[here, 16 * k : 16 * k + 16, :] = rows.astype(BF16)
    r.wio[here, 48:64, :] = jnp.concatenate(
        [bias_low, bias_high, jnp.zeros((14, 128), F32)], axis=0).astype(BF16)

    def wi_view(at):
        return r.wio.at[at, pl.ds(0, 64)]

    for k in (2, 1, 3):
        copy_to("ia", wi_view(here), wi_view(here), a_peer(k), r.ia_r.at[k - 1]).start()
    for k in (2, 1, 3):
        copy_to("ib", wi_view(here), wi_view(here), b_peer(k)).start()

    await_recv("s2", r.s1.at[pl.ds(0, 7), pl.ds(0, 48)])

    def wo_view(at):
        return r.wio.at[at, pl.ds(64, 48)]

    def ff_view(at):
        return r.ff.at[c, at]

    @pl.when(c == 0)
    def _():
        for i in range(8):
            piece = r.s1[i, 32:64, :].astype(F32)
            for row in range(2):
                r.asmf[pl.ds(128 + 2 * i + row, 16, stride=16), :] = (
                    piece[16 * row : 16 * row + 16])
        for j in range(8):
            for half in range(2):
                at = 128 + 16 * (2 * j + half)
                r.ff[0, here, 16 * j : 16 * j + 16, 128 * half : 128 * half + 128] = (
                    r.asmf[at : at + 16, :].astype(BF16))

    @pl.when(c == 1)
    def _():
        for i in range(8):
            for half in range(2):
                r.ff[1, here, 16 * i : 16 * i + 16, 128 * half : 128 * half + 128] = (
                    r.s1[i, 64 + 16 * half : 80 + 16 * half, :])

    for k in (2, 1, 3):
        copy_to("fa", ff_view(here), ff_view(here), a_peer(k), r.fa_r.at[k - 1]).start()

    r.asmf[96:112, :] = jnp.zeros((16, 128), F32)
    shared_at = pl.multiple_of(16 + 80 * c, 16)
    for i in range(8):
        piece = r.s1[i, pl.ds(shared_at, 16), :].astype(F32)
        for row in range(2):
            r.asmf[pl.ds(64 + 2 * i + row, 2, stride=16), :] = piece[2 * row : 2 * row + 2]
        r.asmf[96 + i : 97 + i, :] = piece[4:5]
    r.wio[here, 64:112, :] = r.asmf[64:112, :].astype(BF16)
    for k in (2, 1, 3):
        copy_to("wa", wo_view(here), wo_view(here), a_peer(k)).start()

    for k in (2, 1, 3):
        at = ring(z, -k)
        await_recv("tk", r.img.at[at, c], k - 1)
        copy_to("tf", r.img.at[at, c], r.img.at[at, c], sibling).start()
    sends_end("tf", r.img.at[:, 0])
    for k in (2, 1, 3):
        copy_to("ct", r.cot.at[ring(z, k)], r.cotb.at[z], z_peer(k)).start()
    sends_end("ct", r.cotb.at[pl.ds(0, 3)])
    for i in (1, 3, 2):
        at = group(ring(a, -i), b)
        await_recv("ia", wi_view(at), i - 1)
        for k in (2, 1, 3):
            copy_to("ib", wi_view(at), wi_view(at), b_peer(k)).start()
    for k in (2, 1, 3):
        copy_to("fb", ff_view(here), ff_view(here), b_peer(k)).start()
    sends_end("ia", r.wio.at[pl.ds(0, 3), pl.ds(0, 64)])
    sends_end("ib", r.wio.at[pl.ds(0, 12), pl.ds(0, 64)])
    await_recv("tf", r.img.at[:, 1 - c])

    for i in range(8):
        rows = r.img[i // 2, i % 2].astype(F32)
        for k in range(4):
            at = 4 * i + k
            pos = first_c[at : at + 1] * cos_f + second_c[at : at + 1] * sin_f
            r.sh[32 * at : 32 * at + 32, :] = (rows[32 * k : 32 * k + 32] + pos).astype(BF16)
    image = r.img[...].reshape(1024, 256)

    r.sht[...] = r.sh[...].T
    r.imgt[...] = image.T

    for i in (1, 3, 2):
        at = group(ring(a, -i), b)
        await_recv("fa", ff_view(at), i - 1)
        for k in (2, 1, 3):
            copy_to("fc", ff_view(at), ff_view(at), b_peer(k), r.fc_r.at[k - 1]).start()
    for i in range(4):
        at = group(ring(a, -i), b)
        copy_to("fw", ff_view(at), ff_view(at), sibling).start()
    for k in (2, 1, 3):
        copy_to("wb", wo_view(here), wo_view(here), b_peer(k)).start()
    await_recv("wa", r.wio.at[pl.ds(0, 3), pl.ds(64, 48)])
    for i in (1, 2, 3):
        at = group(ring(a, -i), b)
        for k in (2, 1, 3):
            copy_to("wb", wo_view(at), wo_view(at), b_peer(k)).start()
    sends_end("fa", r.ff.at[c, pl.ds(0, 3)])
    sends_end("fb", r.ff.at[c, pl.ds(0, 3)])
    sends_end("fc", r.ff.at[c, pl.ds(0, 9)])
    sends_end("fw", r.ff.at[c])
    sends_end("wa", r.wio.at[pl.ds(0, 3), pl.ds(64, 48)])
    sends_end("wb", r.wio.at[pl.ds(0, 12), pl.ds(64, 48)])

    await_recv("ib", r.wio.at[pl.ds(0, 12), pl.ds(0, 64)])
    biases = jnp.zeros((16, 128), F32)
    for i in range(16):
        biases = biases + r.wio[i, 48:64, :].astype(F32)

    def w_part(k):
        return r.wio[:, 16 * k : 16 * k + 16, :].reshape(256, 128)

    queries = (dot(r.sh[...], w_part(0)) + biases[0:1]).astype(BF16)
    keys = dot(r.sh[...], w_part(1)).astype(BF16)
    values = (dot(image, w_part(2)) + biases[1:2]).astype(BF16)
    r.qq[...] = queries
    r.vv[...] = values
    r.kt[...] = keys.T
    r.vt[...] = values.T
    r.qt[0:128, :] = queries.T
    ones_row = iota((128, 1024), 0) == 0
    r.qt[128:256, :] = jnp.where(ones_row, 1.0, 0.0).astype(BF16)

    length = r.lens[z]

    zero = jnp.zeros((), BF16)
    head_of_lane = lax.div(iota((1024, 128), 1), HD)
    hidden_key = (iota((1024, 128), 0) >= length) & (iota((1024, 128), 1) == 0)
    bias = jnp.where(hidden_key, -1e30, 0.0).astype(BF16)
    for head in range(4):
        r.kx[head, :, 0:128] = jnp.where(head_of_lane == head, keys, zero)
        r.kx[head, :, 128:256] = bias

    for head in range(4):
        peak = None
        for k in range(0, 1024, 512):
            part = jnp.max(dot(r.kx[head, k : k + 512, :], r.qt[...]), axis=0, keepdims=True)
            peak = part if peak is None else jnp.maximum(peak, part)
        scores = dot(r.kx[head], r.qt[...])
        weights = jnp.exp2(scores * EXP2_SCALE - peak * EXP2_SCALE).astype(BF16)
        r.ee[head] = weights
        rows = slice(head * HD, head * HD + HD)
        left = jnp.concatenate([r.vt[rows, :], jnp.ones((16, 1024), BF16)], axis=0)
        mixed = dot(left, weights)
        inverse = 1.0 / mixed[HD : HD + 1]
        r.ot[rows, :] = mixed[0:HD] * inverse
        r.ri[head : head + 1, :] = inverse
        if head == 2:
            await_recv("fb", r.ff.at[c, pl.ds(0, 3)])
            for k in (2, 1, 3):
                at = group(a, ring(b, -k))
                copy_to("fw", ff_view(at), ff_view(at), sibling).start()

    r.mx[...] = r.ot[...].T.astype(BF16).reshape(4, 2, 128, 128)
    copy_to("mx", r.mx.at[:, 1 - c], r.mr, sibling).start()
    sends_end("mx", r.mr)

    for k in (1, 3, 2):
        await_recv("fc", r.ff.at[c, pl.ds(0, 3)], k - 1)
        for i in (1, 2, 3):
            at = group(ring(a, -i), ring(b, -k))
            copy_to("fw", ff_view(at), ff_view(at), sibling).start()

    await_recv("wb", r.wio.at[pl.ds(0, 12), pl.ds(64, 48)])
    rows = r.wio[:, 96:112, :].reshape(256, 128)
    spot_row, spot_lane = iota((256, 256), 0), iota((256, 256), 1)
    pick = spot_row == 16 * lax.div(spot_lane, 16) + lax.div(lax.rem(spot_lane, 16), 2)
    spread = dot_tn(rows, jnp.where(pick, 1.0, 0.0).astype(BF16))
    even_lane = lax.rem(iota((1, 256), 1), 2) == 0
    for i in range(8):
        r.vecs[i : i + 1, :] = jnp.where(
            even_lane, spread[2 * i : 2 * i + 1], spread[2 * i + 1 : 2 * i + 2])
    tile = iota((128, 256), 0) == 16 + lax.rem(iota((128, 256), 1), 16)
    wide = dot(rows, jnp.where(tile, 1.0, 0.0).astype(BF16))
    keep = lax.rem(spot_row, 32) == (
        16 * lax.div(spot_lane, 128) + lax.rem(lax.div(spot_lane, 16), 8))
    wide = jnp.where(keep, wide, 0.0).reshape(8, 32, 256)
    r.vecs[8:16, :] = jnp.sum(wide, axis=1)

    for head in range(4):
        r.vx[head, :, 0:128] = jnp.where(head_of_lane == head, r.vv[...], zero)
        r.vx[head, :, 128:256] = jnp.where(
            lax.div(iota((1024, 128), 1), 2) == head, 1.0, 0.0).astype(BF16)
        r.qm[head] = jnp.where(head_of_lane == head, r.qq[...], zero)

    def w_out_rows(half):
        low = r.wio[pl.ds(8 * half, 8), 64:80, :].reshape(128, 128)
        high = r.wio[pl.ds(8 * half, 8), 80:96, :].reshape(128, 128)
        return jnp.concatenate([low, high], axis=1)

    def vec(name):
        return r.vecs[ROW[name] : ROW[name] + 1, :]

    mixed_own = r.mx[:, c].reshape(512, 128)
    branch = dot(mixed_own, w_out_rows(c))
    await_recv("mx", r.mr)
    mixed_other = r.mr[...].reshape(512, 128)
    branch = branch + dot(mixed_other, w_out_rows(1 - c))
    first_sum = r.img[:, c].reshape(512, 256).astype(F32) + branch + vec("b_out")
    hidden, unit, inverse = norm_forward(first_sum, vec("gain1"), vec("shift1"))
    r.unit1[...] = unit
    r.inv1[...] = inverse
    r.hid[...] = hidden
    hidden_low = hidden.astype(BF16)
    r.hlow[...] = hidden_low
    r.hlt[...] = hidden_low.T

    await_recv("fw", r.ff.at[1 - c])

    def up_block(j):
        parts = [r.ff[0, :, 16 * k : 16 * k + 16, :].reshape(256, 256) for k in (2 * j, 2 * j + 1)]
        return jnp.concatenate(parts, axis=1)

    def down_block(j):
        return r.ff[1, 4 * j : 4 * j + 4, :, :].reshape(512, 256)

    r.acc[...] = r.hid[...] + vec("b_down")
    for j in range(4):
        up_shift = jnp.concatenate(
            [r.vecs[8 + 2 * j : 9 + 2 * j, :], r.vecs[9 + 2 * j : 10 + 2 * j, :]], axis=1)
        up = dot(r.hlow[...], up_block(j)) + up_shift
        square = up * up
        gate = 0.5 + 0.5 * jnp.tanh(up * (GELU_SCALE + GELU_SCALE * 0.044715 * square))
        active = up * gate
        slope = 2 * GELU_SCALE + 6 * 0.044715 * GELU_SCALE * square
        r.dgl[j] = (gate + active * (1.0 - gate) * slope).astype(BF16)
        active = active.astype(BF16)
        r.act[j] = active
        r.acc[...] += dot(active, down_block(j))

    out, unit, inverse = norm_forward(r.acc[...], vec("gain2"), vec("shift2"))
    r.lob[...] = out.astype(BF16).reshape(4, 128, 256)
    for k in (2, 1, 3):
        copy_to("lo", r.lob.at[ring(z, k)], r.lor.at[z], z_peer(k)).start()
    sends_end("lo", r.lob.at[pl.ds(0, 3)])
    own_copies = [pltpu.make_async_copy(r.lob.at[z], r.lor.at[z], r.own_s.at[0])]
    own_copies[0].start()

    await_recv("ct", r.cotb.at[pl.ds(0, 3)])
    d_out = r.cotb[...].reshape(512, 256).astype(F32)
    r.gv[ROW["gain2"] : ROW["gain2"] + 1, :] = column_sum(d_out * unit)
    r.gv[ROW["shift2"] : ROW["shift2"] + 1, :] = column_sum(d_out)
    d_second = norm_backward(d_out, unit, inverse, vec("gain2"))
    d_ffn = d_second.astype(BF16)
    r.dffn[...] = d_ffn
    r.gv[ROW["b_down"] : ROW["b_down"] + 1, :] = column_sum(d_ffn.astype(F32))
    r.acc[...] = d_second

    def first_sums(half):
        await_recv("gs", r.gs.at[pl.ds(0, 8)], half)

        @pl.when(c == 0)
        def _():
            rows = pl.ds(64 * half, 64)

            def add(g, carry):
                r.rs[g, rows] = (
                    r.gp[0, g, rows].astype(F32) + r.gs[g, rows].astype(F32)).astype(BF16)
                return carry

            lax.fori_loop(0, 16, add, 0)
            for k in (2, 1, 3):
                copy_to(
                    "r1", r.rs.at[pl.ds(4 * ring(a, k), 4), rows], r.r1.at[k - 1, :, rows],
                    a_peer(k)).start()

        @pl.when(c == 1)
        def _():
            def add(i, carry):
                at, to = 8 * half + i, 4 * lax.rem(i, 4) + 2 * half + lax.div(i, 4)
                r.rs[to] = (r.gp[1, at].astype(F32) + r.gs[at].astype(F32)).astype(BF16)
                return carry

            lax.fori_loop(0, 8, add, 0)
            part = pl.ds(2 * half, 2)
            for k in (2, 1, 3):
                copy_to(
                    "r1", r.rs.at[pl.ds(4 * ring(a, k) + 2 * half, 2)], r.r1.at[k - 1, part],
                    a_peer(k)).start()

    for j in range(4):
        d_active = dot_nt(r.dffn[...], down_block(j))
        d_up = (d_active * r.dgl[j].astype(F32)).astype(BF16)
        g_down = dot_tn(r.act[j], r.dffn[...])
        r.gp[1, 4 * j : 4 * j + 4] = g_down.astype(BF16).reshape(4, 128, 256)
        g_up = dot(r.hlt[...], d_up).astype(BF16)
        sums = column_sum(d_up.astype(F32))
        for k in range(2):
            at, lanes = 2 * j + k, slice(256 * k, 256 * k + 256)
            r.gp[0, :, 16 * at : 16 * at + 16, :] = g_up[:, lanes].reshape(16, 16, 256)
            r.gv[8 + at : 9 + at, :] = sums[:, lanes]
        r.acc[...] += dot_nt(d_up, up_block(j))

        @pl.when(c == 0)
        def _():
            part = pl.ds(4 * j, 4)
            copy_to("gs", r.gp.at[1, part], r.gs.at[part], sibling, r.gs_r.at[j // 2]).start()

        @pl.when(c == 1)
        def _():
            part = pl.ds(32 * j, 32)
            copy_to("gs", r.gp.at[0, :, part], r.gs.at[:, part], sibling, r.gs_r.at[j // 2]).start()

    sends_end("gs", r.gs)
    first_sums(0)

    d_hidden = r.acc[...]
    unit = r.unit1[...]
    r.gv[ROW["gain1"] : ROW["gain1"] + 1, :] = column_sum(d_hidden * unit)
    r.gv[ROW["shift1"] : ROW["shift1"] + 1, :] = column_sum(d_hidden)
    d_first = norm_backward(d_hidden, unit, r.inv1[...], vec("gain1"))
    r.dfirst[...] = d_first
    d_branch = d_first.astype(BF16)
    r.gv[ROW["b_out"] : ROW["b_out"] + 1, :] = column_sum(d_branch.astype(F32))
    r.dms[...] = dot_nt(d_branch, w_out_rows(1 - c)).astype(BF16).reshape(4, 128, 128)
    copy_to("dm", r.dms, r.dmx.at[:, c], sibling).start()
    sends_end("dm", r.dms)
    r.dmx[:, c] = dot_nt(d_branch, w_out_rows(c)).astype(BF16).reshape(4, 128, 128)

    def spot(g):
        return g * (1 - c) + (4 * lax.rem(g, 4) + lax.div(g, 4)) * c

    for half, mixed in ((c, r.mx[:, c].reshape(512, 128)), (1 - c, r.mr[...].reshape(512, 128))):
        g_out = dot_tn(mixed, d_branch).astype(BF16)
        for i in range(8):
            at = spot(8 * half + i)
            r.gwo[at, 0:16, :] = g_out[16 * i : 16 * i + 16, 0:128]
            r.gwo[at, 16:32, :] = g_out[16 * i : 16 * i + 16, 128:256]
    r.gv[0:2, :] = jnp.zeros((2, 256), F32)
    r.v0[...] = r.gv[...]

    first_sums(1)
    for k in (2, 1, 3):
        part, to = pl.ds(4 * ring(a, k), 4), a_peer(k)
        copy_to("g1", r.gwo.at[part], r.wo1.at[k - 1], to).start()
        copy_to("v1", r.v0, r.vr1.at[k - 1], to).start()
    sends_end("r1", r.r1)
    sends_end("g1", r.wo1)
    sends_end("v1", r.vr1)

    await_recv("dm", r.dmx.at[:, 1 - c])
    d_mixed_t = r.dmx[...].reshape(1024, 128).astype(F32).T
    extra = []
    for head in range(4):
        rows = slice(32 * head, 32 * head + 32)
        scaled = d_mixed_t[rows] * r.ri[head : head + 1, :]
        r.dot_[rows, :] = scaled.astype(BF16)
        inner = -column_sum(scaled * r.ot[rows, :])
        high = inner.astype(BF16).astype(F32)
        extra += [high, inner - high]
    extra.append(jnp.zeros((8, 1024), F32))
    r.dot_[128:144, :] = jnp.concatenate(extra, axis=0).astype(BF16)
    r.dot_[144:256, :] = jnp.zeros((112, 1024), BF16)
    r.doo[...] = r.dot_[0:128, :].T

    for head in range(4):
        d_probs = dot(r.vx[head], r.dot_[...])
        d_scores = r.ee[head] * d_probs.astype(BF16)
        r.ds[head % 2] = d_scores
        rows = slice(head * HD, head * HD + HD)
        r.dqt[rows, :] = dot(r.kt[rows, :], d_scores)
        if head == 3:
            await_recv("r1", r.r1)
            await_recv("g1", r.wo1)
            await_recv("v1", r.vr1)

            def add_first(i, carry):
                total = r.rs[4 * a + i].astype(F32)
                small = r.gwo[4 * a + i].astype(F32)
                for k in range(3):
                    total = total + r.r1[k, i].astype(F32)
                    small = small + r.wo1[k, i].astype(F32)
                r.s2[i] = total.astype(BF16)
                r.wos[i] = small.astype(BF16)
                return carry

            lax.fori_loop(0, 4, add_first, 0)
            r.v1[...] = r.v0[...] + r.vr1[0] + r.vr1[1] + r.vr1[2]
            for k in (2, 1, 3):
                part, to = ring(b, k), b_peer(k)
                copy_to("r2", r.s2.at[part], r.r2.at[k - 1], to).start()
                copy_to("g2", r.wos.at[part], r.wo2.at[k - 1], to).start()
                copy_to("v2", r.v1, r.vr2.at[k - 1], to).start()
            sends_end("r2", r.r2)
            sends_end("g2", r.wo2)
            sends_end("v2", r.vr2)

        do_masked = jnp.where(head_of_lane == head, r.doo[...], zero)
        for k in range(0, 1024, 256):
            d_key = dot(r.ds[head % 2, k : k + 256, :], r.qm[head])
            d_value = dot(r.ee[head, k : k + 256, :], do_masked)
            if head == 0:
                r.dk[k : k + 256, :] = d_key
                r.dv[k : k + 256, :] = d_value
            else:
                r.dk[k : k + 256, :] += d_key
                r.dv[k : k + 256, :] += d_value

    d_queries = (r.dqt[...] * SCORE_SCALE).T.astype(BF16)
    d_keys = (r.dk[...] * SCORE_SCALE).astype(BF16)
    d_values = r.dv[...].astype(BF16)
    for k, (left, right) in enumerate(((r.sht, d_queries), (r.sht, d_keys), (r.imgt, d_values))):
        g_part = dot(left[...], right).astype(BF16)
        for i in range(16):
            r.gio[i, 16 * k : 16 * k + 16, :] = g_part[16 * i : 16 * i + 16, :]
    ones = jnp.ones((1024, 128), BF16)
    sums = jnp.where(
        iota((128, 128), 1) < 64, dot_tn(d_queries, ones), dot_tn(d_values, ones)).astype(BF16)
    for i in range(8):
        r.gio[8 * c + i, 48:64, :] = sums[16 * i : 16 * i + 16, :]
        r.gio[8 * (1 - c) + i, 48:64, :] = jnp.zeros((16, 128), BF16)
    for k in (10, 6, 14, 9, 11, 2, 8, 5, 7, 13, 15, 1, 3, 4, 12):
        copy_to("q1", r.gio.at[ring(gx, k, 16)], r.q1.at[gx], gx_peer(k)).start()
    sends_end("q1", r.q1.at[pl.ds(0, 15)])

    d_tokens = (
        dot_nt(d_queries, w_part(0)) + dot_nt(d_keys, w_part(1)) + dot_nt(d_values, w_part(2)))
    r.gt[...] = d_tokens.astype(BF16).reshape(4, 2, 128, 256)
    copy_to("gt", r.gt.at[:, 1 - c], r.gtr, sibling).start()
    sends_end("gt", r.gtr)

    await_recv("gt", r.gtr)
    full = (
        r.dfirst[...]
        + r.gt[:, c].reshape(512, 256).astype(F32)
        + r.gtr[...].reshape(512, 256).astype(F32))
    r.gob[...] = full.astype(BF16).reshape(4, 128, 256)
    for k in (2, 1, 3):
        copy_to("go", r.gob.at[ring(z, k)], r.gor.at[z], z_peer(k)).start()
    sends_end("go", r.gob.at[pl.ds(0, 3)])

    await_recv("r2", r.r2)
    await_recv("g2", r.wo2)
    await_recv("v2", r.vr2)
    total = r.s2[b].astype(F32)
    small = r.wos[b].astype(F32)
    for k in range(3):
        total = total + r.r2[k].astype(F32)
        small = small + r.wo2[k].astype(F32)
    r.fin[0, 0:128, :] = total[:, 0:128]
    r.fin[1, 0:128, :] = total[:, 128:256]
    r.fwo[0:32, :] = small
    r.p3f[...] = jnp.zeros((8, 48, 128), F32)

    @pl.when(c == 0)
    def _():
        for i in range(8):
            for half in range(2):
                for row in range(2):
                    at = 16 * half + 8 * row
                    r.p3f[i, at : at + 8, :] = r.fin.at[half][
                        pl.ds(2 * i + row, 8, stride=16), :]

    @pl.when(c == 1)
    def _():
        for i in range(8):
            for half in range(2):
                r.p3f[i, 16 * half : 16 * half + 16, :] = r.fin[half, 16 * i : 16 * i + 16, :]

    for i in range(8):
        for row in range(2):
            at = 32 + 8 * row
            r.p3f[i, at : at + 2, :] = r.fwo[pl.ds(2 * i + row, 2, stride=16), :]
    sums = r.v1[...] + r.vr2[0] + r.vr2[1] + r.vr2[2]
    own_lanes = pltpu.roll(sums[0:8], lax.rem(256 - 16 * gx, 256), axis=1)[:, 0:128]
    up_sums = column_sum(jnp.where(iota((8, 256), 0) == lax.div(gx, 2), sums[8:16], 0.0))
    right = lax.rem(gx, 2).astype(F32)
    up_sums = up_sums[:, 0:128] * (1.0 - right) + up_sums[:, 128:256] * right
    for i in range(8):
        r.p3f[i, 34:40, :] = own_lanes[2:8]
        r.p3f[i, 42:43, :] = up_sums
    r.p3[...] = r.p3f[...].astype(BF16)
    for k in (4, 5, 3, 2, 6, 1, 7):
        copy_to("p3", r.p3.at[ring(gy, k, 8)], r.r3.at[gy], gy_peer(k)).start()
    sends_end("p3", r.p3.at[pl.ds(0, 7)])

    await_recv("q1", r.q1.at[pl.ds(0, 15)])
    total = r.gio[gx].astype(F32)
    for k in range(1, 16):
        total = total + r.q1[ring(gx, -k, 16)].astype(F32)
    r.fio[0:64, :] = total
    r.p4f[...] = jnp.zeros((8, 16, 128), F32)
    for i in range(8):
        for row in range(2):
            at = 8 * row
            r.p4f[i, at : at + 4, :] = r.fio[pl.ds(2 * i + row, 4, stride=16), :]
    r.p4[...] = r.p4f[...].astype(BF16)
    for k in (4, 5, 3, 2, 6, 1, 7):
        copy_to("p4", r.p4.at[ring(gy, k, 8)], r.r4.at[gy], gy_peer(k)).start()
    sends_end("p4", r.p4.at[pl.ds(0, 7)])

    own_copies += [
        pltpu.make_async_copy(r.gob.at[z], r.gor.at[z], r.own_s.at[1]),
        pltpu.make_async_copy(r.p3.at[gy], r.r3.at[gy], r.own_s.at[2]),
        pltpu.make_async_copy(r.p4.at[gy], r.r4.at[gy], r.own_s.at[3]),
    ]
    for copy in own_copies[1:]:
        copy.start()
    await_recv("lo", r.lor.at[pl.ds(0, 3)])
    await_recv("go", r.gor.at[pl.ds(0, 3)])
    await_recv("p3", r.r3.at[pl.ds(0, 7)])
    await_recv("p4", r.r4.at[pl.ds(0, 7)])
    for copy in own_copies:
        copy.wait()
    for make in closing:
        make().wait_send()


def unpack(*refs):
    r = Refs()
    for name, ref in zip(tuple(PACKED) + OUTPUTS, refs):
        setattr(r, name, ref)
    gy = lax.axis_index("gy")
    r.layer_out[...] = r.lor[...]
    r.grad_tokens[...] = r.gor[...].astype(F32)
    core0 = jnp.zeros((48, 128), F32)
    core1 = jnp.zeros((48, 128), F32)
    into0 = jnp.zeros((16, 128), F32)
    into1 = jnp.zeros((16, 128), F32)
    for i in range(4):
        core0 = core0 + r.r3[2 * i].astype(F32)
        core1 = core1 + r.r3[2 * i + 1].astype(F32)
        into0 = into0 + r.r4[2 * i].astype(F32)
        into1 = into1 + r.r4[2 * i + 1].astype(F32)
    r.g_w_down[:, 0:128] = core1[0:16]
    r.g_w_down[:, 128:256] = core1[16:32]
    w_out = core0 + core1
    for row in range(2):
        out_row = slice(row, row + 1)
        for j in range(8):
            for half in range(2):
                at = 16 * half + 8 * row + j
                lanes = 256 * j + 128 * half
                r.g_w_up[out_row, lanes : lanes + 128] = core0[at : at + 1]
        for k in range(3):
            at = 8 * row + k
            r.g_w_in[out_row, 256 * k : 256 * k + 128] = into0[at : at + 1]
            r.g_w_in[out_row, 256 * k + 128 : 256 * k + 256] = into1[at : at + 1]
        at = 32 + 8 * row
        r.g_w_out[out_row, 0:128] = w_out[at : at + 1]
        r.g_w_out[out_row, 128:256] = w_out[at + 1 : at + 2]
    biases = into0 + into1
    for name, lane in (("b_q", 0), ("b_v", 64)):
        pair = jnp.concatenate(
            [biases[3:4, lane : lane + 1], biases[11:12, lane : lane + 1]], axis=1)
        getattr(r, "g_" + name)[...] = pair.reshape(2)
    moved = pltpu.roll(w_out[32:48], lax.rem(128 - 2 * gy, 128), axis=1)
    for name in SMALL[2:]:
        row = ROW[name]
        getattr(r, "g_" + name)[...] = moved[row : row + 1, 0:2].reshape(2)
    moved = pltpu.roll(w_out[40:48], lax.rem(128 - 16 * gy, 128), axis=1)
    r.g_b_up[...] = moved[2:3, 0:16].reshape(16)


def body(
    tokens, lengths, w_in, b_q, b_v, w_out, b_out, gain_first, shift_first, w_up, b_up,
    w_down, b_down, gain_second, shift_second, cotangent,
):
    column = np.arange(D)
    freq = np.power(10000.0, -(2.0 * (column // 2)) / D).astype(np.float32)[None, :]
    args = (
        tokens, cotangent, lengths, jnp.asarray(freq), w_in, w_out, w_up, w_down,
        b_q, b_v, b_out, gain_first, shift_first, b_down, gain_second, shift_second, b_up,
    )
    vmem = pl.BlockSpec(memory_space=pltpu.VMEM)
    anywhere = pl.BlockSpec(memory_space=pl.ANY)
    in_specs = [anywhere] * len(args)
    in_specs[2] = pl.BlockSpec(memory_space=pltpu.SMEM)
    shape = jax.ShapeDtypeStruct
    vector = shape((2,), F32)
    scratch = [pltpu.VMEM(args[INPUTS.index(name)].shape, args[INPUTS.index(name)].dtype)
               for name in LOADED]
    scratch += [pltpu.VMEM(dims, kind) for dims, kind in SCRATCH.values()]
    scratch += [pltpu.SemaphoreType.DMA((count,)) for count in SEMS.values()]
    packed = pl.pallas_call(
        kernel,
        out_shape=tuple(shape(dims, kind) for dims, kind in PACKED.values()),
        in_specs=in_specs,
        out_specs=tuple([anywhere] * len(PACKED)),
        scratch_shapes=scratch,
        compiler_params=pltpu.CompilerParams(
            collective_id=0, has_side_effects=True, vmem_limit_bytes=VMEM_LIMIT),
        name="encoder_layer",
    )(*args)
    out_shape = (
        shape((4, 128, 256), BF16), shape((4, 128, 256), F32), shape((2, 768), F32),
        vector, vector, shape((2, 256), F32), vector, vector, vector,
        shape((2, 2048), F32), shape((16,), F32), shape((16, 256), F32),
        vector, vector, vector,
    )
    return pl.pallas_call(
        unpack,
        out_shape=out_shape,
        in_specs=[vmem] * len(packed),
        out_specs=tuple([vmem] * len(out_shape)),
        name="unpack_results",
    )(*packed)


def solution(mesh):
    both = ("gx", "gy")
    rows, vector, whole = P(both, None), P(both), P("gx", "gy", None)
    return jax.shard_map(
        body,
        mesh=mesh,
        in_specs=(
            whole, P("gx"), rows, vector, vector, rows, vector, vector, vector, rows, vector,
            rows, vector, vector, vector, whole,
        ),
        out_specs=(
            whole, whole, rows, vector, vector, rows, vector, vector, vector, rows, vector,
            rows, vector, vector, vector,
        ),
        check_vma=False,
    )
```
